128 devices in a mesh: dp: 16 (over y, z_hi, core), seq: 8 (over z_lo, x).
Axes of the slice: x: 4, y: 4, z: 4 (z_hi: 2, z_lo: 2; z = z_hi * 2 + z_lo), core: 2. Of those that a mesh axis runs over, the one named last changes fastest.
Arguments:
- prefix_hidden: bfloat16 [256, 816, 2048], P(('dp', 'seq')), may hold values from -24 to 24
- cameras: int32 [256], P(('dp', 'seq')), may hold values from 1 to 3, as said below
- text_length: int32 [256], P(('dp', 'seq')), may hold values from 1 to 48, as said below
- action_noise: bfloat16 [256, 50, 32], P(('dp', 'seq')), may hold values from -6 to 6
- clean_actions: bfloat16 [256, 50, 32], P(('dp', 'seq')), may hold values from -6 to 6
- flow_time: float32 [256], P(('dp', 'seq')), may hold values from 0.05 to 0.95
- input_weight: bfloat16 [32, 1024], replicated, may hold values from -1 to 1
- prefix_kv_weight: bfloat16 [2048, 512], P(('dp', 'seq')), may hold values from -2 to 2
- action_kv_weight: bfloat16 [1024, 512], P(('dp', 'seq')), may hold values from -2 to 2
- query_weight: bfloat16 [1024, 2048], P('dp', 'seq'), may hold values from -2 to 2
- cotangent: bfloat16 [256, 50, 2048], P(('dp', 'seq')), may hold values from -0.59765625 to 0.59765625
Outputs:
- attended: bfloat16 [256, 50, 2048], P(('dp', 'seq'))
- grad_query_weight: float32 [1024, 2048], P('dp', 'seq')
- grad_prefix_kv_weight: float32 [2048, 512], P(('dp', 'seq'))
- grad_action_kv_weight: float32 [1024, 512], P(('dp', 'seq'))
The draws below stay inside these ranges and needn't reach their ends.
Inputs may be any that keep to these rules, and one draw needn't show every extreme that they name: Some sample has 3 cameras and some has 1. `text_length`: some sample has 48 prompt tokens and some has 1.
All inputs are finite; a program needn't handle non-finite values.
Results may differ from the reference program's by a relative error of at most 0.02.
The reference program's roundings to bfloat16 on the way count: a program that leaves them out, or rounds other values in their place, can miss the bound.
Values may be sent and summed in bfloat16 or wider, within the bound.
A program may use at most 128 MiB of HBM per device.

```python
import math
import jax
import jax.numpy as jnp
from jax import lax

D = 2048
DA = 1024
HEADS = 8
HD = 256
IMG = 256
TXT = 48
CAMS = 3
ACT = 50
AD = 32
PMAX = 816
SAMPLES = 256
N_SEQ = 8


def draw_query_weight(key, part):
    key = jax.random.fold_in(key, 11)
    matrix = jax.random.normal(key, (DA, HEADS * HD), jnp.float32) / jnp.sqrt(DA * 1.0)
    return jnp.clip(matrix, -2.0, 2.0).astype(jnp.bfloat16)


def draw_prefix_kv_weight(key, part):
    key = jax.random.fold_in(key, 12)
    matrix = jax.random.normal(key, (D, 2 * HD), jnp.float32) / jnp.sqrt(D * 1.0)
    return jnp.clip(matrix, -2.0, 2.0).astype(jnp.bfloat16)


def draw_action_kv_weight(key, part):
    key = jax.random.fold_in(key, 13)
    matrix = jax.random.normal(key, (DA, 2 * HD), jnp.float32) / jnp.sqrt(DA * 1.0)
    return jnp.clip(matrix, -2.0, 2.0).astype(jnp.bfloat16)


def draw_cameras(key, part):
    key = jax.random.fold_in(key, 3)
    first, second = jax.random.split(key)
    counts = jax.random.randint(first, (SAMPLES,), 1, CAMS + 1, dtype=jnp.int32)
    order = jax.random.permutation(second, SAMPLES)
    counts = counts.at[order[0]].set(CAMS)
    return counts.at[order[1]].set(1)


def draw_text_length(key, part):
    key = jax.random.fold_in(key, 5)
    first, second = jax.random.split(key)
    counts = jax.random.randint(first, (SAMPLES,), 1, TXT + 1, dtype=jnp.int32)
    order = jax.random.permutation(second, SAMPLES)
    counts = counts.at[order[0]].set(TXT)
    return counts.at[order[1]].set(1)


def raised(result, key, source, target, parts, factor):
    owner, partner = [(jnp.arange(result.shape[dim]) // (result.shape[dim] // parts)).reshape([-1 if axis == dim else 1 for axis in range(result.ndim)]) for dim in (source, target)]
    chosen = jax.random.permutation(key, parts)[partner]
    strong = (owner == chosen) | (owner == (partner + parts // 2) % parts)
    return jnp.where(strong, factor * result, result)


def block_scale(stream_key, extent, pieces, smallest, high):
    level, own = 1.0, jax.random.fold_in(stream_key, 6)
    for axis_at, blocks in pieces:
        draws = jnp.exp(jax.random.uniform(jax.random.fold_in(own, axis_at), (blocks,), jnp.float32, smallest / len(pieces), high / len(pieces)))
        level = level * jnp.repeat(draws, extent[axis_at] // blocks).reshape([-1 if axis == axis_at else 1 for axis in range(len(extent))])
    return level


def bell_draw(key, extent, spread, limit, shards=(), held_as=jnp.bfloat16):
    gain = block_scale(key, extent, shards, -0.22, 0.18) if shards else 1.0
    array = jax.random.normal(key, extent, jnp.float32) * spread * gain
    return jnp.minimum(jnp.maximum(array, -limit), limit).astype(held_as)


def gaussian_with(key, shape, scale, reach, cuts, heavy, kind=jnp.bfloat16):
    array = scale * jax.random.normal(key, shape, jnp.float32)
    if cuts:
        array = array * block_scale(key, shape, cuts, -0.22, 0.18)
    return jnp.clip(raised(array, jax.random.fold_in(key, 3), *heavy), -reach, reach).astype(kind)


def setup_inputs(seed: int = 0) -> dict:
    key_of = jax.random.split(jax.random.key(seed), 12)
    return {
        "prefix_hidden": gaussian_with(key_of[0], (SAMPLES, PMAX, D), 1.0, 24.0, ((0, 128),), (0, 2, 128, 5.5)),
        "cameras": draw_cameras(jax.random.fold_in(key_of[11], 71), 0),
        "text_length": draw_text_length(jax.random.fold_in(key_of[11], 71), 0),
        "action_noise": bell_draw(key_of[3], (SAMPLES, ACT, AD), 1.0, 6.0, ((0, 128),)),
        "clean_actions": bell_draw(key_of[4], (SAMPLES, ACT, AD), 1.0, 6.0, ((0, 128),)),
        "flow_time": jnp.clip(0.05 + 0.9 * jax.random.uniform(key_of[5], (SAMPLES,), jnp.float32) ** block_scale(key_of[5], (SAMPLES,), ((0, 128),), -0.2, 0.2), 0.05, 0.95),
        "input_weight": bell_draw(key_of[6], (AD, DA), AD ** -0.5, 1.0),
        "prefix_kv_weight": draw_prefix_kv_weight(jax.random.fold_in(key_of[11], 71), 0),
        "action_kv_weight": draw_action_kv_weight(jax.random.fold_in(key_of[11], 71), 0),
        "query_weight": draw_query_weight(jax.random.fold_in(key_of[11], 71), 0),
        "cotangent": bell_draw(key_of[10], (SAMPLES, ACT, HEADS * HD), 0.1, 0.59765625, ((0, 128),)),
    }


EPS = 1e-06

def rms_rounded(hidden):
    wide = hidden.astype(jnp.float32)
    return (wide * lax.rsqrt(lax.optimization_barrier(jnp.mean(wide * wide, axis=-1, keepdims=True)) + EPS)).astype(jnp.bfloat16)

def time_feature(flow_col, row_width):
    half_width = row_width // 2
    fraction = jnp.arange(half_width, dtype=jnp.float32) / (half_width - 1)
    period = 0.004 * 1000.0 ** fraction
    angle = flow_col[..., None] * (2.0 * math.pi / period)
    return jnp.concatenate([jnp.sin(angle), jnp.cos(angle)], axis=-1)

def attend(query_rows, kv_rows, valid, cot_rows, groups):
    sample_count, step_count, row_width = query_rows.shape
    head_dim = kv_rows.shape[2] // 2
    head_count = row_width // head_dim
    inv_root = head_dim ** (-0.5)
    query_heads = query_rows.reshape(sample_count, step_count, head_count, head_dim).astype(jnp.float32)
    key_part = kv_rows[:, :, :head_dim].astype(jnp.float32)
    value_part = kv_rows[:, :, head_dim:].astype(jnp.float32)
    logits = jnp.einsum('sahd,skd->shak', query_heads, key_part) * inv_root
    logits = jnp.where(valid[:, None, None, :], logits, -1e+30)
    row_peak = lax.optimization_barrier(jnp.max(logits, axis=-1, keepdims=True))
    expo_vals = jnp.exp(logits - row_peak)
    weights = expo_vals / lax.optimization_barrier(jnp.sum(expo_vals, axis=-1, keepdims=True))
    weights_low = weights.astype(jnp.bfloat16)
    attended = jnp.einsum('shak,skd->sahd', weights_low.astype(jnp.float32), value_part)
    attended = attended.astype(jnp.bfloat16).reshape(sample_count, step_count, row_width)
    cot_heads = cot_rows.reshape(sample_count, step_count, head_count, head_dim).astype(jnp.float32)
    dprob = jnp.einsum('sahd,skd->shak', cot_heads, value_part)
    row_inner = lax.optimization_barrier(jnp.sum(weights * dprob, axis=-1, keepdims=True))
    dscore = (weights * (dprob - row_inner) * inv_root).astype(jnp.bfloat16)
    grad_query = jnp.einsum('shak,skd->sahd', dscore.astype(jnp.float32), key_part)
    grad_query = grad_query.astype(jnp.bfloat16).reshape(sample_count, step_count, row_width)
    grad_keys = jnp.einsum('shak,sahd->shkd', dscore.astype(jnp.float32), query_heads)
    grad_values = jnp.einsum('shak,sahd->shkd', weights_low.astype(jnp.float32), cot_heads)
    key_value_grad = jnp.concatenate([grad_keys, grad_values], axis=-1)
    partial_value = key_value_grad.reshape(sample_count, groups, head_count // groups, kv_rows.shape[1], 2 * head_dim)
    return (attended, grad_query, lax.optimization_barrier(jnp.sum(partial_value, axis=2)))

def reference(prefix_hidden, cameras, text_length, action_noise, clean_actions, flow_time, input_weight, prefix_kv_weight, action_kv_weight, query_weight, cotangent):
    lengths = (cameras * IMG + text_length).astype(jnp.int32)
    positions = jnp.arange(PMAX + ACT, dtype=jnp.int32)

    def per_sample(carry, items):
        hidden, length, noise_rows, clean_rows, flow_value, cot_rows = items
        prefix_norm = rms_rounded(hidden)
        prefix_kv = jnp.dot(prefix_norm, prefix_kv_weight, preferred_element_type=jnp.float32).astype(jnp.bfloat16)
        noisy = (flow_value * noise_rows.astype(jnp.float32) + (1.0 - flow_value) * clean_rows.astype(jnp.float32)).astype(jnp.bfloat16)
        action_wide = jnp.dot(noisy, input_weight, preferred_element_type=jnp.float32) + time_feature(flow_value, DA)
        action_norm = rms_rounded(action_wide)
        action_kv = jnp.dot(action_norm, action_kv_weight, preferred_element_type=jnp.float32).astype(jnp.bfloat16)
        kv_rows = jnp.concatenate([prefix_kv, action_kv], axis=0)
        valid = (positions < length) | (positions >= PMAX)
        query_rows = jnp.dot(action_norm, query_weight, preferred_element_type=jnp.float32).astype(jnp.bfloat16)
        attended, grad_query, partial_value = attend(query_rows[None], kv_rows[None], valid[None], cot_rows[None], N_SEQ)
        rounded = lax.optimization_barrier(partial_value.astype(jnp.bfloat16)).astype(jnp.float32)
        grad_kv = lax.optimization_barrier(jnp.sum(rounded, axis=1))[0].astype(jnp.bfloat16)
        sum_query, sum_prefix, sum_action = carry
        sum_query = sum_query + jnp.dot(action_norm.T, grad_query[0], preferred_element_type=jnp.float32)
        sum_prefix = sum_prefix + jnp.dot(prefix_norm.T, grad_kv[:PMAX], preferred_element_type=jnp.float32)
        sum_action = sum_action + jnp.dot(action_norm.T, grad_kv[PMAX:], preferred_element_type=jnp.float32)
        return ((sum_query, sum_prefix, sum_action), attended[0])
    start = (jnp.zeros((DA, HEADS * HD), jnp.float32), jnp.zeros((D, 2 * HD), jnp.float32), jnp.zeros((DA, 2 * HD), jnp.float32))
    totals, attended = lax.scan(per_sample, start, (prefix_hidden, lengths, action_noise, clean_actions, flow_time, cotangent))
    return (attended, totals[0], totals[1], totals[2])
```

```python
import math

import jax
import jax.numpy as jnp
from jax import lax
from jax.experimental import pallas as pl
from jax.experimental.pallas import tpu as pltpu
from jax.sharding import PartitionSpec as P

IMG = 256
EPS = 1e-06
MESH = pl.DeviceIdType.MESH
VMEM_LIMIT = 58 * 1024 * 1024
PREFIX, STEPS, PAD_STEPS, KEYS = 816, 50, 64, 896

ROWS = 48
ORDERS = ("xyz", "yzx", "zxy")
HALVES = (slice(0, 2), slice(2, 4))
FULL = slice(None)


class Place:
    def __init__(self):
        self.dp = lax.axis_index("dp")
        self.seq = lax.axis_index("seq")
        self.core = lax.rem(self.dp, 2)
        self.z_hi = lax.rem(self.dp // 2, 2)
        self.z_lo = self.seq // 4
        self.at = {
            "y": self.dp // 4,
            "z": self.z_hi * 2 + self.z_lo,
            "x": lax.rem(self.seq, 4),
        }
        self.sibling = self.device(core=1 - self.core)
        self.z_far = self.device(z=self.shifted("z", 2))

    def device(self, core=None, **moved):
        at = {**self.at, **moved}
        core = self.core if core is None else core
        return (
            at["y"] * 4 + (at["z"] // 2) * 2 + core,
            lax.rem(at["z"], 2) * 4 + at["x"],
        )

    def shifted(self, axis, by):
        return lax.rem(self.at[axis] + by, 4)

    def group_member(self, offset, sign=1):
        z_lo = lax.rem(self.z_lo + offset // 4, 2)
        x = lax.rem(self.at["x"] + sign * (offset % 4) + 4, 4)
        return z_lo * 4 + x

    def greet(self):
        barrier = pltpu.get_barrier_semaphore()
        others = [self.sibling, self.z_far]
        others += [(self.dp, self.group_member(offset)) for offset in range(1, 8)]
        others += [self.device(y=self.shifted("y", by)) for by in (1, 2, 3)]
        beyond = lax.rem(self.at["z"] + 3 + 2 * self.z_lo, 4)
        others.append(self.device(z=beyond))
        for other in others:
            pl.semaphore_signal(barrier, inc=1, device_id=other, device_id_type=MESH)
        pl.semaphore_wait(barrier, len(others))


class Links:
    def __init__(self, send_sem, recv_sem):
        self.send_sem, self.recv_sem = send_sem, recv_sem
        self.used = 0
        self.sent = []

    def slots(self, count):
        self.used += count
        return self.used - count

    def op(self, src, dst, to, slot):
        return pltpu.make_async_remote_copy(
            src_ref=src,
            dst_ref=dst,
            send_sem=self.send_sem.at[slot],
            recv_sem=self.recv_sem.at[slot],
            device_id=to,
            device_id_type=MESH,
        )

    def go(self, src, dst, to, slot):
        op = self.op(src, dst, to, slot)
        op.start()
        self.sent.append(op)

    def arrived(self, dst, to, slot):
        self.op(dst, dst, to, slot).wait_recv()


def run_together(works, tasks=()):
    live, tasks = list(works), list(tasks)
    while live or tasks:
        live = [work for work in live if next(work, "end") != "end"]
        if tasks:
            tasks.pop(0)()


def direct(links, place, axis, view, slot):
    own = place.at[axis]
    for by in (1, 3, 2):
        to = place.device(**{axis: place.shifted(axis, by)})
        links.go(view(own), view(own), to, slot + by - 1)
    yield
    for by in (1, 3, 2):
        links.arrived(view(place.shifted(axis, 4 - by)), place.sibling, slot + by - 1)


def ring(links, place, axis, view, slot, landed):
    own, right, left, across = (place.shifted(axis, by) for by in (0, 1, 3, 2))
    to_right, to_left = (place.device(**{axis: at}) for at in (right, left))
    links.go(view(own), view(own), to_right, slot)
    links.go(view(own), view(own), to_left, slot + 1)
    landed(own)
    yield
    links.arrived(view(left), to_right, slot)
    links.go(view(left, 0), view(left, 0), to_right, slot + 2)
    links.arrived(view(right), to_left, slot + 1)
    links.go(view(right, 1), view(right, 1), to_left, slot + 3)
    landed(left)
    landed(right)
    yield
    links.arrived(view(across, 0), to_right, slot + 2)
    links.arrived(view(across, 1), to_left, slot + 3)
    landed(across)


class Share:
    def __init__(self, links, place, view):
        self.links, self.place, self.view = links, place, view
        self.slot, self.due = links.slots(4), []

    def __call__(self, block):
        links, core = self.links, self.place.core
        slot = self.slot + len(self.due)
        mine = self.view(core, block)
        links.go(mine, mine, self.place.sibling, slot)
        self.due.append((self.view(1 - core, block), slot))

    def wait(self):
        for view, slot in self.due:
            self.links.arrived(view, self.place.sibling, slot)


def gather_part(links, place, ref, order):
    core = place.core
    first, second, third = order
    slot = links.slots(10)
    at = place.at
    yield from direct(
        links, place, first, lambda block: ref.at[core, at[third], at[second], block], slot
    )
    yield from direct(links, place, second, lambda block: ref.at[core, at[third], block], slot + 3)
    share = Share(links, place, lambda core, block: ref.at[core, block])

    def view(block, half=None):
        return ref.at[core, block] if half is None else ref.at[core, block, HALVES[half]]

    yield from ring(links, place, third, view, slot + 6, share)
    yield
    share.wait()


def gather_query(links, place, query_ref, then):
    core, y, z_hi = place.core, place.at["y"], place.z_hi
    slot = links.slots(5)
    links.go(query_ref.at[y, z_hi, core], query_ref.at[y, z_hi, core], place.z_far, slot)
    yield
    links.arrived(query_ref.at[y, 1 - z_hi, core], place.z_far, slot)
    share = Share(links, place, lambda core, block: query_ref.at[block, :, core])

    def view(block, half=None):
        return query_ref.at[block, FULL if half is None else half, core]

    yield from ring(links, place, "y", view, slot + 1, share)
    yield
    share.wait()
    then()


def reduce_ring(links, place, axis, pack, wire, half, fulls, slot):
    own, right, left, across = (place.shifted(axis, by) for by in (0, 1, 3, 2))
    to_right, to_left = (place.device(**{axis: at}) for at in (right, left))
    pack(across, 0)
    links.go(wire(across, 0), half.at[0], to_right, slot)
    pack(across, 1)
    links.go(wire(across, 1), half.at[1], to_left, slot + 1)
    yield
    pack(right, 1)
    links.go(wire(right, 1), fulls(0, 1), to_right, slot + 2)
    pack(left, 0)
    links.go(wire(left, 0), fulls(1, 0), to_left, slot + 3)
    yield
    links.arrived(half.at[0], to_right, slot)
    pack(right, 0, half.at[0])
    links.go(wire(right, 0), fulls(0, 0), to_right, slot + 4)
    links.arrived(half.at[1], to_left, slot + 1)
    pack(left, 1, half.at[1])
    links.go(wire(left, 1), fulls(1, 1), to_left, slot + 5)
    yield
    links.arrived(fulls(0, 1), to_right, slot + 2)
    links.arrived(fulls(1, 0), to_left, slot + 3)
    links.arrived(fulls(0, 0), to_right, slot + 4)
    links.arrived(fulls(1, 1), to_left, slot + 5)


def reduce_direct(links, place, axis, block_of, landing, slot):
    for by in (2, 1, 3):
        block = place.shifted(axis, by)
        links.go(
            block_of(block), landing.at[by - 1], place.device(**{axis: block}), slot + by - 1
        )
    yield
    for by in (1, 3, 2):
        links.arrived(landing.at[by - 1], place.sibling, slot + by - 1)


def reduce_part(links, place, grad_ref, pair_ref, v, part, finish):
    f32, bf16 = jnp.float32, jnp.bfloat16
    rows = slice(part * 16, part * 16 + 16)
    core = place.core
    first, second, third = ORDERS[part]
    wire, half, full = (v[f"{name}1_{part}"] for name in ("wire", "half", "full"))
    slot = links.slots(12)

    def mine(block, i, j):
        at = {first: block, second: i, third: j}
        y, z, x = at["y"], at["z"], at["x"]
        return grad_ref[y, z // 2, core, lax.rem(z, 2), x, rows, :] + pair_ref[y, z, x, rows, :]

    def pack(block, side, extra=None):
        for i in range(2):
            for j in range(4):
                value = mine(block, side * 2 + i, j)
                if extra is not None:
                    value = value + extra[i, j].astype(f32)
                wire[block, side * 2 + i, j] = value.astype(bf16)

    yield from reduce_ring(
        links, place, first, pack, lambda block, side: wire.at[block, HALVES[side]], half,
        lambda way, side: full.at[way, HALVES[side]], slot,
    )
    total, wire2, full2 = (v[f"{name}2_{part}"] for name in ("sum", "wire", "full"))
    for i in range(4):
        for j in range(4):
            value = mine(place.at[first], i, j)
            value = value + full[0, i, j].astype(f32) + full[1, i, j].astype(f32)
            total[i, j] = value
            wire2[i, j] = value.astype(bf16)
    yield from reduce_direct(links, place, second, lambda block: wire2.at[block], full2, slot + 6)
    total3, full3 = v[f"sum3_{part}"], v[f"full3_{part}"]
    value = total[place.at[second]]
    for k in range(3):
        value = value + full2[k].astype(f32)
    total3[...] = value
    yield from reduce_direct(links, place, third, lambda block: total3.at[block], full3, slot + 9)
    finish(total3[place.at[third]] + full3[0] + full3[1] + full3[2])


def reduce_query(links, place, first, v, out_ref):
    f32, bf16 = jnp.float32, jnp.bfloat16
    core, z_hi = place.core, place.z_hi
    grad_ref, pair_ref, wire = v["grad_query"], v["query_pair"], v["query_wire"]
    half, full, total, far_ref = v["query_half"], v["query_full"], v["query_sum"], v["query_far"]
    slot = links.slots(8)
    first()
    links.go(grad_ref.at[:, :, 1 - core], pair_ref, place.sibling, slot)
    yield
    links.arrived(pair_ref, place.sibling, slot)

    def pack(block, side, extra=None):
        value = grad_ref[block, side, core] + pair_ref[block, side]
        if extra is not None:
            value = value + extra[...].astype(f32)
        wire[block, side] = value.astype(bf16)

    yield from reduce_ring(
        links, place, "y", pack, lambda block, side: wire.at[block, side], half,
        lambda way, side: full.at[way, side], slot + 1,
    )
    own = place.at["y"]
    value = grad_ref[own, :, core] + pair_ref[own]
    total[...] = value + full[0].astype(f32) + full[1].astype(f32)
    links.go(total.at[1 - z_hi], far_ref, place.z_far, slot + 7)
    yield
    links.arrived(far_ref, place.z_far, slot + 7)
    out_ref[...] = total[z_hi] + far_ref[...]


def lanes_dot(left, right):
    return lax.dot_general(
        left, right, (((1,), (1,)), ((), ())), preferred_element_type=jnp.float32
    )


def rows_dot(left, right):
    return lax.dot_general(
        left, right, (((0,), (0,)), ((), ())), preferred_element_type=jnp.float32
    )


def dot(left, right):
    return jnp.dot(left, right, preferred_element_type=jnp.float32)


def step_kernel(
    cameras_ref, text_ref, hidden_ref, noisy_ref, time_ref, input_ref, cot_ref,
    own_prefix_ref, own_action_ref, own_query_ref,
    attended_ref, out_query_ref, out_prefix_ref, out_action_ref,
    v,
):
    f32, bf16 = jnp.float32, jnp.bfloat16
    place = Place()
    core, y, z_hi, z_lo, x = place.core, place.at["y"], place.z_hi, place.z_lo, place.at["x"]
    seq = place.seq
    links = Links(v["send"], v["recv"])

    loads = []
    for s in range(2):
        for i in range(3):
            rows = slice(i * 272, (i + 1) * 272)
            load = pltpu.make_async_copy(
                hidden_ref.at[s, rows, :], v["norm"].at[s, rows, :], v["load"].at[s * 3 + i]
            )
            load.start()
            loads.append(load)

    query_weight = v["query_weight"]
    own_action = own_action_ref[...].astype(f32)
    own_action = jnp.concatenate([own_action[:, 0:256], own_action[:, 256:512]], axis=0)
    own_parts = (own_prefix_ref[:, 0:256], own_prefix_ref[:, 256:512], own_action.astype(bf16))
    for part, (first, second, third) in enumerate(ORDERS):
        at = place.at
        v[f"weight_{part}"][core, at[third], at[second], at[first]] = own_parts[part]
    query_weight[y, z_hi, core] = own_query_ref[...]
    v["noisy"][seq] = noisy_ref[...]
    v["time"][seq] = time_ref[...]
    place.greet()

    packet = links.slots(16)
    for offset in range(1, 8):
        to = (place.dp, place.group_member(offset))
        links.go(noisy_ref, v["noisy"].at[seq], to, packet + offset)
        links.go(time_ref, v["time"].at[seq], to, packet + 8 + offset)

    act, act_t = v["act"], v["act_t"]

    def action_rows(offset):
        def run():
            member = place.group_member(offset, -1)
            if offset:
                to = (place.dp, member)
                links.arrived(v["noisy"].at[member], to, packet + offset)
                links.arrived(v["time"].at[member], to, packet + 8 + offset)
            wide = dot(v["noisy"][member][:, 0:32], input_ref[...])
            time = v["time"][member]
            pieces = []
            for s in range(2):
                rows = slice(s * PAD_STEPS, (s + 1) * PAD_STEPS)
                pieces.append(
                    jnp.concatenate(
                        [
                            wide[rows, i * 128 : (i + 1) * 128] + time[s * 8 + i : s * 8 + i + 1]
                            for i in range(8)
                        ],
                        axis=1,
                    )
                )
            wide = jnp.concatenate(pieces, axis=0)
            scale = lax.rsqrt(jnp.mean(wide * wide, axis=-1, keepdims=True) + EPS)
            rows = (wide * scale).astype(bf16)
            at = pl.ds(pl.multiple_of(member * 128, 128), 128)
            act[at, :] = rows
            act_t[:, at] = rows.T
            if offset == 0:
                row = lax.broadcasted_iota(jnp.int32, (128, 256), 0)
                col = lax.broadcasted_iota(jnp.int32, (128, 256), 1)
                within = col % 16
                origin = (col // 16) * 8 + within
                to_left = jnp.where((within < 8) & (row == origin), 1.0, 0.0).astype(bf16)
                to_right = jnp.where((within >= 8) & (row == origin - 8), 1.0, 0.0).astype(bf16)
                for i in range(8):
                    piece, cols = rows[:, i * 128 : (i + 1) * 128], slice(i * 256, (i + 1) * 256)
                    v["left"][:, cols] = dot(piece, to_left).astype(bf16)
                    v["right"][:, cols] = dot(piece, to_right).astype(bf16)

        return run

    def normalize(chunk):
        def run():
            loads[chunk].wait()
            s, start = chunk // 3, (chunk % 3) * 272

            def body(i, carry):
                at = pl.ds(pl.multiple_of(start + i * 16, 16), 16)
                wide = v["norm"][s, at, :].astype(f32)
                scale = lax.rsqrt(jnp.mean(wide * wide, axis=-1, keepdims=True) + EPS)
                v["norm"][s, at, :] = (wide * scale).astype(bf16)
                return carry

            lax.fori_loop(0, 17, body, 0)

        return run

    def place_cotangent():
        v["cot"][...] = jnp.zeros_like(v["cot"])
        for s in range(2):
            for h in range(8):
                v["cot"][h, s * PAD_STEPS : s * PAD_STEPS + STEPS, :] = cot_ref[
                    s, :, h * 256 : (h + 1) * 256
                ]

    exchange = links.slots(16)

    def send_queries():
        wide = query_weight[...].reshape(1024, 256)
        for offset in (1, 2, 3, 4, 5, 6, 7, 0):
            member = place.group_member(offset)
            at = pl.ds(pl.multiple_of(member * 128, 128), 128)
            value = dot(act[at, :], wide).astype(bf16)
            if offset:
                v["query_out"][offset] = value
                links.go(
                    v["query_out"].at[offset], v["query"].at[seq], (place.dp, member),
                    exchange + offset,
                )
            else:
                v["query"][seq] = value

    works = [gather_query(links, place, query_weight, send_queries)]
    works += [gather_part(links, place, v[f"weight_{part}"], ORDERS[part]) for part in range(3)]
    rows = [action_rows(offset) for offset in range(8)]
    tasks = [rows[0], lambda: [rows[i]() for i in (1, 3, 4)], lambda: [rows[i]() for i in (2, 5, 6, 7)]]
    tasks += [normalize(chunk) for chunk in range(6)] + [place_cotangent]
    run_together(works, tasks)

    wp, kv = v["wp"], v["kv"]

    def block_rows(part, a, b):
        ref, order = v[f"weight_{part}"], ORDERS[part][::-1]
        pieces = []
        for c in range(2):
            for low in range(2):
                at = {"y": a, "z": b * 2 + low}
                if order[2] == "x":
                    pieces.append(ref[c, at[order[0]], at[order[1]]].reshape(64, 256))
                else:
                    for col in range(4):
                        at["x"] = col
                        pieces.append(ref[c, at[order[0]], at[order[1]], at[order[2]]])
        return pieces

    def unpack(k, carry):
        keys, values = carry
        a, b = k // 2, lax.rem(k, 2)
        for part in range(2):
            start = k * 256
            for piece in block_rows(part, a, b):
                at = pl.ds(pl.multiple_of(start, 16), piece.shape[0])
                wp[at, part * 256 : (part + 1) * 256] = piece
                start += piece.shape[0]
        block = jnp.concatenate(block_rows(2, a, b), axis=0)
        at = pl.ds(pl.multiple_of(k * 256, 256), 256)
        return keys + dot(v["left"][:, at], block), values + dot(v["right"][:, at], block)

    zero = jnp.zeros((2 * PAD_STEPS, 256), f32)
    keys, values = lax.fori_loop(0, 8, unpack, (zero, zero))
    keys, values = keys.astype(bf16), values.astype(bf16)
    for s in range(2):
        rows = slice(s * PAD_STEPS, (s + 1) * PAD_STEPS)
        kv[s, PREFIX:KEYS, :] = jnp.zeros((KEYS - PREFIX, 512), bf16)
        kv[s, PREFIX : PREFIX + PAD_STEPS, 0:256] = keys[rows]
        kv[s, PREFIX : PREFIX + PAD_STEPS, 256:512] = values[rows]

    for s in range(2):

        def prefix(i, carry):
            at = pl.ds(pl.multiple_of(i * 272, 16), 272)
            kv[s, at, :] = dot(v["norm"][s, at, :], wp[...]).astype(bf16)
            return carry

        lax.fori_loop(0, 3, prefix, 0)

    for offset in range(1, 8):
        member = place.group_member(offset, -1)
        links.arrived(v["query"].at[member], (place.dp, member), exchange + offset)

    low_ref, ds_ref, gsum, gkv = v["low"], v["ds"], v["gsum"], v["gkv"]

    def sample(s, carry):
        length = cameras_ref[s] * IMG + text_ref[s]
        mine = pl.ds(pl.multiple_of(s * PAD_STEPS, PAD_STEPS), PAD_STEPS)

        def half(i, carry):
            heads = pl.ds(i * 4, 4)
            query = v["query"][heads, mine, :].reshape(256, 256)
            cot = v["cot"][heads, mine, :].reshape(256, 256)
            key, value = kv[s, :, 0:256], kv[s, :, 256:512]
            column = lax.broadcasted_iota(jnp.int32, (256, KEYS), 1)
            valid = (column < length) | ((column >= PREFIX) & (column < PREFIX + STEPS))
            logits = jnp.where(valid, lanes_dot(query, key) * 0.0625, -1e30)
            expo = jnp.exp(logits - jnp.max(logits, axis=-1, keepdims=True))
            probs = expo / jnp.sum(expo, axis=-1, keepdims=True)
            low = probs.astype(bf16)
            low_ref[...] = low
            dprob = lanes_dot(cot, value)
            inner = jnp.sum(probs * dprob, axis=-1, keepdims=True)
            dscore = (probs * (dprob - inner) * 0.0625).astype(bf16)
            ds_ref[...] = dscore
            attended = dot(low, value).astype(bf16)
            for j in range(4):
                at = pl.ds(pl.multiple_of((i * 4 + j) * 256, 256), 256)
                attended_ref[s, :, at] = attended[j * 64 : j * 64 + STEPS]
            v["gq"][heads, mine, :] = dot(dscore, key).astype(bf16).reshape(4, 64, 256)
            for j in range(4):
                rows = slice(j * 64, (j + 1) * 64)
                gsum[0:256, :] += rows_dot(query[rows], ds_ref[rows, :]).astype(bf16).astype(f32)
                gsum[256:512, :] += rows_dot(cot[rows], low_ref[rows, :]).astype(bf16).astype(f32)
            return carry

        gsum[...] = jnp.zeros_like(gsum)
        lax.fori_loop(0, 2, half, 0)
        gkv[s] = gsum[...].astype(bf16)
        return carry

    lax.fori_loop(0, 2, sample, 0)

    for offset in range(1, 8):
        member = place.group_member(offset)
        links.go(
            v["gq"].at[member], v["group_gq"].at[seq], (place.dp, member), exchange + 8 + offset
        )
    v["group_gq"][seq] = v["gq"][seq]

    for s in range(2):
        turned = gkv[s, :, PREFIX - 48 : KEYS].astype(f32).T[48 : 48 + PAD_STEPS]
        ds_ref[s * 64 : (s + 1) * 64, 0:512] = turned.astype(bf16)
    grad, pair = v["grad"], v["pair"]
    pairing = links.slots(8)

    def pair_op(k):
        a, b = k // 2, lax.rem(k, 2)
        return links.op(
            grad.at[a, b, 1 - core], pair.at[a, pl.ds(b * 2, 2)], place.sibling, pairing + k
        )

    def grad_prefix(k, carry):
        at = pl.ds(pl.multiple_of(k * 256, 256), 256)
        a, b = k // 2, lax.rem(k, 2)
        value = dot(gkv[0, :, 0:PREFIX], v["norm"][0, :, at])
        value += dot(gkv[1, :, 0:PREFIX], v["norm"][1, :, at])
        value = value.T
        grad[a, b, :, :, :, 0:16, :] = value[:, 0:256].reshape(2, 2, 4, 16, 256)
        grad[a, b, :, :, :, 16:32, :] = value[:, 256:512].reshape(2, 2, 4, 16, 256)
        action = rows_dot(v["left"][:, at], ds_ref[0:128, 0:256])
        action += rows_dot(v["right"][:, at], ds_ref[0:128, 256:512])
        grad[a, b, :, :, :, 32:48, :] = action.reshape(2, 2, 4, 16, 256)
        pair_op(k).start()
        return carry

    lax.fori_loop(0, 8, grad_prefix, 0)
    for k in range(8):
        pair_op(k).wait_recv()

    def grad_query():
        for offset in range(1, 8):
            member = place.group_member(offset, -1)
            links.arrived(v["group_gq"].at[member], (place.dp, member), exchange + 8 + offset)
        rows = v["group_gq"][...].reshape(1024, 256)
        for a in range(4):
            value = dot(act_t[a * 256 : (a + 1) * 256, :], rows)
            v["grad_query"][a] = value.reshape(2, 2, 64, 256)

    def finish(part):
        def store(value):
            if part == 2:
                out_action_ref[:, 0:256] = value[0:8]
                out_action_ref[:, 256:512] = value[8:16]
            else:
                out_prefix_ref[:, part * 256 : (part + 1) * 256] = value

        return store

    works = [reduce_part(links, place, grad, pair, v, part, finish(part)) for part in range(3)]
    works.append(reduce_query(links, place, grad_query, v, out_query_ref))
    run_together(works)
    for op in links.sent:
        op.wait_send()
    for k in range(8):
        pair_op(k).wait_send()


def step(cameras, text_length, hidden, noisy, time, input_weight, cot, own_prefix, own_action, own_query):
    bf16, f32 = jnp.bfloat16, jnp.float32
    smem, vmem = pl.BlockSpec(memory_space=pltpu.SMEM), pl.BlockSpec(memory_space=pltpu.VMEM)
    scratch = dict(
        norm=pltpu.VMEM((2, PREFIX, 2048), bf16),
        query_weight=pltpu.VMEM((4, 2, 2, 64, 256), bf16),
        noisy=pltpu.VMEM((8, 128, 128), bf16),
        time=pltpu.VMEM((8, 16, 128), f32),
        act=pltpu.VMEM((1024, 1024), bf16),
        act_t=pltpu.VMEM((1024, 1024), bf16),
        left=pltpu.VMEM((128, 2048), bf16),
        right=pltpu.VMEM((128, 2048), bf16),
        cot=pltpu.VMEM((8, 128, 256), bf16),
        query=pltpu.VMEM((8, 128, 256), bf16),
        query_out=pltpu.VMEM((8, 128, 256), bf16),
        gq=pltpu.VMEM((8, 128, 256), bf16),
        group_gq=pltpu.VMEM((8, 128, 256), bf16),
        wp=pltpu.VMEM((2048, 512), bf16),
        kv=pltpu.VMEM((2, KEYS, 512), bf16),
        low=pltpu.VMEM((256, KEYS), bf16),
        ds=pltpu.VMEM((256, KEYS), bf16),
        gsum=pltpu.VMEM((512, KEYS), f32),
        gkv=pltpu.VMEM((2, 512, KEYS), bf16),
        grad=pltpu.VMEM((4, 2, 2, 2, 4, ROWS, 256), f32),
        pair=pltpu.VMEM((4, 4, 4, ROWS, 256), f32),
        grad_query=pltpu.VMEM((4, 2, 2, 64, 256), f32),
        query_pair=pltpu.VMEM((4, 2, 64, 256), f32),
        query_wire=pltpu.VMEM((4, 2, 64, 256), bf16),
        query_half=pltpu.VMEM((2, 64, 256), bf16),
        query_full=pltpu.VMEM((2, 2, 64, 256), bf16),
        query_sum=pltpu.VMEM((2, 64, 256), f32),
        query_far=pltpu.VMEM((64, 256), f32),
        send=pltpu.SemaphoreType.DMA((192,)),
        recv=pltpu.SemaphoreType.DMA((192,)),
        load=pltpu.SemaphoreType.DMA((6,)),
    )
    for part in range(3):
        scratch[f"weight_{part}"] = pltpu.VMEM((2, 4, 4, 4, 16, 256), bf16)
        scratch[f"wire1_{part}"] = pltpu.VMEM((4, 4, 4, 16, 256), bf16)
        scratch[f"half1_{part}"] = pltpu.VMEM((2, 2, 4, 16, 256), bf16)
        scratch[f"full1_{part}"] = pltpu.VMEM((2, 4, 4, 16, 256), bf16)
        scratch[f"sum2_{part}"] = pltpu.VMEM((4, 4, 16, 256), f32)
        scratch[f"wire2_{part}"] = pltpu.VMEM((4, 4, 16, 256), bf16)
        scratch[f"full2_{part}"] = pltpu.VMEM((3, 4, 16, 256), bf16)
        scratch[f"sum3_{part}"] = pltpu.VMEM((4, 16, 256), f32)
        scratch[f"full3_{part}"] = pltpu.VMEM((3, 16, 256), f32)
    return pl.pallas_call(
        step_kernel,
        out_shape=(
            jax.ShapeDtypeStruct((2, STEPS, 2048), bf16),
            jax.ShapeDtypeStruct((64, 256), f32),
            jax.ShapeDtypeStruct((16, 512), f32),
            jax.ShapeDtypeStruct((8, 512), f32),
        ),
        in_specs=[smem] * 2 + [pl.BlockSpec(memory_space=pl.ANY)] + [vmem] * 7,
        out_specs=(vmem,) * 4,
        scratch_shapes=[scratch],
        compiler_params=pltpu.CompilerParams(
            collective_id=1, has_side_effects=True, vmem_limit_bytes=VMEM_LIMIT
        ),
        cost_estimate=pl.CostEstimate(
            flops=10**10, bytes_accessed=9 * 10**6, transcendentals=10**6
        ),
        name="step",
    )(
        cameras, text_length, hidden, noisy, time, input_weight, cot,
        own_prefix, own_action, own_query,
    )


def time_feature(flow_col, row_width):
    half_width = row_width // 2
    fraction = jnp.arange(half_width, dtype=jnp.float32) / (half_width - 1)
    period = 0.004 * 1000.0**fraction
    angle = flow_col[..., None] * (2.0 * math.pi / period)
    return jnp.concatenate([jnp.sin(angle), jnp.cos(angle)], axis=-1)


def on_device(
    prefix_hidden,
    cameras,
    text_length,
    action_noise,
    clean_actions,
    flow_time,
    input_weight,
    prefix_kv_weight,
    action_kv_weight,
    query_weight,
    cotangent,
):
    flow_col = flow_time[:, None, None]
    noisy = (
        flow_col * action_noise.astype(jnp.float32)
        + (1.0 - flow_col) * clean_actions.astype(jnp.float32)
    ).astype(jnp.bfloat16)
    noisy = jnp.pad(noisy, ((0, 0), (0, PAD_STEPS - STEPS), (0, 96))).reshape(128, 128)
    time = time_feature(flow_time, 1024).reshape(16, 128)
    return step(
        cameras,
        text_length,
        prefix_hidden,
        noisy,
        time,
        input_weight,
        cotangent,
        prefix_kv_weight,
        action_kv_weight,
        query_weight,
    )


def solution(mesh):
    return jax.shard_map(
        on_device,
        mesh=mesh,
        in_specs=(
            P(("dp", "seq"), None, None),
            P(("dp", "seq")),
            P(("dp", "seq")),
            P(("dp", "seq"), None, None),
            P(("dp", "seq"), None, None),
            P(("dp", "seq")),
            P(),
            P(("dp", "seq"), None),
            P(("dp", "seq"), None),
            P("dp", "seq"),
            P(("dp", "seq"), None, None),
        ),
        out_specs=(
            P(("dp", "seq"), None, None),
            P("dp", "seq"),
            P(("dp", "seq"), None),
            P(("dp", "seq"), None),
        ),
        check_vma=False,
    )
```

```python
import math

import jax
import jax.numpy as jnp
from jax import lax
from jax.experimental import pallas as pl
from jax.experimental.pallas import tpu as pltpu
from jax.sharding import PartitionSpec as P

IMG = 256
EPS = 1e-06
MESH = pl.DeviceIdType.MESH
VMEM_LIMIT = 58 * 1024 * 1024
PREFIX, STEPS, PAD_STEPS, KEYS = 816, 50, 64, 896

ROWS = 48
ORDERS = ("xyz", "yzx", "zxy")
HALVES = (slice(0, 2), slice(2, 4))
FULL = slice(None)


class Place:
    def __init__(self):
        self.dp = lax.axis_index("dp")
        self.seq = lax.axis_index("seq")
        self.core = lax.rem(self.dp, 2)
        self.z_hi = lax.rem(self.dp // 2, 2)
        self.z_lo = self.seq // 4
        self.at = {
            "y": self.dp // 4,
            "z": self.z_hi * 2 + self.z_lo,
            "x": lax.rem(self.seq, 4),
        }
        self.sibling = self.device(core=1 - self.core)
        self.z_far = self.device(z=self.shifted("z", 2))

    def device(self, core=None, **moved):
        at = {**self.at, **moved}
        core = self.core if core is None else core
        return (
            at["y"] * 4 + (at["z"] // 2) * 2 + core,
            lax.rem(at["z"], 2) * 4 + at["x"],
        )

    def shifted(self, axis, by):
        return lax.rem(self.at[axis] + by, 4)

    def group_member(self, offset, sign=1):
        z_lo = lax.rem(self.z_lo + offset // 4, 2)
        x = lax.rem(self.at["x"] + sign * (offset % 4) + 4, 4)
        return z_lo * 4 + x

    def greet(self):
        barrier = pltpu.get_barrier_semaphore()
        others = [self.sibling, self.z_far]
        others += [(self.dp, self.group_member(offset)) for offset in range(1, 8)]
        others += [self.device(y=self.shifted("y", by)) for by in (1, 2, 3)]
        beyond = lax.rem(self.at["z"] + 3 + 2 * self.z_lo, 4)
        others.append(self.device(z=beyond))
        for other in others:
            pl.semaphore_signal(barrier, inc=1, device_id=other, device_id_type=MESH)
        pl.semaphore_wait(barrier, len(others))


class Links:
    def __init__(self, send_sem, recv_sem):
        self.send_sem, self.recv_sem = send_sem, recv_sem
        self.used = 0
        self.sent = []

    def slots(self, count):
        self.used += count
        return self.used - count

    def op(self, src, dst, to, slot):
        return pltpu.make_async_remote_copy(
            src_ref=src,
            dst_ref=dst,
            send_sem=self.send_sem.at[slot],
            recv_sem=self.recv_sem.at[slot],
            device_id=to,
            device_id_type=MESH,
        )

    def go(self, src, dst, to, slot):
        op = self.op(src, dst, to, slot)
        op.start()
        self.sent.append(op)

    def arrived(self, dst, to, slot):
        self.op(dst, dst, to, slot).wait_recv()


def run_together(works, tasks=()):
    live, tasks = list(works), list(tasks)
    while live or tasks:
        live = [work for work in live if next(work, "end") != "end"]
        if tasks:
            tasks.pop(0)()


def direct(links, place, axis, view, slot):
    own = place.at[axis]
    for by in (1, 3, 2):
        to = place.device(**{axis: place.shifted(axis, by)})
        links.go(view(own), view(own), to, slot + by - 1)
    yield
    for by in (1, 3, 2):
        links.arrived(view(place.shifted(axis, 4 - by)), place.sibling, slot + by - 1)


def ring(links, place, axis, view, slot, landed):
    own, right, left, across = (place.shifted(axis, by) for by in (0, 1, 3, 2))
    to_right, to_left = (place.device(**{axis: at}) for at in (right, left))
    links.go(view(own), view(own), to_right, slot)
    links.go(view(own), view(own), to_left, slot + 1)
    landed(own)
    yield
    links.arrived(view(left), to_right, slot)
    links.go(view(left, 0), view(left, 0), to_right, slot + 2)
    links.arrived(view(right), to_left, slot + 1)
    links.go(view(right, 1), view(right, 1), to_left, slot + 3)
    landed(left)
    landed(right)
    yield
    links.arrived(view(across, 0), to_right, slot + 2)
    links.arrived(view(across, 1), to_left, slot + 3)
    landed(across)


class Share:
    def __init__(self, links, place, view):
        self.links, self.place, self.view = links, place, view
        self.slot, self.due = links.slots(4), []

    def __call__(self, block):
        links, core = self.links, self.place.core
        slot = self.slot + len(self.due)
        mine = self.view(core, block)
        links.go(mine, mine, self.place.sibling, slot)
        self.due.append((self.view(1 - core, block), slot))

    def wait(self):
        for view, slot in self.due:
            self.links.arrived(view, self.place.sibling, slot)


def gather_part(links, place, ref, order):
    core = place.core
    first, second, third = order
    slot = links.slots(10)
    at = place.at
    yield from direct(
        links, place, first, lambda block: ref.at[core, at[third], at[second], block], slot
    )
    yield from direct(links, place, second, lambda block: ref.at[core, at[third], block], slot + 3)
    share = Share(links, place, lambda core, block: ref.at[core, block])

    def view(block, half=None):
        return ref.at[core, block] if half is None else ref.at[core, block, HALVES[half]]

    yield from ring(links, place, third, view, slot + 6, share)
    yield
    share.wait()


def gather_query(links, place, query_ref, then):
    core, y, z_hi = place.core, place.at["y"], place.z_hi
    slot = links.slots(5)
    links.go(query_ref.at[y, z_hi, core], query_ref.at[y, z_hi, core], place.z_far, slot)
    yield
    links.arrived(query_ref.at[y, 1 - z_hi, core], place.z_far, slot)
    share = Share(links, place, lambda core, block: query_ref.at[block, :, core])

    def view(block, half=None):
        return query_ref.at[block, FULL if half is None else half, core]

    yield from ring(links, place, "y", view, slot + 1, share)
    yield
    share.wait()
    then()


def reduce_ring(links, place, axis, pack, wire, half, fulls, slot):
    own, right, left, across = (place.shifted(axis, by) for by in (0, 1, 3, 2))
    to_right, to_left = (place.device(**{axis: at}) for at in (right, left))
    pack(across, 0)
    links.go(wire(across, 0), half.at[0], to_right, slot)
    pack(across, 1)
    links.go(wire(across, 1), half.at[1], to_left, slot + 1)
    yield
    pack(right, 1)
    links.go(wire(right, 1), fulls(0, 1), to_right, slot + 2)
    pack(left, 0)
    links.go(wire(left, 0), fulls(1, 0), to_left, slot + 3)
    yield
    links.arrived(half.at[0], to_right, slot)
    pack(right, 0, half.at[0])
    links.go(wire(right, 0), fulls(0, 0), to_right, slot + 4)
    links.arrived(half.at[1], to_left, slot + 1)
    pack(left, 1, half.at[1])
    links.go(wire(left, 1), fulls(1, 1), to_left, slot + 5)
    yield
    links.arrived(fulls(0, 1), to_right, slot + 2)
    links.arrived(fulls(1, 0), to_left, slot + 3)
    links.arrived(fulls(0, 0), to_right, slot + 4)
    links.arrived(fulls(1, 1), to_left, slot + 5)


def reduce_direct(links, place, axis, block_of, landing, slot):
    for by in (2, 1, 3):
        block = place.shifted(axis, by)
        links.go(
            block_of(block), landing.at[by - 1], place.device(**{axis: block}), slot + by - 1
        )
    yield
    for by in (1, 3, 2):
        links.arrived(landing.at[by - 1], place.sibling, slot + by - 1)


def reduce_part(links, place, grad_ref, pair_ref, v, part, finish):
    f32, bf16 = jnp.float32, jnp.bfloat16
    rows = slice(part * 16, part * 16 + 16)
    core = place.core
    first, second, third = ORDERS[part]
    wire, half, full = (v[f"{name}1_{part}"] for name in ("wire", "half", "full"))
    slot = links.slots(12)

    def mine(block, i, j):
        at = {first: block, second: i, third: j}
        y, z, x = at["y"], at["z"], at["x"]
        return grad_ref[y, z // 2, core, lax.rem(z, 2), x, rows, :] + pair_ref[y, z, x, rows, :]

    def pack(block, side, extra=None):
        for i in range(2):
            for j in range(4):
                value = mine(block, side * 2 + i, j)
                if extra is not None:
                    value = value + extra[i, j].astype(f32)
                wire[block, side * 2 + i, j] = value.astype(bf16)

    yield from reduce_ring(
        links, place, first, pack, lambda block, side: wire.at[block, HALVES[side]], half,
        lambda way, side: full.at[way, HALVES[side]], slot,
    )
    total, wire2, full2 = (v[f"{name}2_{part}"] for name in ("sum", "wire", "full"))
    for i in range(4):
        for j in range(4):
            value = mine(place.at[first], i, j)
            value = value + full[0, i, j].astype(f32) + full[1, i, j].astype(f32)
            total[i, j] = value
            wire2[i, j] = value.astype(bf16)
    yield from reduce_direct(links, place, second, lambda block: wire2.at[block], full2, slot + 6)
    total3, full3 = v[f"sum3_{part}"], v[f"full3_{part}"]
    value = total[place.at[second]]
    for k in range(3):
        value = value + full2[k].astype(f32)
    total3[...] = value
    yield from reduce_direct(links, place, third, lambda block: total3.at[block], full3, slot + 9)
    finish(total3[place.at[third]] + full3[0] + full3[1] + full3[2])


def reduce_query(links, place, first, v, out_ref):
    f32, bf16 = jnp.float32, jnp.bfloat16
    core, z_hi = place.core, place.z_hi
    grad_ref, pair_ref, wire = v["grad_query"], v["query_pair"], v["query_wire"]
    half, full, total, far_ref = v["query_half"], v["query_full"], v["query_sum"], v["query_far"]
    slot = links.slots(8)
    first()
    links.go(grad_ref.at[:, :, 1 - core], pair_ref, place.sibling, slot)
    yield
    links.arrived(pair_ref, place.sibling, slot)

    def pack(block, side, extra=None):
        value = grad_ref[block, side, core] + pair_ref[block, side]
        if extra is not None:
            value = value + extra[...].astype(f32)
        wire[block, side] = value.astype(bf16)

    yield from reduce_ring(
        links, place, "y", pack, lambda block, side: wire.at[block, side], half,
        lambda way, side: full.at[way, side], slot + 1,
    )
    own = place.at["y"]
    value = grad_ref[own, :, core] + pair_ref[own]
    total[...] = value + full[0].astype(f32) + full[1].astype(f32)
    links.go(total.at[1 - z_hi], far_ref, place.z_far, slot + 7)
    yield
    links.arrived(far_ref, place.z_far, slot + 7)
    out_ref[...] = total[z_hi] + far_ref[...]


def lanes_dot(left, right):
    return lax.dot_general(
        left, right, (((1,), (1,)), ((), ())), preferred_element_type=jnp.float32
    )


def rows_dot(left, right):
    return lax.dot_general(
        left, right, (((0,), (0,)), ((), ())), preferred_element_type=jnp.float32
    )


def dot(left, right):
    return jnp.dot(left, right, preferred_element_type=jnp.float32)


def step_kernel(
    cameras_ref, text_ref, flow_ref, hidden_ref, noise_ref, clean_ref, time_ref, input_ref, cot_ref,
    own_prefix_ref, own_action_ref, own_query_ref,
    attended_ref, out_query_ref, out_prefix_ref, out_action_ref,
    v,
):
    f32, bf16 = jnp.float32, jnp.bfloat16
    place = Place()
    core, y, z_hi, z_lo, x = place.core, place.at["y"], place.z_hi, place.z_lo, place.at["x"]
    seq = place.seq
    links = Links(v["send"], v["recv"])

    norm = v["norm"]
    loads = []
    chunks = [(s, start, count) for s in range(2) for start, count in ((0, 288), (288, 288), (576, 240))]
    for k, (s, start, count) in enumerate(chunks):
        load = pltpu.make_async_copy(
            hidden_ref.at[s, pl.ds(start, count), :],
            norm.at[pl.ds(s * KEYS + start, count), :],
            v["load"].at[k],
        )
        load.start()
        loads.append(load)

    query_weight = v["query_weight"]
    own_action = own_action_ref[...].astype(f32)
    own_action = jnp.concatenate([own_action[:, 0:256], own_action[:, 256:512]], axis=0)
    own_parts = (own_prefix_ref[:, 0:256], own_prefix_ref[:, 256:512], own_action.astype(bf16))
    for part, (first, second, third) in enumerate(ORDERS):
        at = place.at
        v[f"weight_{part}"][core, at[third], at[second], at[first]] = own_parts[part]
    query_weight[y, z_hi, core] = own_query_ref[...]
    turn, own_noisy = v["turn"], v["own_noisy"]
    turn[...] = jnp.zeros_like(turn)
    own_noisy[...] = jnp.zeros_like(own_noisy)
    for s in range(2):
        t = flow_ref[s]
        turn[:, 0:STEPS] = t * noise_ref[s].astype(f32) + (1.0 - t) * clean_ref[s].astype(f32)
        own_noisy[s * PAD_STEPS : (s + 1) * PAD_STEPS, 0:32] = (
            turn[...].T[0:PAD_STEPS].astype(bf16)
        )
    v["noisy"][seq] = own_noisy[...]
    v["time"][seq] = time_ref[...]
    place.greet()

    packet = links.slots(16)
    for offset in range(1, 8):
        to = (place.dp, place.group_member(offset))
        links.go(own_noisy, v["noisy"].at[seq], to, packet + offset)
        links.go(time_ref, v["time"].at[seq], to, packet + 8 + offset)

    act, act_t = v["act"], v["act_t"]

    def action_rows(offset):
        def run():
            member = place.group_member(offset, -1)
            if offset:
                to = (place.dp, member)
                links.arrived(v["noisy"].at[member], to, packet + offset)
                links.arrived(v["time"].at[member], to, packet + 8 + offset)
            wide = dot(v["noisy"][member][:, 0:32], input_ref[...])
            time = v["time"][member]
            pieces = []
            for s in range(2):
                rows = slice(s * PAD_STEPS, (s + 1) * PAD_STEPS)
                pieces.append(
                    jnp.concatenate(
                        [
                            wide[rows, i * 128 : (i + 1) * 128] + time[s * 8 + i : s * 8 + i + 1]
                            for i in range(8)
                        ],
                        axis=1,
                    )
                )
            wide = jnp.concatenate(pieces, axis=0)
            scale = lax.rsqrt(jnp.mean(wide * wide, axis=-1, keepdims=True) + EPS)
            rows = (wide * scale).astype(bf16)
            at = pl.ds(pl.multiple_of(member * 128, 128), 128)
            act[at, :] = rows
            act_t[:, at] = rows.T
            if offset == 0:
                row = lax.broadcasted_iota(jnp.int32, (128, 256), 0)
                col = lax.broadcasted_iota(jnp.int32, (128, 256), 1)
                within = col % 16
                origin = (col // 16) * 8 + within
                to_left = jnp.where((within < 8) & (row == origin), 1.0, 0.0).astype(bf16)
                to_right = jnp.where((within >= 8) & (row == origin - 8), 1.0, 0.0).astype(bf16)
                for i in range(8):
                    piece, cols = rows[:, i * 128 : (i + 1) * 128], slice(i * 256, (i + 1) * 256)
                    v["left"][:, cols] = dot(piece, to_left).astype(bf16)
                    v["right"][:, cols] = dot(piece, to_right).astype(bf16)

        return run

    def normalize(chunk):
        def run():
            loads[chunk].wait()
            s, start, count = chunks[chunk]

            def body(i, carry):
                places = [
                    pl.ds(pl.multiple_of(s * KEYS + start + i * 48 + j * 16, 16), 16)
                    for j in range(3)
                ]
                scales = []
                for at in places:
                    wide = norm[at, :].astype(f32)
                    scales.append(lax.rsqrt(jnp.mean(wide * wide, axis=-1, keepdims=True) + EPS))
                for at, scale in zip(places, scales):
                    norm[at, :] = (norm[at, :].astype(f32) * scale).astype(bf16)
                return carry

            lax.fori_loop(0, count // 48, body, 0)

        return run

    def place_cotangent():
        v["cot"][...] = jnp.zeros_like(v["cot"])
        for s in range(2):
            norm[s * KEYS + PREFIX : (s + 1) * KEYS, :] = jnp.zeros((KEYS - PREFIX, 2048), bf16)
        for s in range(2):
            for h in range(8):
                v["cot"][h, s * PAD_STEPS : s * PAD_STEPS + STEPS, :] = cot_ref[
                    :, s, h * 256 : (h + 1) * 256
                ]

    exchange = links.slots(16)

    def send_queries():
        wide = query_weight[...].reshape(1024, 256)
        for offset in (1, 2, 3, 4, 5, 6, 7, 0):
            member = place.group_member(offset)
            at = pl.ds(pl.multiple_of(member * 128, 128), 128)
            value = dot(act[at, :], wide).astype(bf16)
            if offset:
                v["query_out"][offset] = value
                links.go(
                    v["query_out"].at[offset], v["query"].at[seq], (place.dp, member),
                    exchange + offset,
                )
            else:
                v["query"][seq] = value

    works = [gather_query(links, place, query_weight, send_queries)]
    works += [gather_part(links, place, v[f"weight_{part}"], ORDERS[part]) for part in range(3)]
    rows = [action_rows(offset) for offset in range(8)]
    tasks = [rows[0], lambda: [rows[i]() for i in (1, 3, 4)], lambda: [rows[i]() for i in (2, 5, 6, 7)]]
    tasks += [normalize(chunk) for chunk in range(6)] + [place_cotangent]
    run_together(works, tasks)

    wp, kv = v["wp"], v["kv"]

    def block_rows(part, a, b):
        ref, order = v[f"weight_{part}"], ORDERS[part][::-1]
        pieces = []
        for c in range(2):
            for low in range(2):
                at = {"y": a, "z": b * 2 + low}
                if order[2] == "x":
                    pieces.append(ref[c, at[order[0]], at[order[1]]].reshape(64, 256))
                else:
                    for col in range(4):
                        at["x"] = col
                        pieces.append(ref[c, at[order[0]], at[order[1]], at[order[2]]])
        return pieces

    def unpack(k, carry):
        keys, values = carry
        a, b = k // 2, lax.rem(k, 2)
        for part in range(2):
            start = k * 256
            for piece in block_rows(part, a, b):
                at = pl.ds(pl.multiple_of(start, 16), piece.shape[0])
                wp[at, part * 256 : (part + 1) * 256] = piece
                start += piece.shape[0]
        block = jnp.concatenate(block_rows(2, a, b), axis=0)
        at = pl.ds(pl.multiple_of(k * 256, 256), 256)
        return keys + dot(v["left"][:, at], block), values + dot(v["right"][:, at], block)

    zero = jnp.zeros((2 * PAD_STEPS, 256), f32)
    keys, values = lax.fori_loop(0, 8, unpack, (zero, zero))
    keys, values = keys.astype(bf16), values.astype(bf16)

    def prefix(i, carry):
        at = pl.ds(pl.multiple_of(i * 256, 256), 256)
        kv[at, :] = dot(norm[at, :], wp[...]).astype(bf16)
        return carry

    lax.fori_loop(0, 7, prefix, 0)
    for s in range(2):
        rows = slice(s * PAD_STEPS, (s + 1) * PAD_STEPS)
        start = s * KEYS + PREFIX
        kv[start : start + PAD_STEPS, 0:256] = keys[rows]
        kv[start : start + PAD_STEPS, 256:512] = values[rows]

    for offset in range(1, 8):
        member = place.group_member(offset, -1)
        links.arrived(v["query"].at[member], (place.dp, member), exchange + offset)

    low_ref, ds_ref, gkv = v["low"], v["ds"], v["gkv"]
    logits_ref, dprob_ref = v["logits"], v["dprob"]

    def sixteenth(rows):
        return (rows.astype(f32) * 0.0625).astype(bf16)

    def sample(s, carry):
        length = cameras_ref[s] * IMG + text_ref[s]
        mine = pl.ds(pl.multiple_of(s * PAD_STEPS, PAD_STEPS), PAD_STEPS)
        start = pl.multiple_of(s * KEYS, 128)
        tokens = pl.ds(start, KEYS)
        column = lax.broadcasted_iota(jnp.int32, (1, KEYS), 1)
        valid = (column < length) | ((column >= PREFIX) & (column < PREFIX + STEPS))
        bias = jnp.where(valid, 0.0, -1e30)
        for i in range(2):
            heads = slice(i * 4, i * 4 + 4)
            half = slice(i * 256, (i + 1) * 256)
            query = v["query"][heads, mine, :].reshape(256, 256)
            cot = v["cot"][heads, mine, :].reshape(256, 256)
            logits_ref[...] = lanes_dot(sixteenth(query), kv[tokens, 0:256])
            dprob_ref[...] = lanes_dot(sixteenth(cot), kv[tokens, 256:512])

            def softmax(b, carry):
                at = pl.ds(pl.multiple_of(b * 16, 16), 16)
                to = pl.ds(pl.multiple_of(i * 256 + b * 16, 16), 16)
                logits = logits_ref[at, :] + bias
                expo = jnp.exp(logits - jnp.max(logits, axis=-1, keepdims=True))
                probs = expo * (1.0 / jnp.sum(expo, axis=-1, keepdims=True))
                low_ref[to, :] = probs.astype(bf16)
                dprob = dprob_ref[at, :]
                inner = jnp.sum(probs * dprob, axis=-1, keepdims=True)
                ds_ref[to, :] = (probs * (dprob - inner)).astype(bf16)
                return carry

            lax.fori_loop(0, 16, softmax, 0, unroll=4)
            attended = dot(low_ref[half, :], kv[tokens, 256:512]).astype(bf16)
            for j in range(4):
                at = slice((i * 4 + j) * 256, (i * 4 + j + 1) * 256)
                attended_ref[s, :, at] = attended[j * 64 : j * 64 + STEPS]
            grad = dot(ds_ref[half, :], kv[tokens, 0:256]).astype(bf16)
            v["gq"][heads, mine, :] = grad.reshape(4, 64, 256)
        for h in range(8):
            v["query_t"][h] = v["query"][h, mine, :].T
            v["cot_t"][h] = v["cot"][h, mine, :].T

        def tile(t, carry):
            at = pl.ds(pl.multiple_of(t * 128, 128), 128)
            to = pl.ds(pl.multiple_of(s * KEYS + t * 128, 128), 128)
            for left, right, top in ((v["query_t"], ds_ref, 0), (v["cot_t"], low_ref, 256)):
                total = jnp.zeros((256, 128), f32)
                for h in range(8):
                    term = dot(left[h], right[h * 64 : (h + 1) * 64, at])
                    total = total + term.astype(bf16).astype(f32)
                gkv[top : top + 256, to] = total.astype(bf16)
            return carry

        lax.fori_loop(0, 7, tile, 0)
        return carry

    lax.fori_loop(0, 2, sample, 0)

    for offset in range(1, 8):
        member = place.group_member(offset)
        links.go(
            v["gq"].at[member], v["group_gq"].at[seq], (place.dp, member), exchange + 8 + offset
        )
    v["group_gq"][seq] = v["gq"][seq]

    for s in range(2):
        turned = gkv[:, s * KEYS + PREFIX - 48 : (s + 1) * KEYS].astype(f32).T[48 : 48 + PAD_STEPS]
        ds_ref[s * 64 : (s + 1) * 64, 0:512] = turned.astype(bf16)
    grad, pair = v["grad"], v["pair"]
    pairing = links.slots(8)

    def pair_op(k):
        a, b = k // 2, lax.rem(k, 2)
        return links.op(
            grad.at[a, b, 1 - core], pair.at[a, pl.ds(b * 2, 2)], place.sibling, pairing + k
        )

    def grad_prefix(k, carry):
        at = pl.ds(pl.multiple_of(k * 256, 256), 256)
        a, b = k // 2, lax.rem(k, 2)
        value = dot(gkv[...], norm[:, at])
        value = value.T
        grad[a, b, :, :, :, 0:16, :] = value[:, 0:256].reshape(2, 2, 4, 16, 256)
        grad[a, b, :, :, :, 16:32, :] = value[:, 256:512].reshape(2, 2, 4, 16, 256)
        action = rows_dot(v["left"][:, at], ds_ref[0:128, 0:256])
        action += rows_dot(v["right"][:, at], ds_ref[0:128, 256:512])
        grad[a, b, :, :, :, 32:48, :] = action.reshape(2, 2, 4, 16, 256)
        pair_op(k).start()
        return carry

    lax.fori_loop(0, 8, grad_prefix, 0)
    for k in range(8):
        pair_op(k).wait_recv()

    def grad_query():
        for offset in range(1, 8):
            member = place.group_member(offset, -1)
            links.arrived(v["group_gq"].at[member], (place.dp, member), exchange + 8 + offset)
        rows = v["group_gq"][...].reshape(1024, 256)
        for a in range(4):
            value = dot(act_t[a * 256 : (a + 1) * 256, :], rows)
            v["grad_query"][a] = value.reshape(2, 2, 64, 256)

    def finish(part):
        def store(value):
            if part == 2:
                out_action_ref[:, 0:256] = value[0:8]
                out_action_ref[:, 256:512] = value[8:16]
            else:
                out_prefix_ref[:, part * 256 : (part + 1) * 256] = value

        return store

    works = [reduce_part(links, place, grad, pair, v, part, finish(part)) for part in range(3)]
    works.append(reduce_query(links, place, grad_query, v, out_query_ref))
    run_together(works)
    for op in links.sent:
        op.wait_send()
    for k in range(8):
        pair_op(k).wait_send()


def step(cameras, text_length, flow_time, hidden, noise, clean, time, input_weight, cot, own_prefix, own_action, own_query):
    bf16, f32 = jnp.bfloat16, jnp.float32
    smem, vmem = pl.BlockSpec(memory_space=pltpu.SMEM), pl.BlockSpec(memory_space=pltpu.VMEM)
    scratch = dict(
        norm=pltpu.VMEM((2 * KEYS, 2048), bf16),
        turn=pltpu.VMEM((32, 128), f32),
        own_noisy=pltpu.VMEM((128, 128), bf16),
        query_weight=pltpu.VMEM((4, 2, 2, 64, 256), bf16),
        noisy=pltpu.VMEM((8, 128, 128), bf16),
        time=pltpu.VMEM((8, 16, 128), f32),
        act=pltpu.VMEM((1024, 1024), bf16),
        act_t=pltpu.VMEM((1024, 1024), bf16),
        left=pltpu.VMEM((128, 2048), bf16),
        right=pltpu.VMEM((128, 2048), bf16),
        cot=pltpu.VMEM((8, 128, 256), bf16),
        query=pltpu.VMEM((8, 128, 256), bf16),
        query_out=pltpu.VMEM((8, 128, 256), bf16),
        gq=pltpu.VMEM((8, 128, 256), bf16),
        group_gq=pltpu.VMEM((8, 128, 256), bf16),
        wp=pltpu.VMEM((2048, 512), bf16),
        kv=pltpu.VMEM((2 * KEYS, 512), bf16),
        low=pltpu.VMEM((512, KEYS), bf16),
        ds=pltpu.VMEM((512, KEYS), bf16),
        logits=pltpu.VMEM((256, KEYS), f32),
        dprob=pltpu.VMEM((256, KEYS), f32),
        query_t=pltpu.VMEM((8, 256, 64), bf16),
        cot_t=pltpu.VMEM((8, 256, 64), bf16),
        gkv=pltpu.VMEM((512, 2 * KEYS), bf16),
        grad=pltpu.VMEM((4, 2, 2, 2, 4, ROWS, 256), f32),
        pair=pltpu.VMEM((4, 4, 4, ROWS, 256), f32),
        grad_query=pltpu.VMEM((4, 2, 2, 64, 256), f32),
        query_pair=pltpu.VMEM((4, 2, 64, 256), f32),
        query_wire=pltpu.VMEM((4, 2, 64, 256), bf16),
        query_half=pltpu.VMEM((2, 64, 256), bf16),
        query_full=pltpu.VMEM((2, 2, 64, 256), bf16),
        query_sum=pltpu.VMEM((2, 64, 256), f32),
        query_far=pltpu.VMEM((64, 256), f32),
        send=pltpu.SemaphoreType.DMA((192,)),
        recv=pltpu.SemaphoreType.DMA((192,)),
        load=pltpu.SemaphoreType.DMA((6,)),
    )
    for part in range(3):
        scratch[f"weight_{part}"] = pltpu.VMEM((2, 4, 4, 4, 16, 256), bf16)
        scratch[f"wire1_{part}"] = pltpu.VMEM((4, 4, 4, 16, 256), bf16)
        scratch[f"half1_{part}"] = pltpu.VMEM((2, 2, 4, 16, 256), bf16)
        scratch[f"full1_{part}"] = pltpu.VMEM((2, 4, 4, 16, 256), bf16)
        scratch[f"sum2_{part}"] = pltpu.VMEM((4, 4, 16, 256), f32)
        scratch[f"wire2_{part}"] = pltpu.VMEM((4, 4, 16, 256), bf16)
        scratch[f"full2_{part}"] = pltpu.VMEM((3, 4, 16, 256), bf16)
        scratch[f"sum3_{part}"] = pltpu.VMEM((4, 16, 256), f32)
        scratch[f"full3_{part}"] = pltpu.VMEM((3, 16, 256), f32)
    return pl.pallas_call(
        step_kernel,
        out_shape=(
            jax.ShapeDtypeStruct((2, STEPS, 2048), bf16),
            jax.ShapeDtypeStruct((64, 256), f32),
            jax.ShapeDtypeStruct((16, 512), f32),
            jax.ShapeDtypeStruct((8, 512), f32),
        ),
        in_specs=[smem] * 3 + [pl.BlockSpec(memory_space=pl.ANY)] + [vmem] * 8,
        out_specs=(vmem,) * 4,
        scratch_shapes=[scratch],
        compiler_params=pltpu.CompilerParams(
            collective_id=1, has_side_effects=True, vmem_limit_bytes=VMEM_LIMIT
        ),
        cost_estimate=pl.CostEstimate(
            flops=10**10, bytes_accessed=9 * 10**6, transcendentals=10**6
        ),
        name="step",
    )(
        cameras, text_length, flow_time, hidden, noise, clean, time, input_weight, cot,
        own_prefix, own_action, own_query,
    )


def time_feature(flow_col, row_width):
    half_width = row_width // 2
    fraction = jnp.arange(half_width, dtype=jnp.float32) / (half_width - 1)
    period = 0.004 * 1000.0**fraction
    angle = flow_col[..., None] * (2.0 * math.pi / period)
    return jnp.concatenate([jnp.sin(angle), jnp.cos(angle)], axis=-1)


def on_device(
    prefix_hidden,
    cameras,
    text_length,
    action_noise,
    clean_actions,
    flow_time,
    input_weight,
    prefix_kv_weight,
    action_kv_weight,
    query_weight,
    cotangent,
):
    time = time_feature(flow_time, 1024).reshape(16, 128)
    return step(
        cameras,
        text_length,
        flow_time,
        prefix_hidden,
        action_noise.transpose(0, 2, 1),
        clean_actions.transpose(0, 2, 1),
        time,
        input_weight,
        cotangent.transpose(1, 0, 2),
        prefix_kv_weight,
        action_kv_weight,
        query_weight,
    )


def solution(mesh):
    return jax.shard_map(
        on_device,
        mesh=mesh,
        in_specs=(
            P(("dp", "seq"), None, None),
            P(("dp", "seq")),
            P(("dp", "seq")),
            P(("dp", "seq"), None, None),
            P(("dp", "seq"), None, None),
            P(("dp", "seq")),
            P(),
            P(("dp", "seq"), None),
            P(("dp", "seq"), None),
            P("dp", "seq"),
            P(("dp", "seq"), None, None),
        ),
        out_specs=(
            P(("dp", "seq"), None, None),
            P("dp", "seq"),
            P(("dp", "seq"), None),
            P(("dp", "seq"), None),
        ),
        check_vma=False,
    )
```

```python
import math

import jax
import jax.numpy as jnp
from jax import lax
from jax.experimental import pallas as pl
from jax.experimental.pallas import tpu as pltpu
from jax.sharding import PartitionSpec as P

IMG = 256
EPS = 1e-06
MESH = pl.DeviceIdType.MESH
VMEM_LIMIT = 50 * 1024 * 1024
PREFIX, STEPS, PAD_STEPS, KEYS = 816, 50, 64, 896

ROWS = 48
ORDERS = ("xyz", "yzx", "zxy")
HALVES = (slice(0, 2), slice(2, 4))
FULL = slice(None)


class Place:
    def __init__(self):
        self.dp = lax.axis_index("dp")
        self.seq = lax.axis_index("seq")
        self.core = lax.rem(self.dp, 2)
        self.z_hi = lax.rem(self.dp // 2, 2)
        self.z_lo = self.seq // 4
        self.at = {
            "y": self.dp // 4,
            "z": self.z_hi * 2 + self.z_lo,
            "x": lax.rem(self.seq, 4),
        }
        self.sibling = self.device(core=1 - self.core)
        self.z_far = self.device(z=self.shifted("z", 2))

    def device(self, core=None, **moved):
        at = {**self.at, **moved}
        core = self.core if core is None else core
        return (
            at["y"] * 4 + (at["z"] // 2) * 2 + core,
            lax.rem(at["z"], 2) * 4 + at["x"],
        )

    def shifted(self, axis, by):
        return lax.rem(self.at[axis] + by, 4)

    def group_member(self, offset, sign=1):
        z_lo = lax.rem(self.z_lo + lax.div(offset, 4), 2)
        x = lax.rem(self.at["x"] + sign * lax.rem(offset, 4) + 4, 4)
        return z_lo * 4 + x

    def greet(self):
        barrier = pltpu.get_barrier_semaphore()
        others = [self.sibling, self.z_far]
        others += [(self.dp, self.group_member(offset)) for offset in range(1, 8)]
        others += [self.device(y=self.shifted("y", by)) for by in (1, 2, 3)]
        beyond = lax.rem(self.at["z"] + 3 + 2 * self.z_lo, 4)
        others.append(self.device(z=beyond))
        for other in others:
            pl.semaphore_signal(barrier, inc=1, device_id=other, device_id_type=MESH)
        self.greeted = len(others)

    def meet(self):
        pl.semaphore_wait(pltpu.get_barrier_semaphore(), self.greeted)


class Links:
    def __init__(self, send_sem, recv_sem):
        self.send_sem, self.recv_sem = send_sem, recv_sem
        self.used = 0
        self.sent = []

    def slots(self, count):
        self.used += count
        return self.used - count

    def op(self, src, dst, to, slot):
        return pltpu.make_async_remote_copy(
            src_ref=src,
            dst_ref=dst,
            send_sem=self.send_sem.at[slot],
            recv_sem=self.recv_sem.at[slot],
            device_id=to,
            device_id_type=MESH,
        )

    def go(self, src, dst, to, slot):
        op = self.op(src, dst, to, slot)
        op.start()
        self.sent.append(op)

    def arrived(self, dst, to, slot):
        self.op(dst, dst, to, slot).wait_recv()


def run_together(works, tasks=()):
    live, tasks = list(works), list(tasks)
    while live or tasks:
        live = [work for work in live if next(work, "end") != "end"]
        if tasks:
            tasks.pop(0)()


def direct(links, place, axis, view, slot):
    own = place.at[axis]
    for by in (1, 3, 2):
        to = place.device(**{axis: place.shifted(axis, by)})
        links.go(view(own), view(own), to, slot + by - 1)
    yield
    for by in (1, 3, 2):
        links.arrived(view(place.shifted(axis, 4 - by)), place.sibling, slot + by - 1)


def ring(links, place, axis, view, slot, landed):
    own, right, left, across = (place.shifted(axis, by) for by in (0, 1, 3, 2))
    to_right, to_left = (place.device(**{axis: at}) for at in (right, left))
    links.go(view(own), view(own), to_right, slot)
    links.go(view(own), view(own), to_left, slot + 1)
    landed(own)
    yield
    links.arrived(view(left), to_right, slot)
    links.go(view(left, 0), view(left, 0), to_right, slot + 2)
    links.arrived(view(right), to_left, slot + 1)
    links.go(view(right, 1), view(right, 1), to_left, slot + 3)
    landed(left)
    landed(right)
    yield
    links.arrived(view(across, 0), to_right, slot + 2)
    links.arrived(view(across, 1), to_left, slot + 3)
    landed(across)


class Share:
    def __init__(self, links, place, view):
        self.links, self.place, self.view = links, place, view
        self.slot, self.due = links.slots(4), []

    def __call__(self, block):
        links, core = self.links, self.place.core
        slot = self.slot + len(self.due)
        mine = self.view(core, block)
        links.go(mine, mine, self.place.sibling, slot)
        self.due.append((self.view(1 - core, block), slot))

    def wait(self):
        for view, slot in self.due:
            self.links.arrived(view, self.place.sibling, slot)


def gather_part(links, place, ref, order):
    core = place.core
    first, second, third = order
    slot = links.slots(10)
    at = place.at
    yield from direct(
        links, place, first, lambda block: ref.at[core, at[third], at[second], block], slot
    )
    yield from direct(links, place, second, lambda block: ref.at[core, at[third], block], slot + 3)
    share = Share(links, place, lambda core, block: ref.at[core, block])

    def view(block, half=None):
        return ref.at[core, block] if half is None else ref.at[core, block, HALVES[half]]

    yield from ring(links, place, third, view, slot + 6, share)
    yield
    share.wait()


def gather_query(links, place, query_ref, then):
    core, y, z_hi = place.core, place.at["y"], place.z_hi
    slot = links.slots(5)
    links.go(query_ref.at[y, z_hi, core], query_ref.at[y, z_hi, core], place.z_far, slot)
    yield
    links.arrived(query_ref.at[y, 1 - z_hi, core], place.z_far, slot)
    share = Share(links, place, lambda core, block: query_ref.at[block, :, core])

    def view(block, half=None):
        return query_ref.at[block, FULL if half is None else half, core]

    yield from ring(links, place, "y", view, slot + 1, share)
    yield
    share.wait()
    then()


def reduce_ring(links, place, axis, pack, wire, half, fulls, slot):
    own, right, left, across = (place.shifted(axis, by) for by in (0, 1, 3, 2))
    to_right, to_left = (place.device(**{axis: at}) for at in (right, left))
    pack(across, 0)
    links.go(wire(across, 0), half.at[0], to_right, slot)
    pack(across, 1)
    links.go(wire(across, 1), half.at[1], to_left, slot + 1)
    yield
    pack(right, 1)
    links.go(wire(right, 1), fulls(0, 1), to_right, slot + 2)
    pack(left, 0)
    links.go(wire(left, 0), fulls(1, 0), to_left, slot + 3)
    yield
    links.arrived(half.at[0], to_right, slot)
    pack(right, 0, half.at[0])
    links.go(wire(right, 0), fulls(0, 0), to_right, slot + 4)
    links.arrived(half.at[1], to_left, slot + 1)
    pack(left, 1, half.at[1])
    links.go(wire(left, 1), fulls(1, 1), to_left, slot + 5)
    yield
    links.arrived(fulls(0, 1), to_right, slot + 2)
    links.arrived(fulls(1, 0), to_left, slot + 3)
    links.arrived(fulls(0, 0), to_right, slot + 4)
    links.arrived(fulls(1, 1), to_left, slot + 5)


def reduce_direct(links, place, axis, block_of, landing, slot):
    for by in (2, 1, 3):
        block = place.shifted(axis, by)
        links.go(
            block_of(block), landing.at[by - 1], place.device(**{axis: block}), slot + by - 1
        )
    yield
    for by in (1, 3, 2):
        links.arrived(landing.at[by - 1], place.sibling, slot + by - 1)


def reduce_part(links, place, grad_ref, pair_ref, v, part, finish):
    f32, bf16 = jnp.float32, jnp.bfloat16
    rows = slice(part * 16, part * 16 + 16)
    core = place.core
    first, second, third = ORDERS[part]
    wire, half, full = (v[f"{name}1_{part}"] for name in ("wire", "half", "full"))
    slot = links.slots(12)

    def mine(block, i, j):
        at = {first: block, second: i, third: j}
        y, z, x = at["y"], at["z"], at["x"]
        return grad_ref[y, z // 2, core, lax.rem(z, 2), x, rows, :] + pair_ref[y, z, x, rows, :]

    def pack(block, side, extra=None):
        for i in range(2):
            for j in range(4):
                value = mine(block, side * 2 + i, j)
                if extra is not None:
                    value = value + extra[i, j].astype(f32)
                wire[block, side * 2 + i, j] = value.astype(bf16)

    yield from reduce_ring(
        links, place, first, pack, lambda block, side: wire.at[block, HALVES[side]], half,
        lambda way, side: full.at[way, HALVES[side]], slot,
    )
    total, wire2, full2 = (v[f"{name}2_{part}"] for name in ("sum", "wire", "full"))
    for i in range(4):
        for j in range(4):
            value = mine(place.at[first], i, j)
            value = value + full[0, i, j].astype(f32) + full[1, i, j].astype(f32)
            total[i, j] = value
            wire2[i, j] = value.astype(bf16)
    yield from reduce_direct(links, place, second, lambda block: wire2.at[block], full2, slot + 6)
    total3, full3 = v[f"sum3_{part}"], v[f"full3_{part}"]
    value = total[place.at[second]]
    for k in range(3):
        value = value + full2[k].astype(f32)
    total3[...] = value
    yield from reduce_direct(links, place, third, lambda block: total3.at[block], full3, slot + 9)
    finish(total3[place.at[third]] + full3[0] + full3[1] + full3[2])


def reduce_query(links, place, first, v, out_ref):
    f32, bf16 = jnp.float32, jnp.bfloat16
    core, z_hi = place.core, place.z_hi
    grad_ref, pair_ref, wire = v["grad_query"], v["query_pair"], v["query_wire"]
    half, full, total, far_ref = v["query_half"], v["query_full"], v["query_sum"], v["query_far"]
    slot = links.slots(8)
    first()
    links.go(grad_ref.at[:, :, 1 - core], pair_ref, place.sibling, slot)
    yield
    links.arrived(pair_ref, place.sibling, slot)

    def pack(block, side, extra=None):
        value = grad_ref[block, side, core] + pair_ref[block, side]
        if extra is not None:
            value = value + extra[...].astype(f32)
        wire[block, side] = value.astype(bf16)

    yield from reduce_ring(
        links, place, "y", pack, lambda block, side: wire.at[block, side], half,
        lambda way, side: full.at[way, side], slot + 1,
    )
    own = place.at["y"]
    value = grad_ref[own, :, core] + pair_ref[own]
    total[...] = value + full[0].astype(f32) + full[1].astype(f32)
    links.go(total.at[1 - z_hi], far_ref, place.z_far, slot + 7)
    yield
    links.arrived(far_ref, place.z_far, slot + 7)
    out_ref[...] = total[z_hi] + far_ref[...]


def lanes_dot(left, right):
    return lax.dot_general(
        left, right, (((1,), (1,)), ((), ())), preferred_element_type=jnp.float32
    )


def dot(left, right):
    return jnp.dot(left, right, preferred_element_type=jnp.float32)


def step_kernel(
    cameras_ref, text_ref, flow_ref, hidden_ref, noise_ref, clean_ref, sin_ref, cos_ref, input_ref, cot_ref,
    own_prefix_ref, own_action_ref, own_query_ref,
    attended_ref, out_query_ref, out_prefix_ref, out_action_ref,
    v,
):
    f32, bf16 = jnp.float32, jnp.bfloat16
    place = Place()
    core, y, z_hi, z_lo, x = place.core, place.at["y"], place.z_hi, place.z_lo, place.at["x"]
    seq = place.seq
    links = Links(v["send"], v["recv"])
    place.greet()

    norm = v["norm"]
    loads = []
    chunks = [(s, start, count) for s in range(2) for start, count in ((0, 288), (288, 288), (576, 240))]
    for k, (s, start, count) in enumerate(chunks):
        load = pltpu.make_async_copy(
            hidden_ref.at[s, pl.ds(start, count), :],
            norm.at[pl.ds(s * KEYS + start, count), :],
            v["load"].at[k],
        )
        load.start()
        loads.append(load)

    query_weight = v["query_weight"]
    own_action = own_action_ref[...].astype(f32)
    own_action = jnp.concatenate([own_action[:, 0:256], own_action[:, 256:512]], axis=0)
    own_parts = (own_prefix_ref[:, 0:256], own_prefix_ref[:, 256:512], own_action.astype(bf16))
    for part, (first, second, third) in enumerate(ORDERS):
        at = place.at
        v[f"weight_{part}"][core, at[third], at[second], at[first]] = own_parts[part]
    query_weight[y, z_hi, core] = own_query_ref[...]
    turn, own_noisy = v["turn"], v["own_noisy"]
    turn[...] = jnp.zeros_like(turn)
    own_noisy[...] = jnp.zeros_like(own_noisy)
    for s in range(2):
        t = flow_ref[s]
        turn[:, 0:STEPS] = t * noise_ref[s].astype(f32) + (1.0 - t) * clean_ref[s].astype(f32)
        own_noisy[s * PAD_STEPS : (s + 1) * PAD_STEPS, 0:32] = (
            turn[...].T[0:PAD_STEPS].astype(bf16)
        )
    v["noisy"][seq] = own_noisy[...]
    own_time = v["own_time"]
    own_time[:, 0:512] = sin_ref[...]
    own_time[:, 512:1024] = cos_ref[...]
    v["time"][seq] = own_time[...]
    place.meet()

    eye = v["eye"]
    row = lax.broadcasted_iota(jnp.int32, (256, 256), 0)
    col = lax.broadcasted_iota(jnp.int32, (256, 256), 1)
    eye[...] = jnp.where(row == col, 1.0, 0.0).astype(bf16)

    packet = links.slots(16)
    for offset in range(1, 8):
        to = (place.dp, place.group_member(offset))
        links.go(own_noisy, v["noisy"].at[seq], to, packet + offset)
        links.go(own_time, v["time"].at[seq], to, packet + 8 + offset)

    act, act_t = v["act"], v["act_t"]

    def make_rows(member):
        at = pl.ds(pl.multiple_of(member * 128, 128), 128)
        wide = dot(v["noisy"][member][:, 0:32], input_ref[...])
        time = v["time"][member]
        parts = []
        for s in range(2):
            part = wide[s * PAD_STEPS : (s + 1) * PAD_STEPS] + time[s : s + 1]
            scale = lax.rsqrt(jnp.mean(part * part, axis=-1, keepdims=True) + EPS)
            parts.append((part * scale).astype(bf16))
        rows = jnp.concatenate(parts, axis=0)
        act[at, :] = rows
        for f in range(4):
            cols = slice(f * 256, (f + 1) * 256)
            act_t[cols, at] = lanes_dot(eye[...], rows[:, cols]).astype(bf16)

    def spread_rows():
        at = pl.ds(pl.multiple_of(seq * 128, 128), 128)
        feature = lax.broadcasted_iota(jnp.int32, (256, 128), 1)
        k = lax.broadcasted_iota(jnp.int32, (256, 128), 0)
        within = k % 16
        origin = (k // 16) * 8 + within
        first = jnp.where((within < 8) & (feature == origin), 1.0, 0.0).astype(bf16)
        second = jnp.where((within >= 8) & (feature == origin - 8), 1.0, 0.0).astype(bf16)
        for spread, name in ((first, "left"), (second, "right")):
            for i in range(8):
                cols, wide = slice(i * 128, (i + 1) * 128), slice(i * 256, (i + 1) * 256)
                v[name][:, wide] = lanes_dot(act[at, cols], spread).astype(bf16)
                v[name + "_t"][wide, :] = dot(spread, act_t[cols, at]).astype(bf16)

    def group_rows(low, high):
        def run():
            members = [place.group_member(offset, -1) for offset in range(low, high)]
            for offset, member in zip(range(low, high), members):
                if offset == 0:
                    continue
                to = (place.dp, member)
                links.arrived(v["noisy"].at[member], to, packet + offset)
                links.arrived(v["time"].at[member], to, packet + 8 + offset)
            for member in members:
                make_rows(member)

        return run

    def normalize(chunk):
        def run():
            loads[chunk].wait()
            s, start, count = chunks[chunk]

            def places(i):
                return [
                    pl.ds(pl.multiple_of(s * KEYS + start + i * 48 + j * 16, 16), 16)
                    for j in range(3)
                ]

            def scales(i):
                found = []
                for at in places(i):
                    wide = norm[at, :].astype(f32)
                    found.append(lax.rsqrt(jnp.mean(wide * wide, axis=-1, keepdims=True) + EPS))
                return tuple(found)

            def body(i, present):
                following = scales(jnp.minimum(i + 1, count // 48 - 1))
                for at, scale in zip(places(i), present):
                    norm[at, :] = (norm[at, :].astype(f32) * scale).astype(bf16)
                return following

            lax.fori_loop(0, count // 48, body, scales(0))

        return run

    def place_rows():
        v["cot"][...] = jnp.zeros_like(v["cot"])
        for s in range(2):
            for h in range(8):
                v["cot"][h, s * PAD_STEPS : s * PAD_STEPS + STEPS, :] = cot_ref[
                    :, s, h * 256 : (h + 1) * 256
                ]
        for s in range(2):
            norm[s * KEYS + PREFIX : (s + 1) * KEYS, :] = jnp.zeros((KEYS - PREFIX, 2048), bf16)

    exchange = links.slots(16)

    def send_queries():
        wide = query_weight[...].reshape(1024, 256)
        for half in range(2):
            rows = slice(half * 512, (half + 1) * 512)
            value = dot(act[rows, :], wide).astype(bf16)
            v["query_out"][half * 4 : half * 4 + 4] = value.reshape(4, 128, 256)
        for offset in range(1, 8):
            member = place.group_member(offset)
            links.go(
                v["query_out"].at[member], v["query"].at[seq], (place.dp, member),
                exchange + offset,
            )
        v["query"][seq] = v["query_out"][seq]

    works = [gather_query(links, place, query_weight, send_queries)]
    works += [gather_part(links, place, v[f"weight_{part}"], ORDERS[part]) for part in range(3)]
    tasks = [normalize(0), normalize(1), group_rows(0, 4), group_rows(4, 8)]
    tasks += [normalize(chunk) for chunk in range(2, 6)] + [spread_rows, place_rows]
    run_together(works, tasks)

    wp, kv = v["wp"], v["kv"]

    def block_rows(part, a, b):
        ref, order = v[f"weight_{part}"], ORDERS[part][::-1]
        pieces = []
        for c in range(2):
            for low in range(2):
                at = {"y": a, "z": b * 2 + low}
                if order[2] == "x":
                    pieces.append(ref[c, at[order[0]], at[order[1]]].reshape(64, 256))
                else:
                    for col in range(4):
                        at["x"] = col
                        pieces.append(ref[c, at[order[0]], at[order[1]], at[order[2]]])
        return pieces

    def unpack(k, carry):
        keys, values = carry
        a, b = k // 2, lax.rem(k, 2)
        for part in range(2):
            start = k * 256
            for piece in block_rows(part, a, b):
                at = pl.ds(pl.multiple_of(start, 16), piece.shape[0])
                wp[at, part * 256 : (part + 1) * 256] = piece
                start += piece.shape[0]
        block = jnp.concatenate(block_rows(2, a, b), axis=0)
        at = pl.ds(pl.multiple_of(k * 256, 256), 256)
        return keys + dot(v["left"][:, at], block), values + dot(v["right"][:, at], block)

    zero = jnp.zeros((2 * PAD_STEPS, 256), f32)
    keys, values = lax.fori_loop(0, 8, unpack, (zero, zero))
    keys, values = keys.astype(bf16), values.astype(bf16)

    def prefix(i, carry):
        at = pl.ds(pl.multiple_of(i * 448, 64), 448)
        kv[at, :] = dot(norm[at, :], wp[...]).astype(bf16)
        return carry

    lax.fori_loop(0, 4, prefix, 0)
    for s in range(2):
        rows = slice(s * PAD_STEPS, (s + 1) * PAD_STEPS)
        start = s * KEYS + PREFIX
        kv[start : start + PAD_STEPS, 0:256] = keys[rows]
        kv[start : start + PAD_STEPS, 256:512] = values[rows]

    for offset in range(1, 8):
        member = place.group_member(offset, -1)
        links.arrived(v["query"].at[member], (place.dp, member), exchange + offset)

    low_ref, ds_ref, gkv = v["low"], v["ds"], v["gkv"]

    def sixteenth(rows):
        return (rows.astype(f32) * 0.0625).astype(bf16)

    def sample(s, carry):
        length = cameras_ref[s] * IMG + text_ref[s]
        mine = pl.ds(pl.multiple_of(s * PAD_STEPS, PAD_STEPS), PAD_STEPS)
        start = pl.multiple_of(s * KEYS, 128)
        tokens = pl.ds(start, KEYS)
        column = lax.broadcasted_iota(jnp.int32, (1, KEYS), 1)
        valid = (column < length) | ((column >= PREFIX) & (column < PREFIX + STEPS))
        bias = jnp.where(valid, 0.0, -1e30)
        query = v["query"][:, mine, :].reshape(512, 256)
        cot = v["cot"][:, mine, :].reshape(512, 256)
        logits = lanes_dot(sixteenth(query), kv[tokens, 0:256]) + bias
        expo = jnp.exp(logits - jnp.max(logits, axis=-1, keepdims=True))
        probs = expo * (1.0 / jnp.sum(expo, axis=-1, keepdims=True))
        low_ref[...] = probs.astype(bf16)
        dprob = lanes_dot(sixteenth(cot), kv[tokens, 256:512])
        inner = jnp.sum(probs * dprob, axis=-1, keepdims=True)
        ds_ref[...] = (probs * (dprob - inner)).astype(bf16)
        v["gq"][:, mine, :] = dot(ds_ref[...], kv[tokens, 0:256]).astype(bf16).reshape(8, 64, 256)
        attended = dot(low_ref[...], kv[tokens, 256:512]).astype(bf16)
        for h in range(8):
            attended_ref[s, :, h * 256 : (h + 1) * 256] = attended[h * 64 : h * 64 + STEPS]

        first = lax.broadcasted_iota(jnp.int32, (256, 128), 1) < 64
        for rows, turned in ((query, v["query_t"]), (cot, v["cot_t"])):
            across = lanes_dot(eye[...], rows)
            for h in range(8):
                pair = across[:, (h // 2) * 128 : (h // 2 + 1) * 128]
                keep = first if h % 2 == 0 else jnp.logical_not(first)
                turned[h] = jnp.where(keep, pair, 0.0).astype(bf16)

        def tile(begin, width):
            at = pl.ds(begin, width)
            to = pl.ds(pl.multiple_of(start + begin, 128), width)
            for left, right, top in ((v["query_t"], ds_ref, 0), (v["cot_t"], low_ref, 256)):
                total = jnp.zeros((256, width), f32)
                for h in range(8):
                    term = dot(left[h], right[(h // 2) * 128 : (h // 2 + 1) * 128, at])
                    total = total + term.astype(bf16).astype(f32)
                gkv[top : top + 256, to] = total.astype(bf16)

        def wide_tile(t, carry):
            tile(pl.multiple_of(t * 256, 256), 256)
            return carry

        lax.fori_loop(0, 3, wide_tile, 0)
        tile(768, 128)
        return carry

    lax.fori_loop(0, 2, sample, 0)

    for offset in range(1, 8):
        member = place.group_member(offset)
        links.go(
            v["gq"].at[member], v["group_gq"].at[seq], (place.dp, member), exchange + 8 + offset
        )
    v["group_gq"][seq] = v["gq"][seq]

    for s in range(2):
        turned = gkv[:, s * KEYS + PREFIX - 48 : (s + 1) * KEYS].astype(f32).T[48 : 48 + PAD_STEPS]
        ds_ref[s * 64 : (s + 1) * 64, 0:512] = turned.astype(bf16)
    grad, pair = v["grad"], v["pair"]
    pairing = links.slots(8)

    def pair_op(k):
        a, b = k // 2, lax.rem(k, 2)
        return links.op(
            grad.at[a, b, 1 - core], pair.at[a, pl.ds(b * 2, 2)], place.sibling, pairing + k
        )

    def grad_prefix(k, carry):
        at = pl.ds(pl.multiple_of(k * 256, 256), 256)
        a, b = k // 2, lax.rem(k, 2)
        value = dot(gkv[...], norm[:, at])
        high = value.astype(bf16)
        low = (value - high.astype(f32)).astype(bf16)
        value = lanes_dot(eye[...], high) + lanes_dot(eye[...], low)
        grad[a, b, :, :, :, 0:16, :] = value[:, 0:256].reshape(2, 2, 4, 16, 256)
        grad[a, b, :, :, :, 16:32, :] = value[:, 256:512].reshape(2, 2, 4, 16, 256)
        action = dot(v["left_t"][at, :], ds_ref[0:128, 0:256])
        action += dot(v["right_t"][at, :], ds_ref[0:128, 256:512])
        grad[a, b, :, :, :, 32:48, :] = action.reshape(2, 2, 4, 16, 256)
        pair_op(k).start()
        return carry

    lax.fori_loop(0, 8, grad_prefix, 0, unroll=2)
    def grad_query():
        for offset in range(1, 8):
            member = place.group_member(offset, -1)
            links.arrived(v["group_gq"].at[member], (place.dp, member), exchange + 8 + offset)
        rows = v["group_gq"][...].reshape(1024, 256)
        for a in range(4):
            value = dot(act_t[a * 256 : (a + 1) * 256, :], rows)
            v["grad_query"][a] = value.reshape(2, 2, 64, 256)

    def finish(part):
        def store(value):
            if part == 2:
                out_action_ref[:, 0:256] = value[0:8]
                out_action_ref[:, 256:512] = value[8:16]
            else:
                out_prefix_ref[:, part * 256 : (part + 1) * 256] = value

        return store

    def paired():
        for k in range(8):
            pair_op(k).wait_recv()
        yield

    works = [reduce_query(links, place, grad_query, v, out_query_ref), paired()]
    works += [reduce_part(links, place, grad, pair, v, part, finish(part)) for part in range(3)]
    early = list(links.sent)
    links.sent.clear()

    def drain(ops):
        def run():
            for op in ops:
                op.wait_send()

        return run

    run_together(works, [drain(early[i::4]) for i in range(4)])
    for op in links.sent:
        op.wait_send()
    for k in range(8):
        pair_op(k).wait_send()


def step(cameras, text_length, flow_time, hidden, noise, clean, sine, cosine, input_weight, cot, own_prefix, own_action, own_query):
    bf16, f32 = jnp.bfloat16, jnp.float32
    smem, vmem = pl.BlockSpec(memory_space=pltpu.SMEM), pl.BlockSpec(memory_space=pltpu.VMEM)
    scratch = dict(
        norm=pltpu.VMEM((2 * KEYS, 2048), bf16),
        turn=pltpu.VMEM((32, 128), f32),
        own_noisy=pltpu.VMEM((128, 128), bf16),
        query_weight=pltpu.VMEM((4, 2, 2, 64, 256), bf16),
        noisy=pltpu.VMEM((8, 128, 128), bf16),
        time=pltpu.VMEM((8, 2, 1024), f32),
        own_time=pltpu.VMEM((2, 1024), f32),
        act=pltpu.VMEM((1024, 1024), bf16),
        act_t=pltpu.VMEM((1024, 1024), bf16),
        left=pltpu.VMEM((128, 2048), bf16),
        right=pltpu.VMEM((128, 2048), bf16),
        cot=pltpu.VMEM((8, 128, 256), bf16),
        eye=pltpu.VMEM((256, 256), bf16),
        left_t=pltpu.VMEM((2048, 128), bf16),
        right_t=pltpu.VMEM((2048, 128), bf16),
        query=pltpu.VMEM((8, 128, 256), bf16),
        query_out=pltpu.VMEM((8, 128, 256), bf16),
        gq=pltpu.VMEM((8, 128, 256), bf16),
        group_gq=pltpu.VMEM((8, 128, 256), bf16),
        wp=pltpu.VMEM((2048, 512), bf16),
        kv=pltpu.VMEM((2 * KEYS, 512), bf16),
        low=pltpu.VMEM((512, KEYS), bf16),
        ds=pltpu.VMEM((512, KEYS), bf16),
        query_t=pltpu.VMEM((8, 256, 128), bf16),
        cot_t=pltpu.VMEM((8, 256, 128), bf16),
        gkv=pltpu.VMEM((512, 2 * KEYS), bf16),
        grad=pltpu.VMEM((4, 2, 2, 2, 4, ROWS, 256), f32),
        pair=pltpu.VMEM((4, 4, 4, ROWS, 256), f32),
        grad_query=pltpu.VMEM((4, 2, 2, 64, 256), f32),
        query_pair=pltpu.VMEM((4, 2, 64, 256), f32),
        query_wire=pltpu.VMEM((4, 2, 64, 256), bf16),
        query_half=pltpu.VMEM((2, 64, 256), bf16),
        query_full=pltpu.VMEM((2, 2, 64, 256), bf16),
        query_sum=pltpu.VMEM((2, 64, 256), f32),
        query_far=pltpu.VMEM((64, 256), f32),
        send=pltpu.SemaphoreType.DMA((192,)),
        recv=pltpu.SemaphoreType.DMA((192,)),
        load=pltpu.SemaphoreType.DMA((6,)),
    )
    for part in range(3):
        scratch[f"weight_{part}"] = pltpu.VMEM((2, 4, 4, 4, 16, 256), bf16)
        scratch[f"wire1_{part}"] = pltpu.VMEM((4, 4, 4, 16, 256), bf16)
        scratch[f"half1_{part}"] = pltpu.VMEM((2, 2, 4, 16, 256), bf16)
        scratch[f"full1_{part}"] = pltpu.VMEM((2, 4, 4, 16, 256), bf16)
        scratch[f"sum2_{part}"] = pltpu.VMEM((4, 4, 16, 256), f32)
        scratch[f"wire2_{part}"] = pltpu.VMEM((4, 4, 16, 256), bf16)
        scratch[f"full2_{part}"] = pltpu.VMEM((3, 4, 16, 256), bf16)
        scratch[f"sum3_{part}"] = pltpu.VMEM((4, 16, 256), f32)
        scratch[f"full3_{part}"] = pltpu.VMEM((3, 16, 256), f32)
    return pl.pallas_call(
        step_kernel,
        out_shape=(
            jax.ShapeDtypeStruct((2, STEPS, 2048), bf16),
            jax.ShapeDtypeStruct((64, 256), f32),
            jax.ShapeDtypeStruct((16, 512), f32),
            jax.ShapeDtypeStruct((8, 512), f32),
        ),
        in_specs=[smem] * 3 + [pl.BlockSpec(memory_space=pl.ANY)] + [vmem] * 9,
        out_specs=(vmem,) * 4,
        scratch_shapes=[scratch],
        compiler_params=pltpu.CompilerParams(
            collective_id=1, has_side_effects=True, vmem_limit_bytes=VMEM_LIMIT
        ),
        cost_estimate=pl.CostEstimate(
            flops=10**10, bytes_accessed=9 * 10**6, transcendentals=10**6
        ),
        name="step",
    )(
        cameras, text_length, flow_time, hidden, noise, clean, sine, cosine, input_weight, cot,
        own_prefix, own_action, own_query,
    )


def time_feature(flow_col, row_width):
    half_width = row_width // 2
    fraction = jnp.arange(half_width, dtype=jnp.float32) / (half_width - 1)
    period = 0.004 * 1000.0**fraction
    angle = flow_col[..., None] * (2.0 * math.pi / period)
    return jnp.sin(angle), jnp.cos(angle)


def on_device(
    prefix_hidden,
    cameras,
    text_length,
    action_noise,
    clean_actions,
    flow_time,
    input_weight,
    prefix_kv_weight,
    action_kv_weight,
    query_weight,
    cotangent,
):
    sine, cosine = time_feature(flow_time, 1024)
    return step(
        cameras,
        text_length,
        flow_time,
        prefix_hidden,
        action_noise.transpose(0, 2, 1),
        clean_actions.transpose(0, 2, 1),
        sine,
        cosine,
        input_weight,
        cotangent.transpose(1, 0, 2),
        prefix_kv_weight,
        action_kv_weight,
        query_weight,
    )


def solution(mesh):
    return jax.shard_map(
        on_device,
        mesh=mesh,
        in_specs=(
            P(("dp", "seq"), None, None),
            P(("dp", "seq")),
            P(("dp", "seq")),
            P(("dp", "seq"), None, None),
            P(("dp", "seq"), None, None),
            P(("dp", "seq")),
            P(),
            P(("dp", "seq"), None),
            P(("dp", "seq"), None),
            P("dp", "seq"),
            P(("dp", "seq"), None, None),
        ),
        out_specs=(
            P(("dp", "seq"), None, None),
            P("dp", "seq"),
            P(("dp", "seq"), None),
            P(("dp", "seq"), None),
        ),
        check_vma=False,
    )
```

```python
import math

import jax
import jax.numpy as jnp
from jax import lax
from jax.experimental import pallas as pl
from jax.experimental.pallas import tpu as pltpu
from jax.sharding import PartitionSpec as P

IMG = 256
EPS = 1e-06
MESH = pl.DeviceIdType.MESH
VMEM_LIMIT = 50 * 1024 * 1024
PREFIX, STEPS, PAD_STEPS, KEYS = 816, 50, 64, 896

ROWS = 48
ORDERS = ("xyz", "yzx", "zxy")
HALVES = (slice(0, 2), slice(2, 4))
FULL = slice(None)


class Place:
    def __init__(self):
        self.dp = lax.axis_index("dp")
        self.seq = lax.axis_index("seq")
        self.core = lax.rem(self.dp, 2)
        self.z_hi = lax.rem(self.dp // 2, 2)
        self.z_lo = self.seq // 4
        self.at = {
            "y": self.dp // 4,
            "z": self.z_hi * 2 + self.z_lo,
            "x": lax.rem(self.seq, 4),
        }
        self.sibling = self.device(core=1 - self.core)
        self.z_far = self.device(z=self.shifted("z", 2))

    def device(self, core=None, **moved):
        at = {**self.at, **moved}
        core = self.core if core is None else core
        return (
            at["y"] * 4 + (at["z"] // 2) * 2 + core,
            lax.rem(at["z"], 2) * 4 + at["x"],
        )

    def shifted(self, axis, by):
        return lax.rem(self.at[axis] + by, 4)

    def group_member(self, offset, sign=1):
        z_lo = lax.rem(self.z_lo + lax.div(offset, 4), 2)
        x = lax.rem(self.at["x"] + sign * lax.rem(offset, 4) + 4, 4)
        return z_lo * 4 + x

    def greet(self):
        barrier = pltpu.get_barrier_semaphore()
        others = [self.sibling, self.z_far]
        others += [(self.dp, self.group_member(offset)) for offset in range(1, 8)]
        others += [self.device(y=self.shifted("y", by)) for by in (1, 2, 3)]
        beyond = lax.rem(self.at["z"] + 3 + 2 * self.z_lo, 4)
        others.append(self.device(z=beyond))
        for other in others:
            pl.semaphore_signal(barrier, inc=1, device_id=other, device_id_type=MESH)
        self.greeted = len(others)

    def meet(self):
        pl.semaphore_wait(pltpu.get_barrier_semaphore(), self.greeted)


class Links:
    def __init__(self, send_sem, recv_sem):
        self.send_sem, self.recv_sem = send_sem, recv_sem
        self.used = 0
        self.sent = []

    def slots(self, count):
        self.used += count
        return self.used - count

    def op(self, src, dst, to, slot):
        return pltpu.make_async_remote_copy(
            src_ref=src,
            dst_ref=dst,
            send_sem=self.send_sem.at[slot],
            recv_sem=self.recv_sem.at[slot],
            device_id=to,
            device_id_type=MESH,
        )

    def go(self, src, dst, to, slot):
        op = self.op(src, dst, to, slot)
        op.start()
        self.sent.append(op)

    def arrived(self, dst, to, slot):
        self.op(dst, dst, to, slot).wait_recv()


def run_together(works, tasks=()):
    live, tasks = list(works), list(tasks)
    while live or tasks:
        live = [work for work in live if next(work, "end") != "end"]
        if tasks:
            tasks.pop(0)()


def direct(links, place, axis, view, slot):
    own = place.at[axis]
    for by in (1, 3, 2):
        to = place.device(**{axis: place.shifted(axis, by)})
        links.go(view(own), view(own), to, slot + by - 1)
    yield
    for by in (1, 3, 2):
        links.arrived(view(place.shifted(axis, 4 - by)), place.sibling, slot + by - 1)


def ring(links, place, axis, view, slot, landed):
    own, right, left, across = (place.shifted(axis, by) for by in (0, 1, 3, 2))
    to_right, to_left = (place.device(**{axis: at}) for at in (right, left))
    links.go(view(own), view(own), to_right, slot)
    links.go(view(own), view(own), to_left, slot + 1)
    landed(own)
    yield
    links.arrived(view(left), to_right, slot)
    links.go(view(left, 0), view(left, 0), to_right, slot + 2)
    links.arrived(view(right), to_left, slot + 1)
    links.go(view(right, 1), view(right, 1), to_left, slot + 3)
    landed(left)
    landed(right)
    yield
    links.arrived(view(across, 0), to_right, slot + 2)
    links.arrived(view(across, 1), to_left, slot + 3)
    landed(across)


class Share:
    def __init__(self, links, place, view):
        self.links, self.place, self.view = links, place, view
        self.slot, self.due = links.slots(4), []

    def __call__(self, block):
        links, core = self.links, self.place.core
        slot = self.slot + len(self.due)
        mine = self.view(core, block)
        links.go(mine, mine, self.place.sibling, slot)
        self.due.append((self.view(1 - core, block), slot))

    def wait(self):
        for view, slot in self.due:
            self.links.arrived(view, self.place.sibling, slot)


def gather_part(links, place, ref, order):
    core = place.core
    first, second, third = order
    slot = links.slots(10)
    at = place.at
    yield from direct(
        links, place, first, lambda block: ref.at[core, at[third], at[second], block], slot
    )
    yield from direct(links, place, second, lambda block: ref.at[core, at[third], block], slot + 3)
    share = Share(links, place, lambda core, block: ref.at[core, block])

    def view(block, half=None):
        return ref.at[core, block] if half is None else ref.at[core, block, HALVES[half]]

    yield from ring(links, place, third, view, slot + 6, share)
    yield
    share.wait()


def gather_query(links, place, query_ref, then):
    core, y, z_hi = place.core, place.at["y"], place.z_hi
    slot = links.slots(5)
    links.go(query_ref.at[y, z_hi, core], query_ref.at[y, z_hi, core], place.z_far, slot)
    yield
    links.arrived(query_ref.at[y, 1 - z_hi, core], place.z_far, slot)
    share = Share(links, place, lambda core, block: query_ref.at[block, :, core])

    def view(block, half=None):
        return query_ref.at[block, FULL if half is None else half, core]

    yield from ring(links, place, "y", view, slot + 1, share)
    yield
    share.wait()
    then()


def reduce_ring(links, place, axis, pack, wire, half, fulls, slot):
    own, right, left, across = (place.shifted(axis, by) for by in (0, 1, 3, 2))
    to_right, to_left = (place.device(**{axis: at}) for at in (right, left))
    pack(across, 0)
    links.go(wire(across, 0), half.at[0], to_right, slot)
    pack(across, 1)
    links.go(wire(across, 1), half.at[1], to_left, slot + 1)
    yield
    pack(right, 1)
    links.go(wire(right, 1), fulls(0, 1), to_right, slot + 2)
    pack(left, 0)
    links.go(wire(left, 0), fulls(1, 0), to_left, slot + 3)
    yield
    links.arrived(half.at[0], to_right, slot)
    pack(right, 0, half.at[0])
    links.go(wire(right, 0), fulls(0, 0), to_right, slot + 4)
    links.arrived(half.at[1], to_left, slot + 1)
    pack(left, 1, half.at[1])
    links.go(wire(left, 1), fulls(1, 1), to_left, slot + 5)
    yield
    links.arrived(fulls(0, 1), to_right, slot + 2)
    links.arrived(fulls(1, 0), to_left, slot + 3)
    links.arrived(fulls(0, 0), to_right, slot + 4)
    links.arrived(fulls(1, 1), to_left, slot + 5)


def reduce_direct(links, place, axis, block_of, landing, slot):
    for by in (2, 1, 3):
        block = place.shifted(axis, by)
        links.go(
            block_of(block), landing.at[by - 1], place.device(**{axis: block}), slot + by - 1
        )
    yield
    for by in (1, 3, 2):
        links.arrived(landing.at[by - 1], place.sibling, slot + by - 1)


def reduce_part(links, place, grad_ref, pair_ref, v, part, finish):
    f32, bf16 = jnp.float32, jnp.bfloat16
    rows = slice(part * 16, part * 16 + 16)
    core = place.core
    first, second, third = ORDERS[part]
    wire, half, full = (v[f"{name}1_{part}"] for name in ("wire", "half", "full"))
    slot = links.slots(12)

    def mine(block, i, j):
        at = {first: block, second: i, third: j}
        y, z, x = at["y"], at["z"], at["x"]
        return grad_ref[y, z // 2, core, lax.rem(z, 2), x, rows, :] + pair_ref[y, z, x, rows, :]

    def pack(block, side, extra=None):
        for i in range(2):
            for j in range(4):
                value = mine(block, side * 2 + i, j)
                if extra is not None:
                    value = value + extra[i, j].astype(f32)
                wire[block, side * 2 + i, j] = value.astype(bf16)

    yield from reduce_ring(
        links, place, first, pack, lambda block, side: wire.at[block, HALVES[side]], half,
        lambda way, side: full.at[way, HALVES[side]], slot,
    )
    total, wire2, full2 = (v[f"{name}2_{part}"] for name in ("sum", "wire", "full"))
    for i in range(4):
        for j in range(4):
            value = mine(place.at[first], i, j)
            value = value + full[0, i, j].astype(f32) + full[1, i, j].astype(f32)
            total[i, j] = value
            wire2[i, j] = value.astype(bf16)
    yield from reduce_direct(links, place, second, lambda block: wire2.at[block], full2, slot + 6)
    total3, full3 = v[f"sum3_{part}"], v[f"full3_{part}"]
    value = total[place.at[second]]
    for k in range(3):
        value = value + full2[k].astype(f32)
    total3[...] = value
    yield from reduce_direct(links, place, third, lambda block: total3.at[block], full3, slot + 9)
    finish(total3[place.at[third]] + full3[0] + full3[1] + full3[2])


def reduce_query(links, place, first, v, out_ref):
    f32, bf16 = jnp.float32, jnp.bfloat16
    core, z_hi = place.core, place.z_hi
    grad_ref, pair_ref, wire = v["grad_query"], v["query_pair"], v["query_wire"]
    half, full, total, far_ref = v["query_half"], v["query_full"], v["query_sum"], v["query_far"]
    slot = links.slots(8)
    first()
    links.go(grad_ref.at[:, :, 1 - core], pair_ref, place.sibling, slot)
    yield
    links.arrived(pair_ref, place.sibling, slot)

    def pack(block, side, extra=None):
        value = grad_ref[block, side, core] + pair_ref[block, side]
        if extra is not None:
            value = value + extra[...].astype(f32)
        wire[block, side] = value.astype(bf16)

    yield from reduce_ring(
        links, place, "y", pack, lambda block, side: wire.at[block, side], half,
        lambda way, side: full.at[way, side], slot + 1,
    )
    own = place.at["y"]
    value = grad_ref[own, :, core] + pair_ref[own]
    total[...] = value + full[0].astype(f32) + full[1].astype(f32)
    v["query_far_out"][...] = total[1 - z_hi].astype(bf16)
    links.go(v["query_far_out"], far_ref, place.z_far, slot + 7)
    yield
    links.arrived(far_ref, place.z_far, slot + 7)
    out_ref[...] = total[z_hi] + far_ref[...].astype(f32)


def lanes_dot(left, right):
    return lax.dot_general(
        left, right, (((1,), (1,)), ((), ())), preferred_element_type=jnp.float32
    )


def rows_dot(left, right):
    return lax.dot_general(
        left, right, (((0,), (0,)), ((), ())), preferred_element_type=jnp.float32
    )


def dot(left, right):
    return jnp.dot(left, right, preferred_element_type=jnp.float32)


def step_kernel(
    cameras_hbm, text_hbm, flow_hbm, hidden_hbm, noise_hbm, clean_hbm, input_hbm, cot_hbm,
    own_prefix_hbm, own_action_hbm, own_query_hbm, sin_ref, cos_ref,
    attended_ref, out_query_ref, out_prefix_ref, out_action_ref,
    v,
):
    f32, bf16 = jnp.float32, jnp.bfloat16
    place = Place()
    core, y, z_hi, z_lo, x = place.core, place.at["y"], place.z_hi, place.z_lo, place.at["x"]
    seq = place.seq
    links = Links(v["send"], v["recv"])
    place.greet()

    norm = v["norm"]
    operands = dict(
        flow=flow_hbm, noise=noise_hbm, clean=clean_hbm, own_prefix=own_prefix_hbm,
        own_action=own_action_hbm, own_query=own_query_hbm, input=input_hbm, cot_in=cot_hbm,
        cameras=cameras_hbm, text=text_hbm,
    )
    fetches = {}
    for i, (name, ref) in enumerate(operands.items()):
        fetches[name] = pltpu.make_async_copy(ref, v[name], v["load"].at[6 + i])
        fetches[name].start()
    loads = []
    chunks = [(s, start, count) for s in range(2) for start, count in ((0, 288), (288, 288), (576, 240))]
    for k, (s, start, count) in enumerate(chunks):
        load = pltpu.make_async_copy(
            hidden_hbm.at[s, pl.ds(start, count), :],
            norm.at[pl.ds(s * KEYS + start, count), :],
            v["load"].at[k],
        )
        load.start()
        loads.append(load)

    query_weight = v["query_weight"]
    for name in ("flow", "noise", "clean", "own_prefix", "own_action", "own_query"):
        fetches[name].wait()
    own_prefix = v["own_prefix"]
    own_action = v["own_action"][...].astype(f32)
    own_action = jnp.concatenate([own_action[:, 0:256], own_action[:, 256:512]], axis=0)
    own_parts = (own_prefix[:, 0:256], own_prefix[:, 256:512], own_action.astype(bf16))
    for part, (first, second, third) in enumerate(ORDERS):
        at = place.at
        v[f"weight_{part}"][core, at[third], at[second], at[first]] = own_parts[part]
    query_weight[y, z_hi, core] = v["own_query"][...]
    own_noisy = v["own_noisy"]
    noisy = []
    for s in range(2):
        t = v["flow"][s]
        noisy.append(t * v["noise"][s].astype(f32) + (1.0 - t) * v["clean"][s].astype(f32))
    blank = jnp.zeros((32, PAD_STEPS - STEPS), f32)
    own_noisy[...] = jnp.concatenate([noisy[0], blank, noisy[1], blank], axis=1).astype(bf16)
    v["noisy"][seq] = own_noisy[...]
    own_time = v["own_time"]
    own_time[:, 0:512] = sin_ref[...]
    own_time[:, 512:1024] = cos_ref[...]
    v["time"][seq] = own_time[...]
    place.meet()

    eye = v["eye"]
    row = lax.broadcasted_iota(jnp.int32, (256, 256), 0)
    col = lax.broadcasted_iota(jnp.int32, (256, 256), 1)
    eye[...] = jnp.where(row == col, 1.0, 0.0).astype(bf16)

    packet = links.slots(16)
    def send_packets():
        for offset in range(1, 8):
            to = (place.dp, place.group_member(offset))
            links.go(own_noisy, v["noisy"].at[seq], to, packet + offset)
            links.go(own_time, v["time"].at[seq], to, packet + 8 + offset)
        fetches["input"].wait()

    act, act_t = v["act"], v["act_t"]

    def make_rows(member):
        at = pl.ds(pl.multiple_of(member * 128, 128), 128)
        wide = rows_dot(v["noisy"][member], v["input"][...])
        time = v["time"][member]
        parts = []
        for s in range(2):
            part = wide[s * PAD_STEPS : (s + 1) * PAD_STEPS] + time[s : s + 1]
            scale = lax.rsqrt(jnp.mean(part * part, axis=-1, keepdims=True) + EPS)
            parts.append((part * scale).astype(bf16))
        rows = jnp.concatenate(parts, axis=0)
        act[at, :] = rows
        for f in range(4):
            cols = slice(f * 256, (f + 1) * 256)
            act_t[cols, at] = lanes_dot(eye[...], rows[:, cols]).astype(bf16)

    def spread_rows():
        at = pl.ds(pl.multiple_of(seq * 128, 128), 128)
        feature = lax.broadcasted_iota(jnp.int32, (256, 128), 1)
        k = lax.broadcasted_iota(jnp.int32, (256, 128), 0)
        within = k % 16
        origin = (k // 16) * 8 + within
        first = jnp.where((within < 8) & (feature == origin), 1.0, 0.0).astype(bf16)
        second = jnp.where((within >= 8) & (feature == origin - 8), 1.0, 0.0).astype(bf16)
        for spread, name in ((first, "left"), (second, "right")):
            for i in range(8):
                cols, wide = slice(i * 128, (i + 1) * 128), slice(i * 256, (i + 1) * 256)
                v[name][:, wide] = lanes_dot(act[at, cols], spread).astype(bf16)
                v[name + "_t"][wide, :] = dot(spread, act_t[cols, at]).astype(bf16)

    def group_rows(low, high):
        def run():
            members = [place.group_member(offset, -1) for offset in range(low, high)]
            for offset, member in zip(range(low, high), members):
                if offset == 0:
                    continue
                to = (place.dp, member)
                links.arrived(v["noisy"].at[member], to, packet + offset)
                links.arrived(v["time"].at[member], to, packet + 8 + offset)
            for member in members:
                make_rows(member)

        return run

    def normalize(chunk):
        def run():
            loads[chunk].wait()
            s, start, count = chunks[chunk]

            def places(i):
                return [
                    pl.ds(pl.multiple_of(s * KEYS + start + i * 48 + j * 16, 16), 16)
                    for j in range(3)
                ]

            def scales(i):
                found = []
                for at in places(i):
                    wide = norm[at, :].astype(f32)
                    found.append(lax.rsqrt(jnp.mean(wide * wide, axis=-1, keepdims=True) + EPS))
                return tuple(found)

            def body(i, present):
                following = scales(jnp.minimum(i + 1, count // 48 - 1))
                for at, scale in zip(places(i), present):
                    norm[at, :] = (norm[at, :].astype(f32) * scale).astype(bf16)
                return following

            lax.fori_loop(0, count // 48, body, scales(0))

        return run

    def place_rows():
        fetches["cot_in"].wait()
        v["cot"][...] = jnp.zeros_like(v["cot"])
        for s in range(2):
            for h in range(8):
                v["cot"][h, s * PAD_STEPS : s * PAD_STEPS + STEPS, :] = v["cot_in"][
                    :, s, h * 256 : (h + 1) * 256
                ]
        for s in range(2):
            norm[s * KEYS + PREFIX : (s + 1) * KEYS, :] = jnp.zeros((KEYS - PREFIX, 2048), bf16)

    exchange = links.slots(16)

    def send_queries():
        wide = query_weight[...].reshape(1024, 256)
        for half in range(2):
            rows = slice(half * 512, (half + 1) * 512)
            value = dot(act[rows, :], wide).astype(bf16)
            v["query_out"][half * 4 : half * 4 + 4] = value.reshape(4, 128, 256)
        for offset in range(1, 8):
            member = place.group_member(offset)
            links.go(
                v["query_out"].at[member], v["query"].at[seq], (place.dp, member),
                exchange + offset,
            )
        v["query"][seq] = v["query_out"][seq]

    works = [gather_query(links, place, query_weight, send_queries)]
    works += [gather_part(links, place, v[f"weight_{part}"], ORDERS[part]) for part in range(3)]
    tasks = [lambda: (send_packets(), normalize(0)()), normalize(1), group_rows(0, 4), group_rows(4, 8)]
    tasks += [normalize(chunk) for chunk in range(2, 6)] + [spread_rows, place_rows]
    run_together(works, tasks)

    wp, kv = v["wp"], v["kv"]

    def block_rows(part, a, b):
        ref, order = v[f"weight_{part}"], ORDERS[part][::-1]
        pieces = []
        for c in range(2):
            for low in range(2):
                at = {"y": a, "z": b * 2 + low}
                if order[2] == "x":
                    pieces.append(ref[c, at[order[0]], at[order[1]]].reshape(64, 256))
                else:
                    for col in range(4):
                        at["x"] = col
                        pieces.append(ref[c, at[order[0]], at[order[1]], at[order[2]]])
        return pieces

    def unpack(k, carry):
        keys, values = carry
        a, b = k // 2, lax.rem(k, 2)
        for part in range(2):
            start = k * 256
            for piece in block_rows(part, a, b):
                at = pl.ds(pl.multiple_of(start, 16), piece.shape[0])
                wp[at, part * 256 : (part + 1) * 256] = piece
                start += piece.shape[0]
        block = jnp.concatenate(block_rows(2, a, b), axis=0)
        at = pl.ds(pl.multiple_of(k * 256, 256), 256)
        return keys + dot(v["left"][:, at], block), values + dot(v["right"][:, at], block)

    zero = jnp.zeros((2 * PAD_STEPS, 256), f32)
    keys, values = lax.fori_loop(0, 8, unpack, (zero, zero))
    keys, values = keys.astype(bf16), values.astype(bf16)

    def prefix(i, carry):
        at = pl.ds(pl.multiple_of(i * 448, 64), 448)
        kv[at, :] = dot(norm[at, :], wp[...]).astype(bf16)
        return carry

    lax.fori_loop(0, 4, prefix, 0)
    for s in range(2):
        rows = slice(s * PAD_STEPS, (s + 1) * PAD_STEPS)
        start = s * KEYS + PREFIX
        kv[start : start + PAD_STEPS, 0:256] = keys[rows]
        kv[start : start + PAD_STEPS, 256:512] = values[rows]

    for offset in range(1, 8):
        member = place.group_member(offset, -1)
        links.arrived(v["query"].at[member], (place.dp, member), exchange + offset)

    fetches["cameras"].wait()
    fetches["text"].wait()
    low_ref, ds_ref, gkv = v["low"], v["ds"], v["gkv"]

    def sixteenth(rows):
        return (rows.astype(f32) * 0.0625).astype(bf16)

    def sample(s, carry):
        length = v["cameras"][s] * IMG + v["text"][s]
        mine = pl.ds(pl.multiple_of(s * PAD_STEPS, PAD_STEPS), PAD_STEPS)
        start = pl.multiple_of(s * KEYS, 128)
        tokens = pl.ds(start, KEYS)
        column = lax.broadcasted_iota(jnp.int32, (1, KEYS), 1)
        valid = (column < length) | ((column >= PREFIX) & (column < PREFIX + STEPS))
        bias = jnp.where(valid, 0.0, -1e30)
        query = v["query"][:, mine, :].reshape(512, 256)
        cot = v["cot"][:, mine, :].reshape(512, 256)
        logits = lanes_dot(sixteenth(query), kv[tokens, 0:256]) + bias
        expo = jnp.exp(logits - jnp.max(logits, axis=-1, keepdims=True))
        probs = expo * (1.0 / jnp.sum(expo, axis=-1, keepdims=True))
        low_ref[...] = probs.astype(bf16)
        dprob = lanes_dot(sixteenth(cot), kv[tokens, 256:512])
        inner = jnp.sum(probs * dprob, axis=-1, keepdims=True)
        ds_ref[...] = (probs * (dprob - inner)).astype(bf16)
        v["gq"][:, mine, :] = dot(ds_ref[...], kv[tokens, 0:256]).astype(bf16).reshape(8, 64, 256)
        attended = dot(low_ref[...], kv[tokens, 256:512]).astype(bf16)
        for h in range(8):
            attended_ref[s, :, h * 256 : (h + 1) * 256] = attended[h * 64 : h * 64 + STEPS]

        first = lax.broadcasted_iota(jnp.int32, (256, 128), 1) < 64
        for rows, turned in ((query, v["query_t"]), (cot, v["cot_t"])):
            across = lanes_dot(eye[...], rows)
            for h in range(8):
                pair = across[:, (h // 2) * 128 : (h // 2 + 1) * 128]
                keep = first if h % 2 == 0 else jnp.logical_not(first)
                turned[h] = jnp.where(keep, pair, 0.0).astype(bf16)

        def tile(begin, width):
            at = pl.ds(begin, width)
            to = pl.ds(pl.multiple_of(start + begin, 128), width)
            for left, right, top in ((v["query_t"], ds_ref, 0), (v["cot_t"], low_ref, 256)):
                total = jnp.zeros((256, width), f32)
                for h in range(8):
                    term = dot(left[h], right[(h // 2) * 128 : (h // 2 + 1) * 128, at])
                    total = total + term.astype(bf16).astype(f32)
                gkv[top : top + 256, to] = total.astype(bf16)

        def wide_tile(t, carry):
            tile(pl.multiple_of(t * 256, 256), 256)
            return carry

        lax.fori_loop(0, 3, wide_tile, 0)
        tile(768, 128)
        return carry

    lax.fori_loop(0, 2, sample, 0)

    for offset in range(1, 8):
        member = place.group_member(offset)
        links.go(
            v["gq"].at[member], v["group_gq"].at[seq], (place.dp, member), exchange + 8 + offset
        )
    v["group_gq"][seq] = v["gq"][seq]

    for s in range(2):
        turned = gkv[:, s * KEYS + PREFIX - 48 : (s + 1) * KEYS].astype(f32).T[48 : 48 + PAD_STEPS]
        ds_ref[s * 64 : (s + 1) * 64, 0:512] = turned.astype(bf16)
    grad, pair = v["grad"], v["pair"]
    pairing = links.slots(8)

    def pair_op(k):
        a, b = k // 2, lax.rem(k, 2)
        return links.op(
            grad.at[a, b, 1 - core], pair.at[a, pl.ds(b * 2, 2)], place.sibling, pairing + k
        )

    def grad_prefix(k, carry):
        at = pl.ds(pl.multiple_of(k * 256, 256), 256)
        a, b = k // 2, lax.rem(k, 2)
        value = dot(gkv[...], norm[:, at])
        high = value.astype(bf16)
        low = (value - high.astype(f32)).astype(bf16)
        value = lanes_dot(eye[...], high) + lanes_dot(eye[...], low)
        grad[a, b, :, :, :, 0:16, :] = value[:, 0:256].reshape(2, 2, 4, 16, 256)
        grad[a, b, :, :, :, 16:32, :] = value[:, 256:512].reshape(2, 2, 4, 16, 256)
        action = dot(v["left_t"][at, :], ds_ref[0:128, 0:256])
        action += dot(v["right_t"][at, :], ds_ref[0:128, 256:512])
        grad[a, b, :, :, :, 32:48, :] = action.reshape(2, 2, 4, 16, 256)
        pair_op(k).start()
        return carry

    lax.fori_loop(0, 8, grad_prefix, 0, unroll=2)
    def grad_query():
        for offset in range(1, 8):
            member = place.group_member(offset, -1)
            links.arrived(v["group_gq"].at[member], (place.dp, member), exchange + 8 + offset)
        rows = v["group_gq"][...].reshape(1024, 256)
        for a in range(4):
            value = dot(act_t[a * 256 : (a + 1) * 256, :], rows)
            v["grad_query"][a] = value.reshape(2, 2, 64, 256)

    def finish(part):
        def store(value):
            if part == 2:
                out_action_ref[:, 0:256] = value[0:8]
                out_action_ref[:, 256:512] = value[8:16]
            else:
                out_prefix_ref[:, part * 256 : (part + 1) * 256] = value

        return store

    def paired():
        for k in range(8):
            pair_op(k).wait_recv()
        yield

    works = [reduce_query(links, place, grad_query, v, out_query_ref), paired()]
    works += [reduce_part(links, place, grad, pair, v, part, finish(part)) for part in range(3)]
    early = list(links.sent)
    links.sent.clear()

    def drain(ops):
        def run():
            for op in ops:
                op.wait_send()

        return run

    run_together(works, [drain(early[i::4]) for i in range(4)])
    for op in links.sent:
        op.wait_send()
    for k in range(8):
        pair_op(k).wait_send()


def step(
    cameras, text_length, flow_time, hidden, noise, clean, input_weight, cot,
    own_prefix, own_action, own_query, sine, cosine,
):
    bf16, f32 = jnp.bfloat16, jnp.float32
    hbm, vmem = pl.BlockSpec(memory_space=pltpu.HBM), pl.BlockSpec(memory_space=pltpu.VMEM)
    scratch = dict(
        norm=pltpu.VMEM((2 * KEYS, 2048), bf16),
        own_noisy=pltpu.VMEM((32, 128), bf16),
        query_weight=pltpu.VMEM((4, 2, 2, 64, 256), bf16),
        noisy=pltpu.VMEM((8, 32, 128), bf16),
        time=pltpu.VMEM((8, 2, 1024), f32),
        own_time=pltpu.VMEM((2, 1024), f32),
        act=pltpu.VMEM((1024, 1024), bf16),
        act_t=pltpu.VMEM((1024, 1024), bf16),
        left=pltpu.VMEM((128, 2048), bf16),
        right=pltpu.VMEM((128, 2048), bf16),
        cot=pltpu.VMEM((8, 128, 256), bf16),
        eye=pltpu.VMEM((256, 256), bf16),
        left_t=pltpu.VMEM((2048, 128), bf16),
        right_t=pltpu.VMEM((2048, 128), bf16),
        query=pltpu.VMEM((8, 128, 256), bf16),
        query_out=pltpu.VMEM((8, 128, 256), bf16),
        gq=pltpu.VMEM((8, 128, 256), bf16),
        group_gq=pltpu.VMEM((8, 128, 256), bf16),
        wp=pltpu.VMEM((2048, 512), bf16),
        kv=pltpu.VMEM((2 * KEYS, 512), bf16),
        low=pltpu.VMEM((512, KEYS), bf16),
        ds=pltpu.VMEM((512, KEYS), bf16),
        query_t=pltpu.VMEM((8, 256, 128), bf16),
        cot_t=pltpu.VMEM((8, 256, 128), bf16),
        gkv=pltpu.VMEM((512, 2 * KEYS), bf16),
        grad=pltpu.VMEM((4, 2, 2, 2, 4, ROWS, 256), f32),
        pair=pltpu.VMEM((4, 4, 4, ROWS, 256), f32),
        grad_query=pltpu.VMEM((4, 2, 2, 64, 256), f32),
        query_pair=pltpu.VMEM((4, 2, 64, 256), f32),
        query_wire=pltpu.VMEM((4, 2, 64, 256), bf16),
        query_half=pltpu.VMEM((2, 64, 256), bf16),
        query_full=pltpu.VMEM((2, 2, 64, 256), bf16),
        query_sum=pltpu.VMEM((2, 64, 256), f32),
        query_far=pltpu.VMEM((64, 256), bf16),
        query_far_out=pltpu.VMEM((64, 256), bf16),
        send=pltpu.SemaphoreType.DMA((192,)),
        recv=pltpu.SemaphoreType.DMA((192,)),
        load=pltpu.SemaphoreType.DMA((16,)),
        flow=pltpu.SMEM((2,), f32),
        cameras=pltpu.SMEM((2,), jnp.int32),
        text=pltpu.SMEM((2,), jnp.int32),
        noise=pltpu.VMEM((2, 32, STEPS), bf16),
        clean=pltpu.VMEM((2, 32, STEPS), bf16),
        input=pltpu.VMEM((32, 1024), bf16),
        cot_in=pltpu.VMEM((STEPS, 2, 2048), bf16),
        own_prefix=pltpu.VMEM((16, 512), bf16),
        own_action=pltpu.VMEM((8, 512), bf16),
        own_query=pltpu.VMEM((64, 256), bf16),
    )
    for part in range(3):
        scratch[f"weight_{part}"] = pltpu.VMEM((2, 4, 4, 4, 16, 256), bf16)
        scratch[f"wire1_{part}"] = pltpu.VMEM((4, 4, 4, 16, 256), bf16)
        scratch[f"half1_{part}"] = pltpu.VMEM((2, 2, 4, 16, 256), bf16)
        scratch[f"full1_{part}"] = pltpu.VMEM((2, 4, 4, 16, 256), bf16)
        scratch[f"sum2_{part}"] = pltpu.VMEM((4, 4, 16, 256), f32)
        scratch[f"wire2_{part}"] = pltpu.VMEM((4, 4, 16, 256), bf16)
        scratch[f"full2_{part}"] = pltpu.VMEM((3, 4, 16, 256), bf16)
        scratch[f"sum3_{part}"] = pltpu.VMEM((4, 16, 256), f32)
        scratch[f"full3_{part}"] = pltpu.VMEM((3, 16, 256), f32)
    return pl.pallas_call(
        step_kernel,
        out_shape=(
            jax.ShapeDtypeStruct((2, STEPS, 2048), bf16),
            jax.ShapeDtypeStruct((64, 256), f32),
            jax.ShapeDtypeStruct((16, 512), f32),
            jax.ShapeDtypeStruct((8, 512), f32),
        ),
        in_specs=[hbm] * 11 + [vmem] * 2,
        out_specs=(vmem,) * 4,
        scratch_shapes=[scratch],
        compiler_params=pltpu.CompilerParams(
            collective_id=1, has_side_effects=True, vmem_limit_bytes=VMEM_LIMIT
        ),
        cost_estimate=pl.CostEstimate(
            flops=10**10, bytes_accessed=9 * 10**6, transcendentals=10**6
        ),
        name="step",
    )(
        *[
            pltpu.with_memory_space_constraint(operand, pltpu.HBM)
            for operand in (
                cameras, text_length, flow_time, hidden, noise, clean, input_weight, cot,
                own_prefix, own_action, own_query,
            )
        ],
        sine,
        cosine,
    )


def time_feature(flow_col, row_width):
    half_width = row_width // 2
    fraction = jnp.arange(half_width, dtype=jnp.float32) / (half_width - 1)
    period = 0.004 * 1000.0**fraction
    angle = flow_col[..., None] * (2.0 * math.pi / period)
    return jnp.sin(angle), jnp.cos(angle)


def on_device(
    prefix_hidden,
    cameras,
    text_length,
    action_noise,
    clean_actions,
    flow_time,
    input_weight,
    prefix_kv_weight,
    action_kv_weight,
    query_weight,
    cotangent,
):
    sine, cosine = time_feature(flow_time, 1024)
    return step(
        cameras,
        text_length,
        flow_time,
        prefix_hidden,
        action_noise.transpose(0, 2, 1),
        clean_actions.transpose(0, 2, 1),
        input_weight,
        cotangent.transpose(1, 0, 2),
        prefix_kv_weight,
        action_kv_weight,
        query_weight,
        sine,
        cosine,
    )


def solution(mesh):
    return jax.shard_map(
        on_device,
        mesh=mesh,
        in_specs=(
            P(("dp", "seq"), None, None),
            P(("dp", "seq")),
            P(("dp", "seq")),
            P(("dp", "seq"), None, None),
            P(("dp", "seq"), None, None),
            P(("dp", "seq")),
            P(),
            P(("dp", "seq"), None),
            P(("dp", "seq"), None),
            P("dp", "seq"),
            P(("dp", "seq"), None, None),
        ),
        out_specs=(
            P(("dp", "seq"), None, None),
            P("dp", "seq"),
            P(("dp", "seq"), None),
            P(("dp", "seq"), None),
        ),
        check_vma=False,
    )
```

```python
import math

import jax
import jax.numpy as jnp
from jax import lax
from jax.experimental import pallas as pl
from jax.experimental.pallas import tpu as pltpu
from jax.sharding import PartitionSpec as P

IMG = 256
EPS = 1e-06
MESH = pl.DeviceIdType.MESH
VMEM_LIMIT = 50 * 1024 * 1024
PREFIX, STEPS, PAD_STEPS, KEYS = 816, 50, 64, 896

ROWS = 48
ORDERS = ("xyz", "yzx", "zxy")
HALVES = (slice(0, 2), slice(2, 4))
FULL = slice(None)


class Place:
    def __init__(self):
        self.dp = lax.axis_index("dp")
        self.seq = lax.axis_index("seq")
        self.core = lax.rem(self.dp, 2)
        self.z_hi = lax.rem(self.dp // 2, 2)
        self.z_lo = self.seq // 4
        self.at = {
            "y": self.dp // 4,
            "z": self.z_hi * 2 + self.z_lo,
            "x": lax.rem(self.seq, 4),
        }
        self.sibling = self.device(core=1 - self.core)
        self.z_far = self.device(z=self.shifted("z", 2))

    def device(self, core=None, **moved):
        at = {**self.at, **moved}
        core = self.core if core is None else core
        return (
            at["y"] * 4 + (at["z"] // 2) * 2 + core,
            lax.rem(at["z"], 2) * 4 + at["x"],
        )

    def shifted(self, axis, by):
        return lax.rem(self.at[axis] + by, 4)

    def group_member(self, offset, sign=1):
        z_lo = lax.rem(self.z_lo + lax.div(offset, 4), 2)
        x = lax.rem(self.at["x"] + sign * lax.rem(offset, 4) + 4, 4)
        return z_lo * 4 + x

    def greet(self):
        barrier = pltpu.get_barrier_semaphore()
        others = [self.sibling, self.z_far]
        others += [(self.dp, self.group_member(offset)) for offset in range(1, 8)]
        others += [self.device(y=self.shifted("y", by)) for by in (1, 2, 3)]
        beyond = lax.rem(self.at["z"] + 3 + 2 * self.z_lo, 4)
        others.append(self.device(z=beyond))
        for other in others:
            pl.semaphore_signal(barrier, inc=1, device_id=other, device_id_type=MESH)
        self.greeted = len(others)

    def meet(self):
        pl.semaphore_wait(pltpu.get_barrier_semaphore(), self.greeted)


class Links:
    def __init__(self, send_sem, recv_sem):
        self.send_sem, self.recv_sem = send_sem, recv_sem
        self.used = 0
        self.sent = []

    def slots(self, count):
        self.used += count
        return self.used - count

    def op(self, src, dst, to, slot):
        return pltpu.make_async_remote_copy(
            src_ref=src,
            dst_ref=dst,
            send_sem=self.send_sem.at[slot],
            recv_sem=self.recv_sem.at[slot],
            device_id=to,
            device_id_type=MESH,
        )

    def go(self, src, dst, to, slot):
        op = self.op(src, dst, to, slot)
        op.start()
        self.sent.append(op)

    def arrived(self, dst, to, slot):
        self.op(dst, dst, to, slot).wait_recv()


def run_together(works, tasks=()):
    live, tasks = list(works), list(tasks)
    while live or tasks:
        live = [work for work in live if next(work, "end") != "end"]
        if tasks:
            tasks.pop(0)()


def direct(links, place, axis, view, slot):
    own = place.at[axis]
    for by in (1, 3, 2):
        to = place.device(**{axis: place.shifted(axis, by)})
        links.go(view(own), view(own), to, slot + by - 1)
    yield
    for by in (1, 3, 2):
        links.arrived(view(place.shifted(axis, 4 - by)), place.sibling, slot + by - 1)


def ring(links, place, axis, view, slot, landed):
    own, right, left, across = (place.shifted(axis, by) for by in (0, 1, 3, 2))
    to_right, to_left = (place.device(**{axis: at}) for at in (right, left))
    links.go(view(own), view(own), to_right, slot)
    links.go(view(own), view(own), to_left, slot + 1)
    landed(own)
    yield
    links.arrived(view(left), to_right, slot)
    links.go(view(left, 0), view(left, 0), to_right, slot + 2)
    links.arrived(view(right), to_left, slot + 1)
    links.go(view(right, 1), view(right, 1), to_left, slot + 3)
    landed(left)
    landed(right)
    yield
    links.arrived(view(across, 0), to_right, slot + 2)
    links.arrived(view(across, 1), to_left, slot + 3)
    landed(across)


class Share:
    def __init__(self, links, place, view):
        self.links, self.place, self.view = links, place, view
        self.slot, self.due = links.slots(4), []

    def __call__(self, block):
        links, core = self.links, self.place.core
        slot = self.slot + len(self.due)
        mine = self.view(core, block)
        links.go(mine, mine, self.place.sibling, slot)
        self.due.append((self.view(1 - core, block), slot))

    def wait(self):
        for view, slot in self.due:
            self.links.arrived(view, self.place.sibling, slot)


def gather_part(links, place, ref, order):
    core = place.core
    first, second, third = order
    slot = links.slots(10)
    at = place.at
    yield from direct(
        links, place, first, lambda block: ref.at[core, at[third], at[second], block], slot
    )
    yield from direct(links, place, second, lambda block: ref.at[core, at[third], block], slot + 3)
    share = Share(links, place, lambda core, block: ref.at[core, block])

    def view(block, half=None):
        return ref.at[core, block] if half is None else ref.at[core, block, HALVES[half]]

    yield from ring(links, place, third, view, slot + 6, share)
    yield
    share.wait()


def gather_query(links, place, query_ref, then):
    core, y, z_hi = place.core, place.at["y"], place.z_hi
    slot = links.slots(5)
    links.go(query_ref.at[y, z_hi, core], query_ref.at[y, z_hi, core], place.z_far, slot)
    yield
    links.arrived(query_ref.at[y, 1 - z_hi, core], place.z_far, slot)
    share = Share(links, place, lambda core, block: query_ref.at[block, :, core])

    def view(block, half=None):
        return query_ref.at[block, FULL if half is None else half, core]

    yield from ring(links, place, "y", view, slot + 1, share)
    yield
    share.wait()
    then()


def reduce_ring(links, place, axis, pack, wire, half, fulls, slot):
    own, right, left, across = (place.shifted(axis, by) for by in (0, 1, 3, 2))
    to_right, to_left = (place.device(**{axis: at}) for at in (right, left))
    pack(across, 0)
    links.go(wire(across, 0), half.at[0], to_right, slot)
    pack(across, 1)
    links.go(wire(across, 1), half.at[1], to_left, slot + 1)
    yield
    pack(right, 1)
    links.go(wire(right, 1), fulls(0, 1), to_right, slot + 2)
    pack(left, 0)
    links.go(wire(left, 0), fulls(1, 0), to_left, slot + 3)
    yield
    links.arrived(half.at[0], to_right, slot)
    pack(right, 0, half.at[0])
    links.go(wire(right, 0), fulls(0, 0), to_right, slot + 4)
    links.arrived(half.at[1], to_left, slot + 1)
    pack(left, 1, half.at[1])
    links.go(wire(left, 1), fulls(1, 1), to_left, slot + 5)
    yield
    links.arrived(fulls(0, 1), to_right, slot + 2)
    links.arrived(fulls(1, 0), to_left, slot + 3)
    links.arrived(fulls(0, 0), to_right, slot + 4)
    links.arrived(fulls(1, 1), to_left, slot + 5)


def reduce_direct(links, place, axis, block_of, landing, slot):
    for by in (2, 1, 3):
        block = place.shifted(axis, by)
        links.go(
            block_of(block), landing.at[by - 1], place.device(**{axis: block}), slot + by - 1
        )
    yield
    for by in (1, 3, 2):
        links.arrived(landing.at[by - 1], place.sibling, slot + by - 1)


def reduce_part(links, place, grad_ref, pair_ref, v, part, finish):
    f32, bf16 = jnp.float32, jnp.bfloat16
    rows = slice(part * 16, part * 16 + 16)
    core = place.core
    first, second, third = ORDERS[part]
    wire, half, full = (v[f"{name}1_{part}"] for name in ("wire", "half", "full"))
    slot = links.slots(12)

    def mine(block, i, j):
        at = {first: block, second: i, third: j}
        y, z, x = at["y"], at["z"], at["x"]
        return grad_ref[y, z // 2, core, lax.rem(z, 2), x, rows, :] + pair_ref[y, z, x, rows, :]

    def pack(block, side, extra=None):
        for i in range(2):
            for j in range(4):
                value = mine(block, side * 2 + i, j)
                if extra is not None:
                    value = value + extra[i, j].astype(f32)
                wire[block, side * 2 + i, j] = value.astype(bf16)

    yield from reduce_ring(
        links, place, first, pack, lambda block, side: wire.at[block, HALVES[side]], half,
        lambda way, side: full.at[way, HALVES[side]], slot,
    )
    total, wire2, full2 = (v[f"{name}2_{part}"] for name in ("sum", "wire", "full"))
    for i in range(4):
        for j in range(4):
            value = mine(place.at[first], i, j)
            value = value + full[0, i, j].astype(f32) + full[1, i, j].astype(f32)
            total[i, j] = value
            wire2[i, j] = value.astype(bf16)
    yield from reduce_direct(links, place, second, lambda block: wire2.at[block], full2, slot + 6)
    total3, full3 = v[f"sum3_{part}"], v[f"full3_{part}"]
    value = total[place.at[second]]
    for k in range(3):
        value = value + full2[k].astype(f32)
    total3[...] = value
    yield from reduce_direct(links, place, third, lambda block: total3.at[block], full3, slot + 9)
    finish(total3[place.at[third]] + full3[0] + full3[1] + full3[2])


def reduce_query(links, place, first, v, out_ref):
    f32, bf16 = jnp.float32, jnp.bfloat16
    core, z_hi = place.core, place.z_hi
    grad_ref, pair_ref, wire = v["grad_query"], v["query_pair"], v["query_wire"]
    half, full, total, far_ref = v["query_half"], v["query_full"], v["query_sum"], v["query_far"]
    slot = links.slots(8)
    first()
    links.go(grad_ref.at[:, :, 1 - core], pair_ref, place.sibling, slot)
    yield
    links.arrived(pair_ref, place.sibling, slot)

    def pack(block, side, extra=None):
        value = grad_ref[block, side, core] + pair_ref[block, side]
        if extra is not None:
            value = value + extra[...].astype(f32)
        wire[block, side] = value.astype(bf16)

    yield from reduce_ring(
        links, place, "y", pack, lambda block, side: wire.at[block, side], half,
        lambda way, side: full.at[way, side], slot + 1,
    )
    own = place.at["y"]
    value = grad_ref[own, :, core] + pair_ref[own]
    total[...] = value + full[0].astype(f32) + full[1].astype(f32)
    v["query_far_out"][...] = total[1 - z_hi].astype(bf16)
    links.go(v["query_far_out"], far_ref, place.z_far, slot + 7)
    yield
    links.arrived(far_ref, place.z_far, slot + 7)
    out_ref[...] = total[z_hi] + far_ref[...].astype(f32)


def lanes_dot(left, right):
    return lax.dot_general(
        left, right, (((1,), (1,)), ((), ())), preferred_element_type=jnp.float32
    )


def rows_dot(left, right):
    return lax.dot_general(
        left, right, (((0,), (0,)), ((), ())), preferred_element_type=jnp.float32
    )


def dot(left, right):
    return jnp.dot(left, right, preferred_element_type=jnp.float32)


def step_kernel(
    cameras_hbm, text_hbm, flow_hbm, hidden_hbm, noise_hbm, clean_hbm, input_hbm, cot_hbm,
    own_prefix_hbm, own_action_hbm, own_query_hbm, sin_ref, cos_ref,
    attended_ref, out_query_ref, out_prefix_ref, out_action_ref,
    v,
):
    f32, bf16 = jnp.float32, jnp.bfloat16
    place = Place()
    core, y, z_hi, z_lo, x = place.core, place.at["y"], place.z_hi, place.z_lo, place.at["x"]
    seq = place.seq
    links = Links(v["send"], v["recv"])
    place.greet()

    norm = v["norm"]
    operands = dict(
        flow=flow_hbm, noise=noise_hbm, clean=clean_hbm, own_prefix=own_prefix_hbm,
        own_action=own_action_hbm, own_query=own_query_hbm, input=input_hbm, cot_in=cot_hbm,
        cameras=cameras_hbm, text=text_hbm,
    )
    fetches = {}
    for i, (name, ref) in enumerate(operands.items()):
        fetches[name] = pltpu.make_async_copy(ref, v[name], v["load"].at[6 + i])
        fetches[name].start()
    loads = []
    chunks = [(s, start, count) for s in range(2) for start, count in ((0, 288), (288, 288), (576, 240))]
    for k, (s, start, count) in enumerate(chunks):
        load = pltpu.make_async_copy(
            hidden_hbm.at[s, pl.ds(start, count), :],
            norm.at[pl.ds(s * KEYS + start, count), :],
            v["load"].at[k],
        )
        load.start()
        loads.append(load)

    query_weight = v["query_weight"]
    for name in ("flow", "noise", "clean", "own_prefix", "own_action", "own_query"):
        fetches[name].wait()
    own_prefix = v["own_prefix"]
    own_action = v["own_action"][...].astype(f32)
    own_action = jnp.concatenate([own_action[:, 0:256], own_action[:, 256:512]], axis=0)
    own_parts = (own_prefix[:, 0:256], own_prefix[:, 256:512], own_action.astype(bf16))
    for part, (first, second, third) in enumerate(ORDERS):
        at = place.at
        v[f"weight_{part}"][core, at[third], at[second], at[first]] = own_parts[part]
    query_weight[y, z_hi, core] = v["own_query"][...]
    own_noisy = v["own_noisy"]
    noisy = []
    for s in range(2):
        t = v["flow"][s]
        noisy.append(t * v["noise"][s].astype(f32) + (1.0 - t) * v["clean"][s].astype(f32))
    blank = jnp.zeros((32, PAD_STEPS - STEPS), f32)
    own_noisy[...] = jnp.concatenate([noisy[0], blank, noisy[1], blank], axis=1).astype(bf16)
    v["noisy"][seq] = own_noisy[...]
    own_time = v["own_time"]
    own_time[:, 0:512] = sin_ref[...]
    own_time[:, 512:1024] = cos_ref[...]
    v["time"][seq] = own_time[...]
    place.meet()

    eye = v["eye"]
    row = lax.broadcasted_iota(jnp.int32, (256, 256), 0)
    col = lax.broadcasted_iota(jnp.int32, (256, 256), 1)
    eye[...] = jnp.where(row == col, 1.0, 0.0).astype(bf16)

    packet = links.slots(16)
    def send_packets():
        for offset in range(1, 8):
            to = (place.dp, place.group_member(offset))
            links.go(own_noisy, v["noisy"].at[seq], to, packet + offset)
            links.go(own_time, v["time"].at[seq], to, packet + 8 + offset)
        fetches["input"].wait()

    act, act_t = v["act"], v["act_t"]

    def make_rows(member):
        at = pl.ds(pl.multiple_of(member * 128, 128), 128)
        wide = rows_dot(v["noisy"][member], v["input"][...])
        time = v["time"][member]
        parts = []
        for s in range(2):
            part = wide[s * PAD_STEPS : (s + 1) * PAD_STEPS] + time[s : s + 1]
            scale = lax.rsqrt(jnp.mean(part * part, axis=-1, keepdims=True) + EPS)
            parts.append((part * scale).astype(bf16))
        rows = jnp.concatenate(parts, axis=0)
        act[at, :] = rows
        for f in range(4):
            cols = slice(f * 256, (f + 1) * 256)
            act_t[cols, at] = lanes_dot(eye[...], rows[:, cols]).astype(bf16)

    def spread_rows():
        at = pl.ds(pl.multiple_of(seq * 128, 128), 128)
        feature = lax.broadcasted_iota(jnp.int32, (256, 128), 1)
        k = lax.broadcasted_iota(jnp.int32, (256, 128), 0)
        within = k % 16
        origin = (k // 16) * 8 + within
        first = jnp.where((within < 8) & (feature == origin), 1.0, 0.0).astype(bf16)
        second = jnp.where((within >= 8) & (feature == origin - 8), 1.0, 0.0).astype(bf16)
        for spread, name in ((first, "left"), (second, "right")):
            for i in range(8):
                cols, wide = slice(i * 128, (i + 1) * 128), slice(i * 256, (i + 1) * 256)
                v[name][:, wide] = lanes_dot(act[at, cols], spread).astype(bf16)
                v[name + "_t"][wide, :] = dot(spread, act_t[cols, at]).astype(bf16)

    def group_rows(low, high):
        def run():
            members = [place.group_member(offset, -1) for offset in range(low, high)]
            for offset, member in zip(range(low, high), members):
                if offset == 0:
                    continue
                to = (place.dp, member)
                links.arrived(v["noisy"].at[member], to, packet + offset)
                links.arrived(v["time"].at[member], to, packet + 8 + offset)
            for member in members:
                make_rows(member)

        return run

    def normalize(chunk):
        def run():
            loads[chunk].wait()
            s, start, count = chunks[chunk]

            def places(i):
                return [
                    pl.ds(pl.multiple_of(s * KEYS + start + i * 48 + j * 16, 16), 16)
                    for j in range(3)
                ]

            def scales(i):
                found = []
                for at in places(i):
                    wide = norm[at, :].astype(f32)
                    found.append(lax.rsqrt(jnp.mean(wide * wide, axis=-1, keepdims=True) + EPS))
                return tuple(found)

            def body(i, present):
                following = scales(jnp.minimum(i + 1, count // 48 - 1))
                for at, scale in zip(places(i), present):
                    norm[at, :] = (norm[at, :].astype(f32) * scale).astype(bf16)
                return following

            lax.fori_loop(0, count // 48, body, scales(0))

        return run

    def place_rows():
        fetches["cot_in"].wait()
        v["cot"][...] = jnp.zeros_like(v["cot"])
        for s in range(2):
            for h in range(8):
                v["cot"][h, s * PAD_STEPS : s * PAD_STEPS + STEPS, :] = v["cot_in"][
                    :, s, h * 256 : (h + 1) * 256
                ]
        for s in range(2):
            norm[s * KEYS + PREFIX : (s + 1) * KEYS, :] = jnp.zeros((KEYS - PREFIX, 2048), bf16)

    exchange = links.slots(16)

    def send_queries():
        wide = query_weight[...].reshape(1024, 256)
        for half in range(2):
            rows = slice(half * 512, (half + 1) * 512)
            value = dot(act[rows, :], wide).astype(bf16)
            v["query_out"][half * 4 : half * 4 + 4] = value.reshape(4, 128, 256)
        for offset in range(1, 8):
            member = place.group_member(offset)
            links.go(
                v["query_out"].at[member], v["query"].at[seq], (place.dp, member),
                exchange + offset,
            )
        v["query"][seq] = v["query_out"][seq]

    works = [gather_query(links, place, query_weight, send_queries)]
    works += [gather_part(links, place, v[f"weight_{part}"], ORDERS[part]) for part in range(3)]
    tasks = [lambda: (send_packets(), normalize(0)()), normalize(1), group_rows(0, 4), group_rows(4, 8)]
    tasks += [normalize(chunk) for chunk in range(2, 6)] + [spread_rows, place_rows]
    run_together(works, tasks)

    wp, kv = v["wp"], v["kv"]

    def block_rows(part, a, b):
        ref, order = v[f"weight_{part}"], ORDERS[part][::-1]
        pieces = []
        for c in range(2):
            for low in range(2):
                at = {"y": a, "z": b * 2 + low}
                if order[2] == "x":
                    pieces.append(ref[c, at[order[0]], at[order[1]]].reshape(64, 256))
                else:
                    for col in range(4):
                        at["x"] = col
                        pieces.append(ref[c, at[order[0]], at[order[1]], at[order[2]]])
        return pieces

    def unpack(k, carry):
        keys, values = carry
        a, b = k // 2, lax.rem(k, 2)
        for part in range(2):
            start = k * 256
            for piece in block_rows(part, a, b):
                at = pl.ds(pl.multiple_of(start, 16), piece.shape[0])
                wp[at, part * 256 : (part + 1) * 256] = piece
                start += piece.shape[0]
        block = jnp.concatenate(block_rows(2, a, b), axis=0)
        at = pl.ds(pl.multiple_of(k * 256, 256), 256)
        return keys + dot(v["left"][:, at], block), values + dot(v["right"][:, at], block)

    zero = jnp.zeros((2 * PAD_STEPS, 256), f32)
    keys, values = lax.fori_loop(0, 8, unpack, (zero, zero))
    keys, values = keys.astype(bf16), values.astype(bf16)

    def prefix(i, carry):
        at = pl.ds(pl.multiple_of(i * 448, 64), 448)
        kv[at, :] = dot(norm[at, :], wp[...]).astype(bf16)
        return carry

    lax.fori_loop(0, 4, prefix, 0)
    for s in range(2):
        rows = slice(s * PAD_STEPS, (s + 1) * PAD_STEPS)
        start = s * KEYS + PREFIX
        kv[start : start + PAD_STEPS, 0:256] = keys[rows]
        kv[start : start + PAD_STEPS, 256:512] = values[rows]

    low_ref, ds_ref, gkv = v["low"], v["ds"], v["gkv"]

    def sixteenth(rows):
        return (rows.astype(f32) * 0.0625).astype(bf16)

    def turn_pairs(rows, turned):
        first = lax.broadcasted_iota(jnp.int32, (256, 128), 1) < 64
        across = lanes_dot(eye[...], rows)
        for h in range(8):
            pair = across[:, (h // 2) * 128 : (h // 2 + 1) * 128]
            keep = first if h % 2 == 0 else jnp.logical_not(first)
            turned[h] = jnp.where(keep, pair, 0.0).astype(bf16)

    for s in range(2):
        cot = v["cot"][:, s * PAD_STEPS : (s + 1) * PAD_STEPS, :].reshape(512, 256)
        turn_pairs(cot, v["cot_t"].at[s])
    fetches["cameras"].wait()
    fetches["text"].wait()
    for offset in range(1, 8):
        member = place.group_member(offset, -1)
        links.arrived(v["query"].at[member], (place.dp, member), exchange + offset)

    returns = links.slots(16)

    def return_op(s, offset):
        member = place.group_member(offset)
        mine = pl.ds(pl.multiple_of(s * PAD_STEPS, PAD_STEPS), PAD_STEPS)
        return links.op(
            v["gq"].at[member, mine], v["group_gq"].at[seq, mine], (place.dp, member),
            returns + s * 8 + offset,
        )

    def sample(s, carry):
        length = v["cameras"][s] * IMG + v["text"][s]
        mine = pl.ds(pl.multiple_of(s * PAD_STEPS, PAD_STEPS), PAD_STEPS)
        start = pl.multiple_of(s * KEYS, 128)
        tokens = pl.ds(start, KEYS)
        column = lax.broadcasted_iota(jnp.int32, (1, KEYS), 1)
        valid = (column < length) | ((column >= PREFIX) & (column < PREFIX + STEPS))
        bias = jnp.where(valid, 0.0, -1e30)
        query = v["query"][:, mine, :].reshape(512, 256)
        cot = v["cot"][:, mine, :].reshape(512, 256)
        logits = lanes_dot(sixteenth(query), kv[tokens, 0:256]) + bias
        expo = jnp.exp(logits - jnp.max(logits, axis=-1, keepdims=True))
        probs = expo * (1.0 / jnp.sum(expo, axis=-1, keepdims=True))
        low_ref[...] = probs.astype(bf16)
        dprob = lanes_dot(sixteenth(cot), kv[tokens, 256:512])
        inner = jnp.sum(probs * dprob, axis=-1, keepdims=True)
        ds_ref[...] = (probs * (dprob - inner)).astype(bf16)
        v["gq"][:, mine, :] = dot(ds_ref[...], kv[tokens, 0:256]).astype(bf16).reshape(8, 64, 256)
        for offset in range(1, 8):
            return_op(s, offset).start()
        attended = dot(low_ref[...], kv[tokens, 256:512]).astype(bf16)
        for h in range(8):
            attended_ref[s, :, h * 256 : (h + 1) * 256] = attended[h * 64 : h * 64 + STEPS]
        turn_pairs(query, v["query_t"])

        def tile(begin, width):
            at = pl.ds(begin, width)
            to = pl.ds(pl.multiple_of(start + begin, 128), width)
            for left, right, top in ((v["query_t"], ds_ref, 0), (v["cot_t"].at[s], low_ref, 256)):
                total = jnp.zeros((256, width), f32)
                for h in range(8):
                    term = dot(left[h], right[(h // 2) * 128 : (h // 2 + 1) * 128, at])
                    total = total + term.astype(bf16).astype(f32)
                gkv[top : top + 256, to] = total.astype(bf16)

        def wide_tile(t, carry):
            tile(pl.multiple_of(t * 256, 256), 256)
            return carry

        lax.fori_loop(0, 3, wide_tile, 0)
        tile(768, 128)
        return carry

    lax.fori_loop(0, 2, sample, 0)

    v["group_gq"][seq] = v["gq"][seq]

    for s in range(2):
        turned = gkv[:, s * KEYS + PREFIX - 48 : (s + 1) * KEYS].astype(f32).T[48 : 48 + PAD_STEPS]
        ds_ref[s * 64 : (s + 1) * 64, 0:512] = turned.astype(bf16)
    grad, pair = v["grad"], v["pair"]
    pairing = links.slots(8)

    def pair_op(k):
        a, b = k // 2, lax.rem(k, 2)
        return links.op(
            grad.at[a, b, 1 - core], pair.at[a, pl.ds(b * 2, 2)], place.sibling, pairing + k
        )

    def grad_prefix(k, carry):
        at = pl.ds(pl.multiple_of(k * 256, 256), 256)
        a, b = k // 2, lax.rem(k, 2)
        value = dot(gkv[...], norm[:, at])
        high = value.astype(bf16)
        low = (value - high.astype(f32)).astype(bf16)
        value = lanes_dot(eye[...], high) + lanes_dot(eye[...], low)
        grad[a, b, :, :, :, 0:16, :] = value[:, 0:256].reshape(2, 2, 4, 16, 256)
        grad[a, b, :, :, :, 16:32, :] = value[:, 256:512].reshape(2, 2, 4, 16, 256)
        action = dot(v["left_t"][at, :], ds_ref[0:128, 0:256])
        action += dot(v["right_t"][at, :], ds_ref[0:128, 256:512])
        grad[a, b, :, :, :, 32:48, :] = action.reshape(2, 2, 4, 16, 256)
        pair_op(k).start()
        return carry

    def grad_query():
        for offset in range(1, 8):
            member = place.group_member(offset, -1)
            for s in range(2):
                mine = slice(s * PAD_STEPS, (s + 1) * PAD_STEPS)
                links.arrived(
                    v["group_gq"].at[member, mine], (place.dp, member), returns + s * 8 + offset
                )
        rows = v["group_gq"][...].reshape(1024, 256)
        for a in range(4):
            value = dot(act_t[a * 256 : (a + 1) * 256, :], rows)
            v["grad_query"][a] = value.reshape(2, 2, 64, 256)

    def finish(part):
        def store(value):
            if part == 2:
                out_action_ref[:, 0:256] = value[0:8]
                out_action_ref[:, 256:512] = value[8:16]
            else:
                out_prefix_ref[:, part * 256 : (part + 1) * 256] = value

        return store

    def paired():
        for k in range(8):
            pair_op(k).wait_recv()
        yield

    query_work = reduce_query(links, place, grad_query, v, out_query_ref)
    lax.fori_loop(0, 4, grad_prefix, 0, unroll=2)
    next(query_work)
    lax.fori_loop(4, 6, grad_prefix, 0)
    next(query_work)
    lax.fori_loop(6, 8, grad_prefix, 0)
    works = [query_work, paired()]
    works += [reduce_part(links, place, grad, pair, v, part, finish(part)) for part in range(3)]
    early = list(links.sent)
    links.sent.clear()

    def drain(ops):
        def run():
            for op in ops:
                op.wait_send()

        return run

    run_together(works, [drain(early[i::4]) for i in range(4)])
    for op in links.sent:
        op.wait_send()
    for offset in range(1, 8):
        for s in range(2):
            return_op(s, offset).wait_send()
    for k in range(8):
        pair_op(k).wait_send()


def step(
    cameras, text_length, flow_time, hidden, noise, clean, input_weight, cot,
    own_prefix, own_action, own_query, sine, cosine,
):
    bf16, f32 = jnp.bfloat16, jnp.float32
    hbm, vmem = pl.BlockSpec(memory_space=pltpu.HBM), pl.BlockSpec(memory_space=pltpu.VMEM)
    scratch = dict(
        norm=pltpu.VMEM((2 * KEYS, 2048), bf16),
        own_noisy=pltpu.VMEM((32, 128), bf16),
        query_weight=pltpu.VMEM((4, 2, 2, 64, 256), bf16),
        noisy=pltpu.VMEM((8, 32, 128), bf16),
        time=pltpu.VMEM((8, 2, 1024), f32),
        own_time=pltpu.VMEM((2, 1024), f32),
        act=pltpu.VMEM((1024, 1024), bf16),
        act_t=pltpu.VMEM((1024, 1024), bf16),
        left=pltpu.VMEM((128, 2048), bf16),
        right=pltpu.VMEM((128, 2048), bf16),
        cot=pltpu.VMEM((8, 128, 256), bf16),
        eye=pltpu.VMEM((256, 256), bf16),
        left_t=pltpu.VMEM((2048, 128), bf16),
        right_t=pltpu.VMEM((2048, 128), bf16),
        query=pltpu.VMEM((8, 128, 256), bf16),
        query_out=pltpu.VMEM((8, 128, 256), bf16),
        gq=pltpu.VMEM((8, 128, 256), bf16),
        group_gq=pltpu.VMEM((8, 128, 256), bf16),
        wp=pltpu.VMEM((2048, 512), bf16),
        kv=pltpu.VMEM((2 * KEYS, 512), bf16),
        low=pltpu.VMEM((512, KEYS), bf16),
        ds=pltpu.VMEM((512, KEYS), bf16),
        query_t=pltpu.VMEM((8, 256, 128), bf16),
        cot_t=pltpu.VMEM((2, 8, 256, 128), bf16),
        gkv=pltpu.VMEM((512, 2 * KEYS), bf16),
        grad=pltpu.VMEM((4, 2, 2, 2, 4, ROWS, 256), f32),
        pair=pltpu.VMEM((4, 4, 4, ROWS, 256), f32),
        grad_query=pltpu.VMEM((4, 2, 2, 64, 256), f32),
        query_pair=pltpu.VMEM((4, 2, 64, 256), f32),
        query_wire=pltpu.VMEM((4, 2, 64, 256), bf16),
        query_half=pltpu.VMEM((2, 64, 256), bf16),
        query_full=pltpu.VMEM((2, 2, 64, 256), bf16),
        query_sum=pltpu.VMEM((2, 64, 256), f32),
        query_far=pltpu.VMEM((64, 256), bf16),
        query_far_out=pltpu.VMEM((64, 256), bf16),
        send=pltpu.SemaphoreType.DMA((192,)),
        recv=pltpu.SemaphoreType.DMA((192,)),
        load=pltpu.SemaphoreType.DMA((16,)),
        flow=pltpu.SMEM((2,), f32),
        cameras=pltpu.SMEM((2,), jnp.int32),
        text=pltpu.SMEM((2,), jnp.int32),
        noise=pltpu.VMEM((2, 32, STEPS), bf16),
        clean=pltpu.VMEM((2, 32, STEPS), bf16),
        input=pltpu.VMEM((32, 1024), bf16),
        cot_in=pltpu.VMEM((STEPS, 2, 2048), bf16),
        own_prefix=pltpu.VMEM((16, 512), bf16),
        own_action=pltpu.VMEM((8, 512), bf16),
        own_query=pltpu.VMEM((64, 256), bf16),
    )
    for part in range(3):
        scratch[f"weight_{part}"] = pltpu.VMEM((2, 4, 4, 4, 16, 256), bf16)
        scratch[f"wire1_{part}"] = pltpu.VMEM((4, 4, 4, 16, 256), bf16)
        scratch[f"half1_{part}"] = pltpu.VMEM((2, 2, 4, 16, 256), bf16)
        scratch[f"full1_{part}"] = pltpu.VMEM((2, 4, 4, 16, 256), bf16)
        scratch[f"sum2_{part}"] = pltpu.VMEM((4, 4, 16, 256), f32)
        scratch[f"wire2_{part}"] = pltpu.VMEM((4, 4, 16, 256), bf16)
        scratch[f"full2_{part}"] = pltpu.VMEM((3, 4, 16, 256), bf16)
        scratch[f"sum3_{part}"] = pltpu.VMEM((4, 16, 256), f32)
        scratch[f"full3_{part}"] = pltpu.VMEM((3, 16, 256), f32)
    return pl.pallas_call(
        step_kernel,
        out_shape=(
            jax.ShapeDtypeStruct((2, STEPS, 2048), bf16),
            jax.ShapeDtypeStruct((64, 256), f32),
            jax.ShapeDtypeStruct((16, 512), f32),
            jax.ShapeDtypeStruct((8, 512), f32),
        ),
        in_specs=[hbm] * 11 + [vmem] * 2,
        out_specs=(vmem,) * 4,
        scratch_shapes=[scratch],
        compiler_params=pltpu.CompilerParams(
            collective_id=1, has_side_effects=True, vmem_limit_bytes=VMEM_LIMIT
        ),
        cost_estimate=pl.CostEstimate(
            flops=10**10, bytes_accessed=9 * 10**6, transcendentals=10**6
        ),
        name="step",
    )(
        *[
            pltpu.with_memory_space_constraint(operand, pltpu.HBM)
            for operand in (
                cameras, text_length, flow_time, hidden, noise, clean, input_weight, cot,
                own_prefix, own_action, own_query,
            )
        ],
        sine,
        cosine,
    )


def time_feature(flow_col, row_width):
    half_width = row_width // 2
    fraction = jnp.arange(half_width, dtype=jnp.float32) / (half_width - 1)
    period = 0.004 * 1000.0**fraction
    angle = flow_col[..., None] * (2.0 * math.pi / period)
    return jnp.sin(angle), jnp.cos(angle)


def on_device(
    prefix_hidden,
    cameras,
    text_length,
    action_noise,
    clean_actions,
    flow_time,
    input_weight,
    prefix_kv_weight,
    action_kv_weight,
    query_weight,
    cotangent,
):
    sine, cosine = time_feature(flow_time, 1024)
    return step(
        cameras,
        text_length,
        flow_time,
        prefix_hidden,
        action_noise.transpose(0, 2, 1),
        clean_actions.transpose(0, 2, 1),
        input_weight,
        cotangent.transpose(1, 0, 2),
        prefix_kv_weight,
        action_kv_weight,
        query_weight,
        sine,
        cosine,
    )


def solution(mesh):
    return jax.shard_map(
        on_device,
        mesh=mesh,
        in_specs=(
            P(("dp", "seq"), None, None),
            P(("dp", "seq")),
            P(("dp", "seq")),
            P(("dp", "seq"), None, None),
            P(("dp", "seq"), None, None),
            P(("dp", "seq")),
            P(),
            P(("dp", "seq"), None),
            P(("dp", "seq"), None),
            P("dp", "seq"),
            P(("dp", "seq"), None, None),
        ),
        out_specs=(
            P(("dp", "seq"), None, None),
            P("dp", "seq"),
            P(("dp", "seq"), None),
            P(("dp", "seq"), None),
        ),
        check_vma=False,
    )
```

```python
import math

import jax
import jax.numpy as jnp
from jax import lax
from jax.experimental import pallas as pl
from jax.experimental.pallas import tpu as pltpu
from jax.sharding import PartitionSpec as P

IMG = 256
EPS = 1e-06
MESH = pl.DeviceIdType.MESH
VMEM_LIMIT = 50 * 1024 * 1024
PREFIX, STEPS, PAD_STEPS, KEYS = 816, 50, 64, 896

ROWS = 48
ORDERS = ("xyz", "yzx", "zxy")
HALVES = (slice(0, 2), slice(2, 4))
FULL = slice(None)


class Place:
    def __init__(self):
        self.dp = lax.axis_index("dp")
        self.seq = lax.axis_index("seq")
        self.core = lax.rem(self.dp, 2)
        self.z_hi = lax.rem(self.dp // 2, 2)
        self.z_lo = self.seq // 4
        self.at = {
            "y": self.dp // 4,
            "z": self.z_hi * 2 + self.z_lo,
            "x": lax.rem(self.seq, 4),
        }
        self.sibling = self.device(core=1 - self.core)
        self.z_far = self.device(z=self.shifted("z", 2))

    def device(self, core=None, **moved):
        at = {**self.at, **moved}
        core = self.core if core is None else core
        return (
            at["y"] * 4 + (at["z"] // 2) * 2 + core,
            lax.rem(at["z"], 2) * 4 + at["x"],
        )

    def shifted(self, axis, by):
        return lax.rem(self.at[axis] + by, 4)

    def group_member(self, offset, sign=1):
        z_lo = lax.rem(self.z_lo + lax.div(offset, 4), 2)
        x = lax.rem(self.at["x"] + sign * lax.rem(offset, 4) + 4, 4)
        return z_lo * 4 + x

    def greet(self):
        barrier = pltpu.get_barrier_semaphore()
        others = [self.sibling, self.z_far]
        others += [(self.dp, self.group_member(offset)) for offset in range(1, 8)]
        others += [self.device(y=self.shifted("y", by)) for by in (1, 2, 3)]
        beyond = lax.rem(self.at["z"] + 3 + 2 * self.z_lo, 4)
        others.append(self.device(z=beyond))
        for other in others:
            pl.semaphore_signal(barrier, inc=1, device_id=other, device_id_type=MESH)
        self.greeted = len(others)

    def meet(self):
        pl.semaphore_wait(pltpu.get_barrier_semaphore(), self.greeted)


class Links:
    def __init__(self, send_sem, recv_sem):
        self.send_sem, self.recv_sem = send_sem, recv_sem
        self.used = 0
        self.sent = []

    def slots(self, count):
        self.used += count
        return self.used - count

    def op(self, src, dst, to, slot):
        return pltpu.make_async_remote_copy(
            src_ref=src,
            dst_ref=dst,
            send_sem=self.send_sem.at[slot],
            recv_sem=self.recv_sem.at[slot],
            device_id=to,
            device_id_type=MESH,
        )

    def go(self, src, dst, to, slot):
        op = self.op(src, dst, to, slot)
        op.start()
        self.sent.append(op)

    def arrived(self, dst, to, slot):
        self.op(dst, dst, to, slot).wait_recv()


def run_together(works, tasks=()):
    live, tasks = list(works), list(tasks)
    while live or tasks:
        live = [work for work in live if next(work, "end") != "end"]
        if tasks:
            tasks.pop(0)()


def direct(links, place, axis, view, slot):
    own = place.at[axis]
    for by in (1, 3, 2):
        to = place.device(**{axis: place.shifted(axis, by)})
        links.go(view(own), view(own), to, slot + by - 1)
    yield
    for by in (1, 3, 2):
        links.arrived(view(place.shifted(axis, 4 - by)), place.sibling, slot + by - 1)


def ring(links, place, axis, view, slot, landed):
    own, right, left, across = (place.shifted(axis, by) for by in (0, 1, 3, 2))
    to_right, to_left = (place.device(**{axis: at}) for at in (right, left))
    links.go(view(own), view(own), to_right, slot)
    links.go(view(own), view(own), to_left, slot + 1)
    landed(own)
    yield
    links.arrived(view(left), to_right, slot)
    links.go(view(left, 0), view(left, 0), to_right, slot + 2)
    links.arrived(view(right), to_left, slot + 1)
    links.go(view(right, 1), view(right, 1), to_left, slot + 3)
    landed(left)
    landed(right)
    yield
    links.arrived(view(across, 0), to_right, slot + 2)
    links.arrived(view(across, 1), to_left, slot + 3)
    landed(across)


class Share:
    def __init__(self, links, place, view):
        self.links, self.place, self.view = links, place, view
        self.slot, self.due = links.slots(4), []

    def __call__(self, block):
        links, core = self.links, self.place.core
        slot = self.slot + len(self.due)
        mine = self.view(core, block)
        links.go(mine, mine, self.place.sibling, slot)
        self.due.append((self.view(1 - core, block), slot))

    def wait(self):
        for view, slot in self.due:
            self.links.arrived(view, self.place.sibling, slot)


def gather_part(links, place, ref, order):
    core = place.core
    first, second, third = order
    slot = links.slots(10)
    at = place.at
    yield from direct(
        links, place, first, lambda block: ref.at[core, at[third], at[second], block], slot
    )
    yield from direct(links, place, second, lambda block: ref.at[core, at[third], block], slot + 3)
    share = Share(links, place, lambda core, block: ref.at[core, block])

    def view(block, half=None):
        return ref.at[core, block] if half is None else ref.at[core, block, HALVES[half]]

    yield from ring(links, place, third, view, slot + 6, share)
    yield
    share.wait()


def gather_query(links, place, query_ref, then):
    core, y, z_hi = place.core, place.at["y"], place.z_hi
    slot = links.slots(5)
    links.go(query_ref.at[y, z_hi, core], query_ref.at[y, z_hi, core], place.z_far, slot)
    yield
    links.arrived(query_ref.at[y, 1 - z_hi, core], place.z_far, slot)
    share = Share(links, place, lambda core, block: query_ref.at[block, :, core])

    def view(block, half=None):
        return query_ref.at[block, FULL if half is None else half, core]

    yield from ring(links, place, "y", view, slot + 1, share)
    yield
    share.wait()
    then()


def reduce_ring(links, place, axis, pack, wire, half, fulls, slot):
    own, right, left, across = (place.shifted(axis, by) for by in (0, 1, 3, 2))
    to_right, to_left = (place.device(**{axis: at}) for at in (right, left))
    pack(across, 0)
    links.go(wire(across, 0), half.at[0], to_right, slot)
    pack(across, 1)
    links.go(wire(across, 1), half.at[1], to_left, slot + 1)
    yield
    pack(right, 1)
    links.go(wire(right, 1), fulls(0, 1), to_right, slot + 2)
    pack(left, 0)
    links.go(wire(left, 0), fulls(1, 0), to_left, slot + 3)
    yield
    links.arrived(half.at[0], to_right, slot)
    pack(right, 0, half.at[0])
    links.go(wire(right, 0), fulls(0, 0), to_right, slot + 4)
    links.arrived(half.at[1], to_left, slot + 1)
    pack(left, 1, half.at[1])
    links.go(wire(left, 1), fulls(1, 1), to_left, slot + 5)
    yield
    links.arrived(fulls(0, 1), to_right, slot + 2)
    links.arrived(fulls(1, 0), to_left, slot + 3)
    links.arrived(fulls(0, 0), to_right, slot + 4)
    links.arrived(fulls(1, 1), to_left, slot + 5)


def reduce_direct(links, place, axis, block_of, landing, slot):
    for by in (2, 1, 3):
        block = place.shifted(axis, by)
        links.go(
            block_of(block), landing.at[by - 1], place.device(**{axis: block}), slot + by - 1
        )
    yield
    for by in (1, 3, 2):
        links.arrived(landing.at[by - 1], place.sibling, slot + by - 1)


def reduce_part(links, place, grad_ref, pair_ref, v, part, finish):
    f32, bf16 = jnp.float32, jnp.bfloat16
    rows = slice(part * 16, part * 16 + 16)
    core = place.core
    first, second, third = ORDERS[part]
    wire, half, full = (v[f"{name}1_{part}"] for name in ("wire", "half", "full"))
    slot = links.slots(12)

    def mine(block, i, j):
        at = {first: block, second: i, third: j}
        y, z, x = at["y"], at["z"], at["x"]
        return grad_ref[y, z // 2, core, lax.rem(z, 2), x, rows, :] + pair_ref[y, z, x, rows, :]

    def pack(block, side, extra=None):
        for i in range(2):
            for j in range(4):
                value = mine(block, side * 2 + i, j)
                if extra is not None:
                    value = value + extra[i, j].astype(f32)
                wire[block, side * 2 + i, j] = value.astype(bf16)

    yield from reduce_ring(
        links, place, first, pack, lambda block, side: wire.at[block, HALVES[side]], half,
        lambda way, side: full.at[way, HALVES[side]], slot,
    )
    total, wire2, full2 = (v[f"{name}2_{part}"] for name in ("sum", "wire", "full"))
    for i in range(4):
        for j in range(4):
            value = mine(place.at[first], i, j)
            value = value + full[0, i, j].astype(f32) + full[1, i, j].astype(f32)
            total[i, j] = value
            wire2[i, j] = value.astype(bf16)
    yield from reduce_direct(links, place, second, lambda block: wire2.at[block], full2, slot + 6)
    total3, full3 = v[f"sum3_{part}"], v[f"full3_{part}"]
    value = total[place.at[second]]
    for k in range(3):
        value = value + full2[k].astype(f32)
    total3[...] = value
    yield from reduce_direct(links, place, third, lambda block: total3.at[block], full3, slot + 9)
    finish(total3[place.at[third]] + full3[0] + full3[1] + full3[2])


def reduce_query(links, place, first, v, out_ref):
    f32, bf16 = jnp.float32, jnp.bfloat16
    core, z_hi = place.core, place.z_hi
    grad_ref, pair_ref, wire = v["grad_query"], v["query_pair"], v["query_wire"]
    half, full, total, far_ref = v["query_half"], v["query_full"], v["query_sum"], v["query_far"]
    slot = links.slots(8)
    first()
    links.go(grad_ref.at[:, :, 1 - core], pair_ref, place.sibling, slot)
    yield
    links.arrived(pair_ref, place.sibling, slot)

    def pack(block, side, extra=None):
        value = grad_ref[block, side, core] + pair_ref[block, side]
        if extra is not None:
            value = value + extra[...].astype(f32)
        wire[block, side] = value.astype(bf16)

    yield from reduce_ring(
        links, place, "y", pack, lambda block, side: wire.at[block, side], half,
        lambda way, side: full.at[way, side], slot + 1,
    )
    own = place.at["y"]
    value = grad_ref[own, :, core] + pair_ref[own]
    total[...] = value + full[0].astype(f32) + full[1].astype(f32)
    v["query_far_out"][...] = total[1 - z_hi].astype(bf16)
    links.go(v["query_far_out"], far_ref, place.z_far, slot + 7)
    yield
    links.arrived(far_ref, place.z_far, slot + 7)
    out_ref[...] = total[z_hi] + far_ref[...].astype(f32)


def lanes_dot(left, right):
    return lax.dot_general(
        left, right, (((1,), (1,)), ((), ())), preferred_element_type=jnp.float32
    )


def rows_dot(left, right):
    return lax.dot_general(
        left, right, (((0,), (0,)), ((), ())), preferred_element_type=jnp.float32
    )


def dot(left, right):
    return jnp.dot(left, right, preferred_element_type=jnp.float32)


def step_kernel(
    cameras_hbm, text_hbm, flow_hbm, hidden_hbm, noise_hbm, clean_hbm, input_hbm, cot_hbm,
    own_prefix_hbm, own_action_hbm, own_query_hbm, sin_ref, cos_ref,
    attended_ref, out_query_ref, out_prefix_ref, out_action_ref,
    v,
):
    f32, bf16 = jnp.float32, jnp.bfloat16
    place = Place()
    core, y, z_hi, z_lo, x = place.core, place.at["y"], place.z_hi, place.z_lo, place.at["x"]
    seq = place.seq
    links = Links(v["send"], v["recv"])
    place.greet()

    norm = v["norm"]
    operands = dict(
        flow=flow_hbm, noise=noise_hbm, clean=clean_hbm, own_prefix=own_prefix_hbm,
        own_action=own_action_hbm, own_query=own_query_hbm, input=input_hbm, cot_in=cot_hbm,
        cameras=cameras_hbm, text=text_hbm,
    )
    fetches = {}
    for i, (name, ref) in enumerate(operands.items()):
        fetches[name] = pltpu.make_async_copy(ref, v[name], v["load"].at[6 + i])
        fetches[name].start()
    loads = []
    chunks = [(s, start, count) for s in range(2) for start, count in ((0, 288), (288, 288), (576, 240))]
    for k, (s, start, count) in enumerate(chunks):
        load = pltpu.make_async_copy(
            hidden_hbm.at[s, pl.ds(start, count), :],
            norm.at[pl.ds(s * KEYS + start, count), :],
            v["load"].at[k],
        )
        load.start()
        loads.append(load)

    query_weight, eye = v["query_weight"], v["eye"]
    for name in ("own_prefix", "own_action", "own_query"):
        fetches[name].wait()
    own_prefix = v["own_prefix"]
    own_action = v["own_action"][...].astype(f32)
    own_action = jnp.concatenate([own_action[:, 0:256], own_action[:, 256:512]], axis=0)
    own_parts = (own_prefix[:, 0:256], own_prefix[:, 256:512], own_action.astype(bf16))
    for part, (first, second, third) in enumerate(ORDERS):
        at = place.at
        v[f"weight_{part}"][core, at[third], at[second], at[first]] = own_parts[part]
    query_weight[y, z_hi, core] = v["own_query"][...]
    place.meet()

    packet = links.slots(16)
    def send_packets():
        for name in ("flow", "noise", "clean"):
            fetches[name].wait()
        own_noisy = v["own_noisy"]
        noisy = []
        for s in range(2):
            t = v["flow"][s]
            noisy.append(t * v["noise"][s].astype(f32) + (1.0 - t) * v["clean"][s].astype(f32))
        blank = jnp.zeros((32, PAD_STEPS - STEPS), f32)
        own_noisy[...] = jnp.concatenate([noisy[0], blank, noisy[1], blank], axis=1).astype(bf16)
        v["noisy"][seq] = own_noisy[...]
        own_time = v["own_time"]
        own_time[:, 0:512] = sin_ref[...]
        own_time[:, 512:1024] = cos_ref[...]
        v["time"][seq] = own_time[...]
        for offset in range(1, 8):
            to = (place.dp, place.group_member(offset))
            links.go(own_noisy, v["noisy"].at[seq], to, packet + offset)
            links.go(own_time, v["time"].at[seq], to, packet + 8 + offset)
        fetches["input"].wait()
        row = lax.broadcasted_iota(jnp.int32, (256, 256), 0)
        col = lax.broadcasted_iota(jnp.int32, (256, 256), 1)
        eye[...] = jnp.where(row == col, 1.0, 0.0).astype(bf16)

    act, act_t = v["act"], v["act_t"]

    def make_rows(member):
        at = pl.ds(pl.multiple_of(member * 128, 128), 128)
        wide = rows_dot(v["noisy"][member], v["input"][...])
        time = v["time"][member]
        parts = []
        for s in range(2):
            part = wide[s * PAD_STEPS : (s + 1) * PAD_STEPS] + time[s : s + 1]
            scale = lax.rsqrt(jnp.mean(part * part, axis=-1, keepdims=True) + EPS)
            parts.append((part * scale).astype(bf16))
        rows = jnp.concatenate(parts, axis=0)
        act[at, :] = rows
        for f in range(4):
            cols = slice(f * 256, (f + 1) * 256)
            act_t[cols, at] = lanes_dot(eye[...], rows[:, cols]).astype(bf16)

    def spread_rows():
        at = pl.ds(pl.multiple_of(seq * 128, 128), 128)
        feature = lax.broadcasted_iota(jnp.int32, (256, 128), 1)
        k = lax.broadcasted_iota(jnp.int32, (256, 128), 0)
        within = k % 16
        origin = (k // 16) * 8 + within
        first = jnp.where((within < 8) & (feature == origin), 1.0, 0.0).astype(bf16)
        second = jnp.where((within >= 8) & (feature == origin - 8), 1.0, 0.0).astype(bf16)
        for spread, name in ((first, "left"), (second, "right")):
            for i in range(8):
                cols, wide = slice(i * 128, (i + 1) * 128), slice(i * 256, (i + 1) * 256)
                v[name][:, wide] = lanes_dot(act[at, cols], spread).astype(bf16)
                v[name + "_t"][wide, :] = dot(spread, act_t[cols, at]).astype(bf16)

    def group_rows(low, high):
        def run():
            members = [place.group_member(offset, -1) for offset in range(low, high)]
            for offset, member in zip(range(low, high), members):
                if offset == 0:
                    continue
                to = (place.dp, member)
                links.arrived(v["noisy"].at[member], to, packet + offset)
                links.arrived(v["time"].at[member], to, packet + 8 + offset)
            for member in members:
                make_rows(member)

        return run

    def normalize(chunk):
        def run():
            loads[chunk].wait()
            s, start, count = chunks[chunk]

            def places(i):
                return [
                    pl.ds(pl.multiple_of(s * KEYS + start + i * 48 + j * 16, 16), 16)
                    for j in range(3)
                ]

            def scales(i):
                found = []
                for at in places(i):
                    wide = norm[at, :].astype(f32)
                    found.append(lax.rsqrt(jnp.mean(wide * wide, axis=-1, keepdims=True) + EPS))
                return tuple(found)

            def body(i, present):
                following = scales(jnp.minimum(i + 1, count // 48 - 1))
                for at, scale in zip(places(i), present):
                    norm[at, :] = (norm[at, :].astype(f32) * scale).astype(bf16)
                return following

            lax.fori_loop(0, count // 48, body, scales(0))

        return run

    def place_rows():
        fetches["cot_in"].wait()
        v["cot"][...] = jnp.zeros_like(v["cot"])
        for s in range(2):
            for h in range(8):
                v["cot"][h, s * PAD_STEPS : s * PAD_STEPS + STEPS, :] = v["cot_in"][
                    :, s, h * 256 : (h + 1) * 256
                ]
        for s in range(2):
            norm[s * KEYS + PREFIX : (s + 1) * KEYS, :] = jnp.zeros((KEYS - PREFIX, 2048), bf16)

    exchange = links.slots(16)

    def send_queries():
        wide = query_weight[...].reshape(1024, 256)
        for half in range(2):
            rows = slice(half * 512, (half + 1) * 512)
            value = dot(act[rows, :], wide).astype(bf16)
            v["query_out"][half * 4 : half * 4 + 4] = value.reshape(4, 128, 256)
        for s in range(2):
            mine = slice(s * PAD_STEPS, (s + 1) * PAD_STEPS)
            for offset in (2, 6, 1, 3, 5, 7, 4):
                member = place.group_member(offset)
                links.go(
                    v["query_out"].at[member, mine], v["query"].at[seq, mine],
                    (place.dp, member), exchange + s * 8 + offset,
                )
        v["query"][seq] = v["query_out"][seq]

    works = [gather_query(links, place, query_weight, send_queries)]
    works += [gather_part(links, place, v[f"weight_{part}"], ORDERS[part]) for part in range(3)]
    tasks = [lambda: (send_packets(), normalize(0)()), normalize(1), group_rows(0, 4), group_rows(4, 8)]
    tasks += [normalize(chunk) for chunk in range(2, 6)] + [spread_rows, place_rows]
    run_together(works, tasks)

    wp, kv = v["wp"], v["kv"]

    def block_rows(part, a, b):
        ref, order = v[f"weight_{part}"], ORDERS[part][::-1]
        pieces = []
        for c in range(2):
            for low in range(2):
                at = {"y": a, "z": b * 2 + low}
                if order[2] == "x":
                    pieces.append(ref[c, at[order[0]], at[order[1]]].reshape(64, 256))
                else:
                    for col in range(4):
                        at["x"] = col
                        pieces.append(ref[c, at[order[0]], at[order[1]], at[order[2]]])
        return pieces

    def unpack(k, carry):
        keys, values = carry
        a, b = k // 2, lax.rem(k, 2)
        for part in range(2):
            start = k * 256
            for piece in block_rows(part, a, b):
                at = pl.ds(pl.multiple_of(start, 16), piece.shape[0])
                wp[at, part * 256 : (part + 1) * 256] = piece
                start += piece.shape[0]
        block = jnp.concatenate(block_rows(2, a, b), axis=0)
        at = pl.ds(pl.multiple_of(k * 256, 256), 256)
        return keys + dot(v["left"][:, at], block), values + dot(v["right"][:, at], block)

    zero = jnp.zeros((2 * PAD_STEPS, 256), f32)
    keys, values = lax.fori_loop(0, 8, unpack, (zero, zero))
    keys, values = keys.astype(bf16), values.astype(bf16)

    def prefix(i, carry):
        at = pl.ds(pl.multiple_of(i * 448, 64), 448)
        kv[at, :] = dot(norm[at, :], wp[...]).astype(bf16)
        return carry

    lax.fori_loop(0, 4, prefix, 0)
    for s in range(2):
        rows = slice(s * PAD_STEPS, (s + 1) * PAD_STEPS)
        start = s * KEYS + PREFIX
        kv[start : start + PAD_STEPS, 0:256] = keys[rows]
        kv[start : start + PAD_STEPS, 256:512] = values[rows]

    low_ref, ds_ref, gkv = v["low"], v["ds"], v["gkv"]

    def sixteenth(rows):
        return (rows.astype(f32) * 0.0625).astype(bf16)

    def turn_pairs(rows, turned):
        first = lax.broadcasted_iota(jnp.int32, (256, 128), 1) < 64
        across = lanes_dot(eye[...], rows)
        for h in range(8):
            pair = across[:, (h // 2) * 128 : (h // 2 + 1) * 128]
            keep = first if h % 2 == 0 else jnp.logical_not(first)
            turned[h] = jnp.where(keep, pair, 0.0).astype(bf16)

    for s in range(2):
        cot = v["cot"][:, s * PAD_STEPS : (s + 1) * PAD_STEPS, :].reshape(512, 256)
        turn_pairs(cot, v["cot_t"].at[s])
    fetches["cameras"].wait()
    fetches["text"].wait()
    returns = links.slots(16)

    def return_op(s, offset):
        member = place.group_member(offset)
        mine = pl.ds(pl.multiple_of(s * PAD_STEPS, PAD_STEPS), PAD_STEPS)
        return links.op(
            v["gq"].at[member, mine], v["group_gq"].at[seq, mine], (place.dp, member),
            returns + s * 8 + offset,
        )

    def sample(s, carry):
        length = v["cameras"][s] * IMG + v["text"][s]
        mine = pl.ds(pl.multiple_of(s * PAD_STEPS, PAD_STEPS), PAD_STEPS)
        start = pl.multiple_of(s * KEYS, 128)
        tokens = pl.ds(start, KEYS)
        column = lax.broadcasted_iota(jnp.int32, (1, KEYS), 1)
        valid = (column < length) | ((column >= PREFIX) & (column < PREFIX + STEPS))
        bias = jnp.where(valid, 0.0, -1e30)
        for offset in range(1, 8):
            member = place.group_member(offset, -1)
            links.arrived(
                v["query"].at[member, mine], (place.dp, member), exchange + s * 8 + offset
            )
        query = v["query"][:, mine, :].reshape(512, 256)
        cot = v["cot"][:, mine, :].reshape(512, 256)
        logits = lanes_dot(sixteenth(query), kv[tokens, 0:256]) + bias
        expo = jnp.exp(logits - jnp.max(logits, axis=-1, keepdims=True))
        probs = expo * (1.0 / jnp.sum(expo, axis=-1, keepdims=True))
        low_ref[...] = probs.astype(bf16)
        dprob = lanes_dot(sixteenth(cot), kv[tokens, 256:512])
        inner = jnp.sum(probs * dprob, axis=-1, keepdims=True)
        ds_ref[...] = (probs * (dprob - inner)).astype(bf16)
        v["gq"][:, mine, :] = dot(ds_ref[...], kv[tokens, 0:256]).astype(bf16).reshape(8, 64, 256)
        for offset in range(1, 8):
            return_op(s, offset).start()
        attended = dot(low_ref[...], kv[tokens, 256:512]).astype(bf16)
        for h in range(8):
            attended_ref[s, :, h * 256 : (h + 1) * 256] = attended[h * 64 : h * 64 + STEPS]
        turn_pairs(query, v["query_t"])

        def tile(begin, width):
            at = pl.ds(begin, width)
            to = pl.ds(pl.multiple_of(start + begin, 128), width)
            for left, right, top in ((v["query_t"], ds_ref, 0), (v["cot_t"].at[s], low_ref, 256)):
                total = jnp.zeros((256, width), f32)
                for h in range(8):
                    term = dot(left[h], right[(h // 2) * 128 : (h // 2 + 1) * 128, at])
                    total = total + term.astype(bf16).astype(f32)
                gkv[top : top + 256, to] = total.astype(bf16)

        def wide_tile(t, carry):
            tile(pl.multiple_of(t * 256, 256), 256)
            return carry

        lax.fori_loop(0, 3, wide_tile, 0)
        tile(768, 128)
        return carry

    lax.fori_loop(0, 2, sample, 0)

    v["group_gq"][seq] = v["gq"][seq]

    for s in range(2):
        turned = gkv[:, s * KEYS + PREFIX - 48 : (s + 1) * KEYS].astype(f32).T[48 : 48 + PAD_STEPS]
        ds_ref[s * 64 : (s + 1) * 64, 0:512] = turned.astype(bf16)
    grad, pair = v["grad"], v["pair"]
    pairing = links.slots(8)

    def pair_op(k):
        a, b = k // 2, lax.rem(k, 2)
        return links.op(
            grad.at[a, b, 1 - core], pair.at[a, pl.ds(b * 2, 2)], place.sibling, pairing + k
        )

    def grad_prefix(k, carry):
        at = pl.ds(pl.multiple_of(k * 256, 256), 256)
        a, b = k // 2, lax.rem(k, 2)
        value = dot(gkv[...], norm[:, at])
        high = value.astype(bf16)
        low = (value - high.astype(f32)).astype(bf16)
        value = lanes_dot(eye[...], high) + lanes_dot(eye[...], low)
        grad[a, b, :, :, :, 0:16, :] = value[:, 0:256].reshape(2, 2, 4, 16, 256)
        grad[a, b, :, :, :, 16:32, :] = value[:, 256:512].reshape(2, 2, 4, 16, 256)
        action = dot(v["left_t"][at, :], ds_ref[0:128, 0:256])
        action += dot(v["right_t"][at, :], ds_ref[0:128, 256:512])
        grad[a, b, :, :, :, 32:48, :] = action.reshape(2, 2, 4, 16, 256)
        pair_op(k).start()
        return carry

    def grad_query():
        for offset in range(1, 8):
            member = place.group_member(offset, -1)
            for s in range(2):
                mine = slice(s * PAD_STEPS, (s + 1) * PAD_STEPS)
                links.arrived(
                    v["group_gq"].at[member, mine], (place.dp, member), returns + s * 8 + offset
                )
        rows = v["group_gq"][...].reshape(1024, 256)
        for a in range(4):
            value = dot(act_t[a * 256 : (a + 1) * 256, :], rows)
            v["grad_query"][a] = value.reshape(2, 2, 64, 256)

    def finish(part):
        def store(value):
            if part == 2:
                out_action_ref[:, 0:256] = value[0:8]
                out_action_ref[:, 256:512] = value[8:16]
            else:
                out_prefix_ref[:, part * 256 : (part + 1) * 256] = value

        return store

    def paired():
        for k in range(8):
            pair_op(k).wait_recv()
        yield

    lax.fori_loop(0, 8, grad_prefix, 0, unroll=2)
    query_work = reduce_query(links, place, grad_query, v, out_query_ref)
    works = [query_work, paired()]
    works += [reduce_part(links, place, grad, pair, v, part, finish(part)) for part in range(3)]
    early = list(links.sent)
    links.sent.clear()

    def drain(ops):
        def run():
            for op in ops:
                op.wait_send()

        return run

    run_together(works, [drain(early[i::4]) for i in range(4)])
    for op in links.sent:
        op.wait_send()
    for offset in range(1, 8):
        for s in range(2):
            return_op(s, offset).wait_send()
    for k in range(8):
        pair_op(k).wait_send()


def step(
    cameras, text_length, flow_time, hidden, noise, clean, input_weight, cot,
    own_prefix, own_action, own_query, sine, cosine,
):
    bf16, f32 = jnp.bfloat16, jnp.float32
    hbm, vmem = pl.BlockSpec(memory_space=pltpu.HBM), pl.BlockSpec(memory_space=pltpu.VMEM)
    scratch = dict(
        norm=pltpu.VMEM((2 * KEYS, 2048), bf16),
        own_noisy=pltpu.VMEM((32, 128), bf16),
        query_weight=pltpu.VMEM((4, 2, 2, 64, 256), bf16),
        noisy=pltpu.VMEM((8, 32, 128), bf16),
        time=pltpu.VMEM((8, 2, 1024), f32),
        own_time=pltpu.VMEM((2, 1024), f32),
        act=pltpu.VMEM((1024, 1024), bf16),
        act_t=pltpu.VMEM((1024, 1024), bf16),
        left=pltpu.VMEM((128, 2048), bf16),
        right=pltpu.VMEM((128, 2048), bf16),
        cot=pltpu.VMEM((8, 128, 256), bf16),
        eye=pltpu.VMEM((256, 256), bf16),
        left_t=pltpu.VMEM((2048, 128), bf16),
        right_t=pltpu.VMEM((2048, 128), bf16),
        query=pltpu.VMEM((8, 128, 256), bf16),
        query_out=pltpu.VMEM((8, 128, 256), bf16),
        gq=pltpu.VMEM((8, 128, 256), bf16),
        group_gq=pltpu.VMEM((8, 128, 256), bf16),
        wp=pltpu.VMEM((2048, 512), bf16),
        kv=pltpu.VMEM((2 * KEYS, 512), bf16),
        low=pltpu.VMEM((512, KEYS), bf16),
        ds=pltpu.VMEM((512, KEYS), bf16),
        query_t=pltpu.VMEM((8, 256, 128), bf16),
        cot_t=pltpu.VMEM((2, 8, 256, 128), bf16),
        gkv=pltpu.VMEM((512, 2 * KEYS), bf16),
        grad=pltpu.VMEM((4, 2, 2, 2, 4, ROWS, 256), f32),
        pair=pltpu.VMEM((4, 4, 4, ROWS, 256), f32),
        grad_query=pltpu.VMEM((4, 2, 2, 64, 256), f32),
        query_pair=pltpu.VMEM((4, 2, 64, 256), f32),
        query_wire=pltpu.VMEM((4, 2, 64, 256), bf16),
        query_half=pltpu.VMEM((2, 64, 256), bf16),
        query_full=pltpu.VMEM((2, 2, 64, 256), bf16),
        query_sum=pltpu.VMEM((2, 64, 256), f32),
        query_far=pltpu.VMEM((64, 256), bf16),
        query_far_out=pltpu.VMEM((64, 256), bf16),
        send=pltpu.SemaphoreType.DMA((192,)),
        recv=pltpu.SemaphoreType.DMA((192,)),
        load=pltpu.SemaphoreType.DMA((16,)),
        flow=pltpu.SMEM((2,), f32),
        cameras=pltpu.SMEM((2,), jnp.int32),
        text=pltpu.SMEM((2,), jnp.int32),
        noise=pltpu.VMEM((2, 32, STEPS), bf16),
        clean=pltpu.VMEM((2, 32, STEPS), bf16),
        input=pltpu.VMEM((32, 1024), bf16),
        cot_in=pltpu.VMEM((STEPS, 2, 2048), bf16),
        own_prefix=pltpu.VMEM((16, 512), bf16),
        own_action=pltpu.VMEM((8, 512), bf16),
        own_query=pltpu.VMEM((64, 256), bf16),
    )
    for part in range(3):
        scratch[f"weight_{part}"] = pltpu.VMEM((2, 4, 4, 4, 16, 256), bf16)
        scratch[f"wire1_{part}"] = pltpu.VMEM((4, 4, 4, 16, 256), bf16)
        scratch[f"half1_{part}"] = pltpu.VMEM((2, 2, 4, 16, 256), bf16)
        scratch[f"full1_{part}"] = pltpu.VMEM((2, 4, 4, 16, 256), bf16)
        scratch[f"sum2_{part}"] = pltpu.VMEM((4, 4, 16, 256), f32)
        scratch[f"wire2_{part}"] = pltpu.VMEM((4, 4, 16, 256), bf16)
        scratch[f"full2_{part}"] = pltpu.VMEM((3, 4, 16, 256), bf16)
        scratch[f"sum3_{part}"] = pltpu.VMEM((4, 16, 256), f32)
        scratch[f"full3_{part}"] = pltpu.VMEM((3, 16, 256), f32)
    return pl.pallas_call(
        step_kernel,
        out_shape=(
            jax.ShapeDtypeStruct((2, STEPS, 2048), bf16),
            jax.ShapeDtypeStruct((64, 256), f32),
            jax.ShapeDtypeStruct((16, 512), f32),
            jax.ShapeDtypeStruct((8, 512), f32),
        ),
        in_specs=[hbm] * 11 + [vmem] * 2,
        out_specs=(vmem,) * 4,
        scratch_shapes=[scratch],
        compiler_params=pltpu.CompilerParams(
            collective_id=1, has_side_effects=True, vmem_limit_bytes=VMEM_LIMIT
        ),
        cost_estimate=pl.CostEstimate(
            flops=10**10, bytes_accessed=9 * 10**6, transcendentals=10**6
        ),
        name="step",
    )(
        *[
            pltpu.with_memory_space_constraint(operand, pltpu.HBM)
            for operand in (
                cameras, text_length, flow_time, hidden, noise, clean, input_weight, cot,
                own_prefix, own_action, own_query,
            )
        ],
        sine,
        cosine,
    )


def time_feature(flow_col, row_width):
    half_width = row_width // 2
    fraction = jnp.arange(half_width, dtype=jnp.float32) / (half_width - 1)
    period = 0.004 * 1000.0**fraction
    angle = flow_col[..., None] * (2.0 * math.pi / period)
    return jnp.sin(angle), jnp.cos(angle)


def on_device(
    prefix_hidden,
    cameras,
    text_length,
    action_noise,
    clean_actions,
    flow_time,
    input_weight,
    prefix_kv_weight,
    action_kv_weight,
    query_weight,
    cotangent,
):
    sine, cosine = time_feature(flow_time, 1024)
    return step(
        cameras,
        text_length,
        flow_time,
        prefix_hidden,
        action_noise.transpose(0, 2, 1),
        clean_actions.transpose(0, 2, 1),
        input_weight,
        cotangent.transpose(1, 0, 2),
        prefix_kv_weight,
        action_kv_weight,
        query_weight,
        sine,
        cosine,
    )


def solution(mesh):
    return jax.shard_map(
        on_device,
        mesh=mesh,
        in_specs=(
            P(("dp", "seq"), None, None),
            P(("dp", "seq")),
            P(("dp", "seq")),
            P(("dp", "seq"), None, None),
            P(("dp", "seq"), None, None),
            P(("dp", "seq")),
            P(),
            P(("dp", "seq"), None),
            P(("dp", "seq"), None),
            P("dp", "seq"),
            P(("dp", "seq"), None, None),
        ),
        out_specs=(
            P(("dp", "seq"), None, None),
            P("dp", "seq"),
            P(("dp", "seq"), None),
            P(("dp", "seq"), None),
        ),
        check_vma=False,
    )
```

```python
import math

import jax
import jax.numpy as jnp
from jax import lax
from jax.experimental import pallas as pl
from jax.experimental.pallas import tpu as pltpu
from jax.sharding import PartitionSpec as P

IMG = 256
EPS = 1e-06
MESH = pl.DeviceIdType.MESH
VMEM_LIMIT = 52 * 1024 * 1024
PREFIX, STEPS, PAD_STEPS, KEYS = 816, 50, 64, 896

ROWS = 48
ORDERS = ("xyz", "yzx", "zxy")
HALVES = (slice(0, 2), slice(2, 4))
FULL = slice(None)


class Place:
    def __init__(self):
        self.dp = lax.axis_index("dp")
        self.seq = lax.axis_index("seq")
        self.core = lax.rem(self.dp, 2)
        self.z_hi = lax.rem(self.dp // 2, 2)
        self.z_lo = self.seq // 4
        self.at = {
            "y": self.dp // 4,
            "z": self.z_hi * 2 + self.z_lo,
            "x": lax.rem(self.seq, 4),
        }
        self.sibling = self.device(core=1 - self.core)
        self.z_far = self.device(z=self.shifted("z", 2))

    def device(self, core=None, **moved):
        at = {**self.at, **moved}
        core = self.core if core is None else core
        return (
            at["y"] * 4 + (at["z"] // 2) * 2 + core,
            lax.rem(at["z"], 2) * 4 + at["x"],
        )

    def shifted(self, axis, by):
        return lax.rem(self.at[axis] + by, 4)

    def group_member(self, offset, sign=1):
        z_lo = lax.rem(self.z_lo + lax.div(offset, 4), 2)
        x = lax.rem(self.at["x"] + sign * lax.rem(offset, 4) + 4, 4)
        return z_lo * 4 + x

    def greet(self):
        barrier = pltpu.get_barrier_semaphore()
        others = [self.sibling, self.z_far]
        others += [(self.dp, self.group_member(offset)) for offset in range(1, 8)]
        others += [self.device(y=self.shifted("y", by)) for by in (1, 2, 3)]
        beyond = lax.rem(self.at["z"] + 3 + 2 * self.z_lo, 4)
        others.append(self.device(z=beyond))
        for other in others:
            pl.semaphore_signal(barrier, inc=1, device_id=other, device_id_type=MESH)
        self.greeted = len(others)

    def meet(self):
        pl.semaphore_wait(pltpu.get_barrier_semaphore(), self.greeted)


class Links:
    def __init__(self, send_sem, recv_sem):
        self.send_sem, self.recv_sem = send_sem, recv_sem
        self.used = 0
        self.sent = []

    def slots(self, count):
        self.used += count
        return self.used - count

    def op(self, src, dst, to, slot):
        return pltpu.make_async_remote_copy(
            src_ref=src,
            dst_ref=dst,
            send_sem=self.send_sem.at[slot],
            recv_sem=self.recv_sem.at[slot],
            device_id=to,
            device_id_type=MESH,
        )

    def go(self, src, dst, to, slot):
        op = self.op(src, dst, to, slot)
        op.start()
        self.sent.append(op)

    def arrived(self, dst, to, slot):
        self.op(dst, dst, to, slot).wait_recv()


def run_together(works, tasks=()):
    live, tasks = list(works), list(tasks)
    while live or tasks:
        live = [work for work in live if next(work, "end") != "end"]
        if tasks:
            tasks.pop(0)()


def direct(links, place, axis, view, slot):
    own = place.at[axis]
    for by in (2, 1, 3):
        to = place.device(**{axis: place.shifted(axis, by)})
        links.go(view(own), view(own), to, slot + by - 1)
    yield
    for by in (1, 3, 2):
        links.arrived(view(place.shifted(axis, 4 - by)), place.sibling, slot + by - 1)


def ring(links, place, axis, view, slot, landed):
    own, right, left, across = (place.shifted(axis, by) for by in (0, 1, 3, 2))
    to_right, to_left = (place.device(**{axis: at}) for at in (right, left))
    for half in (0, 1):
        links.go(view(own, half), view(own, half), to_right, slot + half)
        links.go(view(own, 1 - half), view(own, 1 - half), to_left, slot + 2 + half)
    landed(own)
    yield
    links.arrived(view(left, 0), to_right, slot)
    links.go(view(left, 0), view(left, 0), to_right, slot + 4)
    links.arrived(view(right, 1), to_left, slot + 2)
    links.go(view(right, 1), view(right, 1), to_left, slot + 5)
    yield
    links.arrived(view(left, 1), to_right, slot + 1)
    landed(left)
    links.arrived(view(right, 0), to_left, slot + 3)
    landed(right)
    yield
    links.arrived(view(across, 0), to_right, slot + 4)
    links.arrived(view(across, 1), to_left, slot + 5)
    landed(across)


class Share:
    def __init__(self, links, place, view):
        self.links, self.place, self.view = links, place, view
        self.slot, self.due = links.slots(4), []

    def __call__(self, block):
        links, core = self.links, self.place.core
        slot = self.slot + len(self.due)
        mine = self.view(core, block)
        links.go(mine, mine, self.place.sibling, slot)
        self.due.append((self.view(1 - core, block), slot))

    def wait(self):
        for view, slot in self.due:
            self.links.arrived(view, self.place.sibling, slot)


def gather_part(links, place, ref, order):
    core = place.core
    first, second, third = order
    slot = links.slots(12)
    at = place.at
    yield from direct(
        links, place, first, lambda block: ref.at[core, at[third], at[second], block], slot
    )
    yield from direct(links, place, second, lambda block: ref.at[core, at[third], block], slot + 3)
    share = Share(links, place, lambda core, block: ref.at[core, block])

    def view(block, half=None):
        return ref.at[core, block] if half is None else ref.at[core, block, HALVES[half]]

    yield from ring(links, place, third, view, slot + 6, share)
    yield
    share.wait()


def gather_query(links, place, query_ref, then):
    core, y, z_hi = place.core, place.at["y"], place.z_hi
    slot = links.slots(7)
    links.go(query_ref.at[y, z_hi, core], query_ref.at[y, z_hi, core], place.z_far, slot)
    yield
    links.arrived(query_ref.at[y, 1 - z_hi, core], place.z_far, slot)
    share = Share(links, place, lambda core, block: query_ref.at[block, :, core])

    def view(block, half=None):
        return query_ref.at[block, FULL if half is None else half, core]

    yield from ring(links, place, "y", view, slot + 1, share)
    yield
    share.wait()
    then()


def reduce_ring(links, place, axis, pack, wire, half, fulls, slot):
    own, right, left, across = (place.shifted(axis, by) for by in (0, 1, 3, 2))
    to_right, to_left = (place.device(**{axis: at}) for at in (right, left))
    pack(across, 0)
    links.go(wire(across, 0), half.at[0], to_right, slot)
    pack(across, 1)
    links.go(wire(across, 1), half.at[1], to_left, slot + 1)
    yield
    pack(right, 1)
    links.go(wire(right, 1), fulls(0, 1), to_right, slot + 2)
    pack(left, 0)
    links.go(wire(left, 0), fulls(1, 0), to_left, slot + 3)
    yield
    links.arrived(half.at[0], to_right, slot)
    pack(right, 0, half.at[0])
    links.go(wire(right, 0), fulls(0, 0), to_right, slot + 4)
    links.arrived(half.at[1], to_left, slot + 1)
    pack(left, 1, half.at[1])
    links.go(wire(left, 1), fulls(1, 1), to_left, slot + 5)
    yield
    links.arrived(fulls(0, 1), to_right, slot + 2)
    links.arrived(fulls(1, 0), to_left, slot + 3)
    links.arrived(fulls(0, 0), to_right, slot + 4)
    links.arrived(fulls(1, 1), to_left, slot + 5)


def reduce_direct(links, place, axis, block_of, landing, slot):
    for by in (2, 1, 3):
        block = place.shifted(axis, by)
        links.go(
            block_of(block), landing.at[by - 1], place.device(**{axis: block}), slot + by - 1
        )
    yield
    for by in (1, 3, 2):
        links.arrived(landing.at[by - 1], place.sibling, slot + by - 1)


def reduce_part(links, place, grad_ref, pair_ref, v, part, finish):
    f32, bf16 = jnp.float32, jnp.bfloat16
    rows = slice(part * 16, part * 16 + 16)
    core = place.core
    first, second, third = ORDERS[part]
    wire, half, full = (v[f"{name}1_{part}"] for name in ("wire", "half", "full"))
    slot = links.slots(12)

    def mine(block, i, j):
        at = {first: block, second: i, third: j}
        y, z, x = at["y"], at["z"], at["x"]
        return grad_ref[y, z // 2, core, lax.rem(z, 2), x, rows, :] + pair_ref[y, z, x, rows, :]

    def pack(block, side, extra=None):
        for i in range(2):
            for j in range(4):
                value = mine(block, side * 2 + i, j)
                if extra is not None:
                    value = value + extra[i, j].astype(f32)
                wire[block, side * 2 + i, j] = value.astype(bf16)

    yield from reduce_ring(
        links, place, first, pack, lambda block, side: wire.at[block, HALVES[side]], half,
        lambda way, side: full.at[way, HALVES[side]], slot,
    )
    total, wire2, full2 = (v[f"{name}2_{part}"] for name in ("sum", "wire", "full"))
    for i in range(4):
        for j in range(4):
            value = mine(place.at[first], i, j)
            value = value + full[0, i, j].astype(f32) + full[1, i, j].astype(f32)
            total[i, j] = value
            wire2[i, j] = value.astype(bf16)
    yield from reduce_direct(links, place, second, lambda block: wire2.at[block], full2, slot + 6)
    total3, full3 = v[f"sum3_{part}"], v[f"full3_{part}"]
    value = total[place.at[second]]
    for k in range(3):
        value = value + full2[k].astype(f32)
    total3[...] = value
    yield from reduce_direct(links, place, third, lambda block: total3.at[block], full3, slot + 9)
    finish(total3[place.at[third]] + full3[0] + full3[1] + full3[2])


def reduce_query(links, place, first, v, out_ref):
    f32, bf16 = jnp.float32, jnp.bfloat16
    core, z_hi = place.core, place.z_hi
    grad_ref, pair_ref, wire = v["grad_query"], v["query_pair"], v["query_wire"]
    half, full, total, far_ref = v["query_half"], v["query_full"], v["query_sum"], v["query_far"]
    slot = links.slots(8)
    first()
    links.go(grad_ref.at[:, :, 1 - core], pair_ref, place.sibling, slot)
    yield
    links.arrived(pair_ref, place.sibling, slot)

    def pack(block, side, extra=None):
        value = grad_ref[block, side, core] + pair_ref[block, side]
        if extra is not None:
            value = value + extra[...].astype(f32)
        wire[block, side] = value.astype(bf16)

    yield from reduce_ring(
        links, place, "y", pack, lambda block, side: wire.at[block, side], half,
        lambda way, side: full.at[way, side], slot + 1,
    )
    own = place.at["y"]
    value = grad_ref[own, :, core] + pair_ref[own]
    total[...] = value + full[0].astype(f32) + full[1].astype(f32)
    v["query_far_out"][...] = total[1 - z_hi].astype(bf16)
    links.go(v["query_far_out"], far_ref, place.z_far, slot + 7)
    yield
    links.arrived(far_ref, place.z_far, slot + 7)
    out_ref[...] = total[z_hi] + far_ref[...].astype(f32)


def lanes_dot(left, right):
    return lax.dot_general(
        left, right, (((1,), (1,)), ((), ())), preferred_element_type=jnp.float32
    )


def rows_dot(left, right):
    return lax.dot_general(
        left, right, (((0,), (0,)), ((), ())), preferred_element_type=jnp.float32
    )


def dot(left, right):
    return jnp.dot(left, right, preferred_element_type=jnp.float32)


def step_kernel(
    cameras_hbm, text_hbm, flow_hbm, hidden_hbm, noise_hbm, clean_hbm, input_hbm, cot_hbm,
    own_prefix_hbm, own_action_hbm, own_query_hbm, sin_ref, cos_ref,
    attended_ref, out_query_ref, out_prefix_ref, out_action_ref,
    v,
):
    f32, bf16 = jnp.float32, jnp.bfloat16
    place = Place()
    core, y, z_hi, z_lo, x = place.core, place.at["y"], place.z_hi, place.z_lo, place.at["x"]
    seq = place.seq
    links = Links(v["send"], v["recv"])
    place.greet()

    norm = v["norm"]
    operands = dict(
        flow=flow_hbm, noise=noise_hbm, clean=clean_hbm, own_prefix=own_prefix_hbm,
        own_action=own_action_hbm, own_query=own_query_hbm, input=input_hbm, cot_in=cot_hbm,
        cameras=cameras_hbm, text=text_hbm,
    )
    fetches = {}
    for i, (name, ref) in enumerate(operands.items()):
        fetches[name] = pltpu.make_async_copy(ref, v[name], v["load"].at[6 + i])
        fetches[name].start()
    loads = []
    chunks = [(s, start, count) for s in range(2) for start, count in ((0, 288), (288, 288), (576, 240))]
    for k, (s, start, count) in enumerate(chunks):
        load = pltpu.make_async_copy(
            hidden_hbm.at[s, pl.ds(start, count), :],
            norm.at[pl.ds(s * KEYS + start, count), :],
            v["load"].at[k],
        )
        load.start()
        loads.append(load)

    query_weight, eye = v["query_weight"], v["eye"]
    for name in ("own_prefix", "own_action", "own_query"):
        fetches[name].wait()
    own_prefix = v["own_prefix"]
    own_action = v["own_action"][...].astype(f32)
    own_action = jnp.concatenate([own_action[:, 0:256], own_action[:, 256:512]], axis=0)
    own_parts = (own_prefix[:, 0:256], own_prefix[:, 256:512], own_action.astype(bf16))
    for part, (first, second, third) in enumerate(ORDERS):
        at = place.at
        v[f"weight_{part}"][core, at[third], at[second], at[first]] = own_parts[part]
    query_weight[y, z_hi, core] = v["own_query"][...]
    place.meet()

    packet = links.slots(16)
    def send_packets():
        for name in ("flow", "noise", "clean"):
            fetches[name].wait()
        own_noisy = v["own_noisy"]
        noisy = []
        for s in range(2):
            t = v["flow"][s]
            noisy.append(t * v["noise"][s].astype(f32) + (1.0 - t) * v["clean"][s].astype(f32))
        blank = jnp.zeros((32, PAD_STEPS - STEPS), f32)
        own_noisy[...] = jnp.concatenate([noisy[0], blank, noisy[1], blank], axis=1).astype(bf16)
        v["noisy"][seq] = own_noisy[...]
        own_time = v["own_time"]
        own_time[:, 0:512] = sin_ref[...]
        own_time[:, 512:1024] = cos_ref[...]
        v["time"][seq] = own_time[...]
        for offset in range(1, 8):
            to = (place.dp, place.group_member(offset))
            links.go(own_noisy, v["noisy"].at[seq], to, packet + offset)
            links.go(own_time, v["time"].at[seq], to, packet + 8 + offset)
        fetches["input"].wait()
        row = lax.broadcasted_iota(jnp.int32, (256, 256), 0)
        col = lax.broadcasted_iota(jnp.int32, (256, 256), 1)
        eye[...] = jnp.where(row == col, 1.0, 0.0).astype(bf16)

    act, act_t = v["act"], v["act_t"]

    def make_rows(member):
        at = pl.ds(pl.multiple_of(member * 128, 128), 128)
        wide = rows_dot(v["noisy"][member], v["input"][...])
        time = v["time"][member]
        parts = []
        for s in range(2):
            part = wide[s * PAD_STEPS : (s + 1) * PAD_STEPS] + time[s : s + 1]
            scale = lax.rsqrt(jnp.mean(part * part, axis=-1, keepdims=True) + EPS)
            parts.append((part * scale).astype(bf16))
        rows = jnp.concatenate(parts, axis=0)
        act[at, :] = rows
        for f in range(4):
            cols = slice(f * 256, (f + 1) * 256)
            act_t[cols, at] = lanes_dot(eye[...], rows[:, cols]).astype(bf16)

    def spread_rows():
        at = pl.ds(pl.multiple_of(seq * 128, 128), 128)
        feature = lax.broadcasted_iota(jnp.int32, (256, 128), 1)
        k = lax.broadcasted_iota(jnp.int32, (256, 128), 0)
        within = k % 16
        origin = (k // 16) * 8 + within
        first = jnp.where((within < 8) & (feature == origin), 1.0, 0.0).astype(bf16)
        second = jnp.where((within >= 8) & (feature == origin - 8), 1.0, 0.0).astype(bf16)
        for spread, name in ((first, "left"), (second, "right")):
            for i in range(8):
                cols, wide = slice(i * 128, (i + 1) * 128), slice(i * 256, (i + 1) * 256)
                v[name][:, wide] = lanes_dot(act[at, cols], spread).astype(bf16)
                v[name + "_t"][wide, :] = dot(spread, act_t[cols, at]).astype(bf16)

    def group_rows(low, high):
        def run():
            members = [place.group_member(offset, -1) for offset in range(low, high)]
            for offset, member in zip(range(low, high), members):
                if offset == 0:
                    continue
                to = (place.dp, member)
                links.arrived(v["noisy"].at[member], to, packet + offset)
                links.arrived(v["time"].at[member], to, packet + 8 + offset)
            for member in members:
                make_rows(member)

        return run

    def normalize(chunk):
        def run():
            loads[chunk].wait()
            s, start, count = chunks[chunk]

            def places(i):
                return [
                    pl.ds(pl.multiple_of(s * KEYS + start + i * 48 + j * 16, 16), 16)
                    for j in range(3)
                ]

            def scales(i):
                found = []
                for at in places(i):
                    wide = norm[at, :].astype(f32)
                    found.append(lax.rsqrt(jnp.mean(wide * wide, axis=-1, keepdims=True) + EPS))
                return tuple(found)

            def body(i, present):
                following = scales(jnp.minimum(i + 1, count // 48 - 1))
                for at, scale in zip(places(i), present):
                    norm[at, :] = (norm[at, :].astype(f32) * scale).astype(bf16)
                return following

            lax.fori_loop(0, count // 48, body, scales(0))

        return run

    def place_rows():
        fetches["cot_in"].wait()
        v["cot"][...] = jnp.zeros_like(v["cot"])
        for s in range(2):
            for h in range(8):
                v["cot"][h, s * PAD_STEPS : s * PAD_STEPS + STEPS, :] = v["cot_in"][
                    :, s, h * 256 : (h + 1) * 256
                ]
        for s in range(2):
            norm[s * KEYS + PREFIX : (s + 1) * KEYS, :] = jnp.zeros((KEYS - PREFIX, 2048), bf16)

    exchange = links.slots(16)

    def send_queries():
        wide = query_weight[...].reshape(1024, 256)
        for half in range(2):
            rows = slice(half * 512, (half + 1) * 512)
            value = dot(act[rows, :], wide).astype(bf16)
            v["query_out"][half * 4 : half * 4 + 4] = value.reshape(4, 128, 256)
        for offset in (2, 6, 1, 3, 5, 7, 4):
            member = place.group_member(offset)
            links.go(
                v["query_out"].at[member], v["query"].at[seq], (place.dp, member),
                exchange + offset,
            )
        v["query"][seq] = v["query_out"][seq]

    works = [gather_query(links, place, query_weight, send_queries)]
    works += [gather_part(links, place, v[f"weight_{part}"], ORDERS[part]) for part in range(3)]
    tasks = [lambda: (send_packets(), normalize(0)()), normalize(1), group_rows(0, 4), group_rows(4, 8)]
    tasks += [normalize(chunk) for chunk in range(2, 6)] + [spread_rows, place_rows]
    run_together(works, tasks)

    wp, kv = v["wp"], v["kv"]

    def block_rows(part, a, b):
        ref, order = v[f"weight_{part}"], ORDERS[part][::-1]
        pieces = []
        for c in range(2):
            for low in range(2):
                at = {"y": a, "z": b * 2 + low}
                if order[2] == "x":
                    pieces.append(ref[c, at[order[0]], at[order[1]]].reshape(64, 256))
                else:
                    for col in range(4):
                        at["x"] = col
                        pieces.append(ref[c, at[order[0]], at[order[1]], at[order[2]]])
        return pieces

    def unpack(k, carry):
        keys, values = carry
        a, b = k // 2, lax.rem(k, 2)
        for part in range(2):
            start = k * 256
            for piece in block_rows(part, a, b):
                at = pl.ds(pl.multiple_of(start, 16), piece.shape[0])
                wp[at, part * 256 : (part + 1) * 256] = piece
                start += piece.shape[0]
        block = jnp.concatenate(block_rows(2, a, b), axis=0)
        at = pl.ds(pl.multiple_of(k * 256, 256), 256)
        return keys + dot(v["left"][:, at], block), values + dot(v["right"][:, at], block)

    zero = jnp.zeros((2 * PAD_STEPS, 256), f32)
    keys, values = lax.fori_loop(0, 8, unpack, (zero, zero))
    keys, values = keys.astype(bf16), values.astype(bf16)

    def prefix(i, carry):
        at = pl.ds(pl.multiple_of(i * 448, 64), 448)
        kv[at, :] = dot(norm[at, :], wp[...]).astype(bf16)
        return carry

    lax.fori_loop(0, 4, prefix, 0)
    for s in range(2):
        rows = slice(s * PAD_STEPS, (s + 1) * PAD_STEPS)
        start = s * KEYS + PREFIX
        kv[start : start + PAD_STEPS, 0:256] = keys[rows]
        kv[start : start + PAD_STEPS, 256:512] = values[rows]

    low_ref, ds_ref, gkv = v["low"], v["ds"], v["gkv"]

    def sixteenth(rows):
        return (rows.astype(f32) * 0.0625).astype(bf16)

    def turn_pairs(rows, turned):
        first = lax.broadcasted_iota(jnp.int32, (256, 128), 1) < 64
        across = lanes_dot(eye[...], rows)
        for h in range(8):
            pair = across[:, (h // 2) * 128 : (h // 2 + 1) * 128]
            keep = first if h % 2 == 0 else jnp.logical_not(first)
            turned[h] = jnp.where(keep, pair, 0.0).astype(bf16)

    for s in range(2):
        cot = v["cot"][:, s * PAD_STEPS : (s + 1) * PAD_STEPS, :].reshape(512, 256)
        turn_pairs(cot, v["cot_t"].at[s])
    fetches["cameras"].wait()
    fetches["text"].wait()
    for offset in range(1, 8):
        member = place.group_member(offset, -1)
        links.arrived(v["query"].at[member], (place.dp, member), exchange + offset)

    def sample(s, carry):
        length = v["cameras"][s] * IMG + v["text"][s]
        mine = pl.ds(pl.multiple_of(s * PAD_STEPS, PAD_STEPS), PAD_STEPS)
        start = pl.multiple_of(s * KEYS, 128)
        tokens = pl.ds(start, KEYS)
        column = lax.broadcasted_iota(jnp.int32, (1, KEYS), 1)
        valid = (column < length) | ((column >= PREFIX) & (column < PREFIX + STEPS))
        bias = jnp.where(valid, 0.0, -1e30)
        query = v["query"][:, mine, :].reshape(512, 256)
        cot = v["cot"][:, mine, :].reshape(512, 256)
        logits = lanes_dot(sixteenth(query), kv[tokens, 0:256]) + bias
        expo = jnp.exp(logits - jnp.max(logits, axis=-1, keepdims=True))
        probs = expo * (1.0 / jnp.sum(expo, axis=-1, keepdims=True))
        low_ref[...] = probs.astype(bf16)
        dprob = lanes_dot(sixteenth(cot), kv[tokens, 256:512])
        inner = jnp.sum(probs * dprob, axis=-1, keepdims=True)
        ds_ref[...] = (probs * (dprob - inner)).astype(bf16)
        v["gq"][:, mine, :] = dot(ds_ref[...], kv[tokens, 0:256]).astype(bf16).reshape(8, 64, 256)
        attended = dot(low_ref[...], kv[tokens, 256:512]).astype(bf16)
        for h in range(8):
            attended_ref[s, :, h * 256 : (h + 1) * 256] = attended[h * 64 : h * 64 + STEPS]
        turn_pairs(query, v["query_t"])

        def tile(begin, width):
            at = pl.ds(begin, width)
            to = pl.ds(pl.multiple_of(start + begin, 128), width)
            for left, right, top in ((v["query_t"], ds_ref, 0), (v["cot_t"].at[s], low_ref, 256)):
                total = jnp.zeros((256, width), f32)
                for h in range(8):
                    term = dot(left[h], right[(h // 2) * 128 : (h // 2 + 1) * 128, at])
                    total = total + term.astype(bf16).astype(f32)
                gkv[top : top + 256, to] = total.astype(bf16)

        def wide_tile(t, carry):
            tile(pl.multiple_of(t * 256, 256), 256)
            return carry

        lax.fori_loop(0, 3, wide_tile, 0)
        tile(768, 128)
        return carry

    lax.fori_loop(0, 2, sample, 0)

    for offset in (2, 6, 1, 3, 5, 7, 4):
        member = place.group_member(offset)
        links.go(
            v["gq"].at[member], v["group_gq"].at[seq], (place.dp, member), exchange + 8 + offset
        )
    v["group_gq"][seq] = v["gq"][seq]

    for s in range(2):
        turned = gkv[:, s * KEYS + PREFIX - 48 : (s + 1) * KEYS].astype(f32).T[48 : 48 + PAD_STEPS]
        ds_ref[s * 64 : (s + 1) * 64, 0:512] = turned.astype(bf16)
    grad, pair = v["grad"], v["pair"]
    pairing = links.slots(8)

    def pair_op(k):
        a, b = k // 2, lax.rem(k, 2)
        return links.op(
            grad.at[a, b, 1 - core], pair.at[a, pl.ds(b * 2, 2)], place.sibling, pairing + k
        )

    def multiply(k):
        at = pl.ds(pl.multiple_of(k * 256, 256), 256)
        v["product"][lax.rem(k, 2)] = dot(gkv[...], norm[:, at])

    def deliver(k):
        at = pl.ds(pl.multiple_of(k * 256, 256), 256)
        a, b = lax.div(k, 2), lax.rem(k, 2)
        value = v["product"][b]
        high = value.astype(bf16)
        low = (value - high.astype(f32)).astype(bf16)
        value = lanes_dot(eye[...], high) + lanes_dot(eye[...], low)
        grad[a, b, :, :, :, 0:16, :] = value[:, 0:256].reshape(2, 2, 4, 16, 256)
        grad[a, b, :, :, :, 16:32, :] = value[:, 256:512].reshape(2, 2, 4, 16, 256)
        action = dot(v["left_t"][at, :], ds_ref[0:128, 0:256])
        action += dot(v["right_t"][at, :], ds_ref[0:128, 256:512])
        grad[a, b, :, :, :, 32:48, :] = action.reshape(2, 2, 4, 16, 256)
        pair_op(k).start()

    def grad_prefix(k, carry):
        deliver(k - 1)
        multiply(k)
        return carry

    multiply(0)
    lax.fori_loop(1, 8, grad_prefix, 0)
    deliver(7)

    def grad_query():
        for offset in range(1, 8):
            member = place.group_member(offset, -1)
            links.arrived(v["group_gq"].at[member], (place.dp, member), exchange + 8 + offset)
        rows = v["group_gq"][...].reshape(1024, 256)
        for a in range(4):
            value = dot(act_t[a * 256 : (a + 1) * 256, :], rows)
            v["grad_query"][a] = value.reshape(2, 2, 64, 256)

    def finish(part):
        def store(value):
            if part == 2:
                out_action_ref[:, 0:256] = value[0:8]
                out_action_ref[:, 256:512] = value[8:16]
            else:
                out_prefix_ref[:, part * 256 : (part + 1) * 256] = value

        return store

    def paired():
        for k in range(8):
            pair_op(k).wait_recv()
        yield

    query_work = reduce_query(links, place, grad_query, v, out_query_ref)
    works = [query_work, paired()]
    works += [reduce_part(links, place, grad, pair, v, part, finish(part)) for part in range(3)]
    early = list(links.sent)
    links.sent.clear()

    def drain(ops):
        def run():
            for op in ops:
                op.wait_send()

        return run

    run_together(works, [drain(early[i::4]) for i in range(4)])
    for op in links.sent:
        op.wait_send()
    for k in range(8):
        pair_op(k).wait_send()


def step(
    cameras, text_length, flow_time, hidden, noise, clean, input_weight, cot,
    own_prefix, own_action, own_query, sine, cosine,
):
    bf16, f32 = jnp.bfloat16, jnp.float32
    hbm, vmem = pl.BlockSpec(memory_space=pltpu.HBM), pl.BlockSpec(memory_space=pltpu.VMEM)
    scratch = dict(
        norm=pltpu.VMEM((2 * KEYS, 2048), bf16),
        own_noisy=pltpu.VMEM((32, 128), bf16),
        query_weight=pltpu.VMEM((4, 2, 2, 64, 256), bf16),
        noisy=pltpu.VMEM((8, 32, 128), bf16),
        time=pltpu.VMEM((8, 2, 1024), f32),
        own_time=pltpu.VMEM((2, 1024), f32),
        act=pltpu.VMEM((1024, 1024), bf16),
        act_t=pltpu.VMEM((1024, 1024), bf16),
        left=pltpu.VMEM((128, 2048), bf16),
        right=pltpu.VMEM((128, 2048), bf16),
        cot=pltpu.VMEM((8, 128, 256), bf16),
        eye=pltpu.VMEM((256, 256), bf16),
        left_t=pltpu.VMEM((2048, 128), bf16),
        right_t=pltpu.VMEM((2048, 128), bf16),
        query=pltpu.VMEM((8, 128, 256), bf16),
        query_out=pltpu.VMEM((8, 128, 256), bf16),
        gq=pltpu.VMEM((8, 128, 256), bf16),
        group_gq=pltpu.VMEM((8, 128, 256), bf16),
        wp=pltpu.VMEM((2048, 512), bf16),
        kv=pltpu.VMEM((2 * KEYS, 512), bf16),
        low=pltpu.VMEM((512, KEYS), bf16),
        ds=pltpu.VMEM((512, KEYS), bf16),
        query_t=pltpu.VMEM((8, 256, 128), bf16),
        cot_t=pltpu.VMEM((2, 8, 256, 128), bf16),
        gkv=pltpu.VMEM((512, 2 * KEYS), bf16),
        grad=pltpu.VMEM((4, 2, 2, 2, 4, ROWS, 256), f32),
        pair=pltpu.VMEM((4, 4, 4, ROWS, 256), f32),
        product=pltpu.VMEM((2, 512, 256), f32),
        grad_query=pltpu.VMEM((4, 2, 2, 64, 256), f32),
        query_pair=pltpu.VMEM((4, 2, 64, 256), f32),
        query_wire=pltpu.VMEM((4, 2, 64, 256), bf16),
        query_half=pltpu.VMEM((2, 64, 256), bf16),
        query_full=pltpu.VMEM((2, 2, 64, 256), bf16),
        query_sum=pltpu.VMEM((2, 64, 256), f32),
        query_far=pltpu.VMEM((64, 256), bf16),
        query_far_out=pltpu.VMEM((64, 256), bf16),
        send=pltpu.SemaphoreType.DMA((192,)),
        recv=pltpu.SemaphoreType.DMA((192,)),
        load=pltpu.SemaphoreType.DMA((16,)),
        flow=pltpu.SMEM((2,), f32),
        cameras=pltpu.SMEM((2,), jnp.int32),
        text=pltpu.SMEM((2,), jnp.int32),
        noise=pltpu.VMEM((2, 32, STEPS), bf16),
        clean=pltpu.VMEM((2, 32, STEPS), bf16),
        input=pltpu.VMEM((32, 1024), bf16),
        cot_in=pltpu.VMEM((STEPS, 2, 2048), bf16),
        own_prefix=pltpu.VMEM((16, 512), bf16),
        own_action=pltpu.VMEM((8, 512), bf16),
        own_query=pltpu.VMEM((64, 256), bf16),
    )
    for part in range(3):
        scratch[f"weight_{part}"] = pltpu.VMEM((2, 4, 4, 4, 16, 256), bf16)
        scratch[f"wire1_{part}"] = pltpu.VMEM((4, 4, 4, 16, 256), bf16)
        scratch[f"half1_{part}"] = pltpu.VMEM((2, 2, 4, 16, 256), bf16)
        scratch[f"full1_{part}"] = pltpu.VMEM((2, 4, 4, 16, 256), bf16)
        scratch[f"sum2_{part}"] = pltpu.VMEM((4, 4, 16, 256), f32)
        scratch[f"wire2_{part}"] = pltpu.VMEM((4, 4, 16, 256), bf16)
        scratch[f"full2_{part}"] = pltpu.VMEM((3, 4, 16, 256), bf16)
        scratch[f"sum3_{part}"] = pltpu.VMEM((4, 16, 256), f32)
        scratch[f"full3_{part}"] = pltpu.VMEM((3, 16, 256), f32)
    return pl.pallas_call(
        step_kernel,
        out_shape=(
            jax.ShapeDtypeStruct((2, STEPS, 2048), bf16),
            jax.ShapeDtypeStruct((64, 256), f32),
            jax.ShapeDtypeStruct((16, 512), f32),
            jax.ShapeDtypeStruct((8, 512), f32),
        ),
        in_specs=[hbm] * 11 + [vmem] * 2,
        out_specs=(vmem,) * 4,
        scratch_shapes=[scratch],
        compiler_params=pltpu.CompilerParams(
            collective_id=1, has_side_effects=True, vmem_limit_bytes=VMEM_LIMIT
        ),
        cost_estimate=pl.CostEstimate(
            flops=10**10, bytes_accessed=9 * 10**6, transcendentals=10**6
        ),
        name="step",
    )(
        *[
            pltpu.with_memory_space_constraint(operand, pltpu.HBM)
            for operand in (
                cameras, text_length, flow_time, hidden, noise, clean, input_weight, cot,
                own_prefix, own_action, own_query,
            )
        ],
        sine,
        cosine,
    )


def time_feature(flow_col, row_width):
    half_width = row_width // 2
    fraction = jnp.arange(half_width, dtype=jnp.float32) / (half_width - 1)
    period = 0.004 * 1000.0**fraction
    angle = flow_col[..., None] * (2.0 * math.pi / period)
    return jnp.sin(angle), jnp.cos(angle)


def on_device(
    prefix_hidden,
    cameras,
    text_length,
    action_noise,
    clean_actions,
    flow_time,
    input_weight,
    prefix_kv_weight,
    action_kv_weight,
    query_weight,
    cotangent,
):
    sine, cosine = time_feature(flow_time, 1024)
    return step(
        cameras,
        text_length,
        flow_time,
        prefix_hidden,
        action_noise.transpose(0, 2, 1),
        clean_actions.transpose(0, 2, 1),
        input_weight,
        cotangent.transpose(1, 0, 2),
        prefix_kv_weight,
        action_kv_weight,
        query_weight,
        sine,
        cosine,
    )


def solution(mesh):
    return jax.shard_map(
        on_device,
        mesh=mesh,
        in_specs=(
            P(("dp", "seq"), None, None),
            P(("dp", "seq")),
            P(("dp", "seq")),
            P(("dp", "seq"), None, None),
            P(("dp", "seq"), None, None),
            P(("dp", "seq")),
            P(),
            P(("dp", "seq"), None),
            P(("dp", "seq"), None),
            P("dp", "seq"),
            P(("dp", "seq"), None, None),
        ),
        out_specs=(
            P(("dp", "seq"), None, None),
            P("dp", "seq"),
            P(("dp", "seq"), None),
            P(("dp", "seq"), None),
        ),
        check_vma=False,
    )
```

```python
import math

import jax
import jax.numpy as jnp
from jax import lax
from jax.experimental import pallas as pl
from jax.experimental.pallas import tpu as pltpu
from jax.sharding import PartitionSpec as P

IMG = 256
EPS = 1e-06
MESH = pl.DeviceIdType.MESH
VMEM_LIMIT = 52 * 1024 * 1024
PREFIX, STEPS, PAD_STEPS, KEYS = 816, 50, 64, 896

ROWS = 48
ORDERS = ("xyz", "yzx", "zxy")
HALVES = (slice(0, 2), slice(2, 4))
FULL = slice(None)


class Place:
    def __init__(self):
        self.dp = lax.axis_index("dp")
        self.seq = lax.axis_index("seq")
        self.core = lax.rem(self.dp, 2)
        self.z_hi = lax.rem(self.dp // 2, 2)
        self.z_lo = self.seq // 4
        self.at = {
            "y": self.dp // 4,
            "z": self.z_hi * 2 + self.z_lo,
            "x": lax.rem(self.seq, 4),
        }
        self.sibling = self.device(core=1 - self.core)
        self.z_far = self.device(z=self.shifted("z", 2))

    def device(self, core=None, **moved):
        at = {**self.at, **moved}
        core = self.core if core is None else core
        return (
            at["y"] * 4 + (at["z"] // 2) * 2 + core,
            lax.rem(at["z"], 2) * 4 + at["x"],
        )

    def shifted(self, axis, by):
        return lax.rem(self.at[axis] + by, 4)

    def group_member(self, offset, sign=1):
        z_lo = lax.rem(self.z_lo + lax.div(offset, 4), 2)
        x = lax.rem(self.at["x"] + sign * lax.rem(offset, 4) + 4, 4)
        return z_lo * 4 + x

    def greet(self):
        barrier = pltpu.get_barrier_semaphore()
        others = [self.sibling, self.z_far]
        others += [(self.dp, self.group_member(offset)) for offset in range(1, 8)]
        others += [self.device(y=self.shifted("y", by)) for by in (1, 2, 3)]
        beyond = lax.rem(self.at["z"] + 3 + 2 * self.z_lo, 4)
        others.append(self.device(z=beyond))
        for other in others:
            pl.semaphore_signal(barrier, inc=1, device_id=other, device_id_type=MESH)
        self.greeted = len(others)

    def meet(self):
        pl.semaphore_wait(pltpu.get_barrier_semaphore(), self.greeted)


class Links:
    def __init__(self, send_sem, recv_sem):
        self.send_sem, self.recv_sem = send_sem, recv_sem
        self.used = 0
        self.sent = []

    def slots(self, count):
        self.used += count
        return self.used - count

    def op(self, src, dst, to, slot):
        return pltpu.make_async_remote_copy(
            src_ref=src,
            dst_ref=dst,
            send_sem=self.send_sem.at[slot],
            recv_sem=self.recv_sem.at[slot],
            device_id=to,
            device_id_type=MESH,
        )

    def go(self, src, dst, to, slot):
        op = self.op(src, dst, to, slot)
        op.start()
        self.sent.append(op)

    def arrived(self, dst, to, slot):
        self.op(dst, dst, to, slot).wait_recv()


def run_together(works, tasks=()):
    live, tasks = list(works), list(tasks)
    while live or tasks:
        live = [work for work in live if next(work, "end") != "end"]
        if tasks:
            tasks.pop(0)()


def direct(links, place, axis, view, slot):
    own = place.at[axis]
    for by in (2, 1, 3):
        to = place.device(**{axis: place.shifted(axis, by)})
        links.go(view(own), view(own), to, slot + by - 1)
    yield
    for by in (1, 3, 2):
        links.arrived(view(place.shifted(axis, 4 - by)), place.sibling, slot + by - 1)


def ring(links, place, axis, view, slot, landed):
    own, right, left, across = (place.shifted(axis, by) for by in (0, 1, 3, 2))
    to_right, to_left = (place.device(**{axis: at}) for at in (right, left))
    for half in (0, 1):
        links.go(view(own, half), view(own, half), to_right, slot + half)
        links.go(view(own, 1 - half), view(own, 1 - half), to_left, slot + 2 + half)
    landed(own)
    yield
    links.arrived(view(left, 0), to_right, slot)
    links.go(view(left, 0), view(left, 0), to_right, slot + 4)
    links.arrived(view(right, 1), to_left, slot + 2)
    links.go(view(right, 1), view(right, 1), to_left, slot + 5)
    yield
    links.arrived(view(left, 1), to_right, slot + 1)
    landed(left)
    links.arrived(view(right, 0), to_left, slot + 3)
    landed(right)
    yield
    links.arrived(view(across, 0), to_right, slot + 4)
    links.arrived(view(across, 1), to_left, slot + 5)
    landed(across)


class Share:
    def __init__(self, links, place, view):
        self.links, self.place, self.view = links, place, view
        self.slot, self.due = links.slots(4), []

    def __call__(self, block):
        links, core = self.links, self.place.core
        slot = self.slot + len(self.due)
        mine = self.view(core, block)
        links.go(mine, mine, self.place.sibling, slot)
        self.due.append((self.view(1 - core, block), slot))

    def wait(self):
        for view, slot in self.due:
            self.links.arrived(view, self.place.sibling, slot)


def gather_part(links, place, ref, order):
    core = place.core
    first, second, third = order
    slot = links.slots(12)
    at = place.at
    yield from direct(
        links, place, first, lambda block: ref.at[core, at[third], at[second], block], slot
    )
    yield from direct(links, place, second, lambda block: ref.at[core, at[third], block], slot + 3)
    share = Share(links, place, lambda core, block: ref.at[core, block])

    def view(block, half=None):
        return ref.at[core, block] if half is None else ref.at[core, block, HALVES[half]]

    yield from ring(links, place, third, view, slot + 6, share)
    yield
    share.wait()


def gather_query(links, place, query_ref, then):
    core, y, z_hi = place.core, place.at["y"], place.z_hi
    slot = links.slots(7)
    links.go(query_ref.at[y, z_hi, core], query_ref.at[y, z_hi, core], place.z_far, slot)
    yield
    links.arrived(query_ref.at[y, 1 - z_hi, core], place.z_far, slot)
    share = Share(links, place, lambda core, block: query_ref.at[block, :, core])

    def view(block, half=None):
        return query_ref.at[block, FULL if half is None else half, core]

    yield from ring(links, place, "y", view, slot + 1, share)
    yield
    share.wait()
    then()


def reduce_ring(links, place, axis, pack, wire, half, fulls, slot):
    own, right, left, across = (place.shifted(axis, by) for by in (0, 1, 3, 2))
    to_right, to_left = (place.device(**{axis: at}) for at in (right, left))
    pack(across, 0)
    links.go(wire(across, 0), half.at[0], to_right, slot)
    pack(across, 1)
    links.go(wire(across, 1), half.at[1], to_left, slot + 1)
    yield
    pack(right, 1)
    links.go(wire(right, 1), fulls(0, 1), to_right, slot + 2)
    pack(left, 0)
    links.go(wire(left, 0), fulls(1, 0), to_left, slot + 3)
    yield
    links.arrived(half.at[0], to_right, slot)
    pack(right, 0, half.at[0])
    links.go(wire(right, 0), fulls(0, 0), to_right, slot + 4)
    links.arrived(half.at[1], to_left, slot + 1)
    pack(left, 1, half.at[1])
    links.go(wire(left, 1), fulls(1, 1), to_left, slot + 5)
    yield
    links.arrived(fulls(0, 1), to_right, slot + 2)
    links.arrived(fulls(1, 0), to_left, slot + 3)
    links.arrived(fulls(0, 0), to_right, slot + 4)
    links.arrived(fulls(1, 1), to_left, slot + 5)


def reduce_direct(links, place, axis, block_of, landing, slot, ready=lambda block: None):
    for by in (2, 1, 3):
        block = place.shifted(axis, by)
        ready(block)
        links.go(
            block_of(block), landing.at[by - 1], place.device(**{axis: block}), slot + by - 1
        )
    yield
    for by in (1, 3, 2):
        links.arrived(landing.at[by - 1], place.sibling, slot + by - 1)


def reduce_part(links, place, grad_ref, pair_ref, v, part, finish):
    f32, bf16 = jnp.float32, jnp.bfloat16
    rows = slice(part * 16, part * 16 + 16)
    core = place.core
    first, second, third = ORDERS[part]
    wire, half, full = (v[f"{name}1_{part}"] for name in ("wire", "half", "full"))
    slot = links.slots(12)

    def mine(block, i, j):
        at = {first: block, second: i, third: j}
        y, z, x = at["y"], at["z"], at["x"]
        return grad_ref[y, z // 2, core, lax.rem(z, 2), x, rows, :] + pair_ref[y, z, x, rows, :]

    def pack(block, side, extra=None):
        for i in range(2):
            for j in range(4):
                value = mine(block, side * 2 + i, j)
                if extra is not None:
                    value = value + extra[i, j].astype(f32)
                wire[block, side * 2 + i, j] = value.astype(bf16)

    yield from reduce_ring(
        links, place, first, pack, lambda block, side: wire.at[block, HALVES[side]], half,
        lambda way, side: full.at[way, HALVES[side]], slot,
    )
    wire2, full2 = v[f"wire2_{part}"], v[f"full2_{part}"]

    def summed(i, j):
        value = mine(place.at[first], i, j)
        return value + full[0, i, j].astype(f32) + full[1, i, j].astype(f32)

    def ready(block):
        for j in range(4):
            wire2[block, j] = summed(block, j).astype(bf16)

    yield from reduce_direct(
        links, place, second, lambda block: wire2.at[block], full2, slot + 6, ready
    )
    total3, full3 = v[f"sum3_{part}"], v[f"full3_{part}"]
    for j in range(4):
        value = summed(place.at[second], j)
        for k in range(3):
            value = value + full2[k, j].astype(f32)
        total3[j] = value
    yield from reduce_direct(links, place, third, lambda block: total3.at[block], full3, slot + 9)
    finish(total3[place.at[third]] + full3[0] + full3[1] + full3[2])


def reduce_query(links, place, first, v, out_ref):
    f32, bf16 = jnp.float32, jnp.bfloat16
    core, z_hi = place.core, place.z_hi
    grad_ref, pair_ref, wire = v["grad_query"], v["query_pair"], v["query_wire"]
    half, full, total, far_ref = v["query_half"], v["query_full"], v["query_sum"], v["query_far"]
    slot = links.slots(8)
    first()
    links.go(grad_ref.at[:, :, 1 - core], pair_ref, place.sibling, slot)
    yield
    links.arrived(pair_ref, place.sibling, slot)

    def pack(block, side, extra=None):
        value = grad_ref[block, side, core] + pair_ref[block, side]
        if extra is not None:
            value = value + extra[...].astype(f32)
        wire[block, side] = value.astype(bf16)

    yield from reduce_ring(
        links, place, "y", pack, lambda block, side: wire.at[block, side], half,
        lambda way, side: full.at[way, side], slot + 1,
    )
    own = place.at["y"]
    value = grad_ref[own, :, core] + pair_ref[own]
    total[...] = value + full[0].astype(f32) + full[1].astype(f32)
    v["query_far_out"][...] = total[1 - z_hi].astype(bf16)
    links.go(v["query_far_out"], far_ref, place.z_far, slot + 7)
    yield
    links.arrived(far_ref, place.z_far, slot + 7)
    out_ref[...] = total[z_hi] + far_ref[...].astype(f32)


def lanes_dot(left, right):
    return lax.dot_general(
        left, right, (((1,), (1,)), ((), ())), preferred_element_type=jnp.float32
    )


def rows_dot(left, right):
    return lax.dot_general(
        left, right, (((0,), (0,)), ((), ())), preferred_element_type=jnp.float32
    )


def dot(left, right):
    return jnp.dot(left, right, preferred_element_type=jnp.float32)


def step_kernel(
    cameras_hbm, text_hbm, flow_hbm, hidden_hbm, noise_hbm, clean_hbm, input_hbm, cot_hbm,
    own_prefix_hbm, own_action_hbm, own_query_hbm, sin_ref, cos_ref,
    attended_ref, out_query_ref, out_prefix_ref, out_action_ref,
    v,
):
    f32, bf16 = jnp.float32, jnp.bfloat16
    place = Place()
    core, y, z_hi, z_lo, x = place.core, place.at["y"], place.z_hi, place.z_lo, place.at["x"]
    seq = place.seq
    links = Links(v["send"], v["recv"])
    place.greet()

    norm = v["norm"]
    operands = dict(
        flow=flow_hbm, noise=noise_hbm, clean=clean_hbm, own_prefix=own_prefix_hbm,
        own_action=own_action_hbm, own_query=own_query_hbm, input=input_hbm, cot_in=cot_hbm,
        cameras=cameras_hbm, text=text_hbm,
    )
    fetches = {}
    for i, (name, ref) in enumerate(operands.items()):
        fetches[name] = pltpu.make_async_copy(ref, v[name], v["load"].at[6 + i])
        fetches[name].start()
    loads = []
    chunks = [(s, start, count) for s in range(2) for start, count in ((0, 288), (288, 288), (576, 240))]
    for k, (s, start, count) in enumerate(chunks):
        load = pltpu.make_async_copy(
            hidden_hbm.at[s, pl.ds(start, count), :],
            norm.at[pl.ds(s * KEYS + start, count), :],
            v["load"].at[k],
        )
        load.start()
        loads.append(load)

    query_weight, eye = v["query_weight"], v["eye"]
    for name in ("own_prefix", "own_action", "own_query"):
        fetches[name].wait()
    own_prefix = v["own_prefix"]
    own_action = v["own_action"][...].astype(f32)
    own_action = jnp.concatenate([own_action[:, 0:256], own_action[:, 256:512]], axis=0)
    own_parts = (own_prefix[:, 0:256], own_prefix[:, 256:512], own_action.astype(bf16))
    for part, (first, second, third) in enumerate(ORDERS):
        at = place.at
        v[f"weight_{part}"][core, at[third], at[second], at[first]] = own_parts[part]
    query_weight[y, z_hi, core] = v["own_query"][...]
    place.meet()

    packet = links.slots(16)
    def send_packets():
        for name in ("flow", "noise", "clean"):
            fetches[name].wait()
        own_noisy = v["own_noisy"]
        noisy = []
        for s in range(2):
            t = v["flow"][s]
            noisy.append(t * v["noise"][s].astype(f32) + (1.0 - t) * v["clean"][s].astype(f32))
        blank = jnp.zeros((32, PAD_STEPS - STEPS), f32)
        own_noisy[...] = jnp.concatenate([noisy[0], blank, noisy[1], blank], axis=1).astype(bf16)
        v["noisy"][seq] = own_noisy[...]
        own_time = v["own_time"]
        own_time[:, 0:512] = sin_ref[...]
        own_time[:, 512:1024] = cos_ref[...]
        v["time"][seq] = own_time[...]
        for offset in range(1, 8):
            to = (place.dp, place.group_member(offset))
            links.go(own_noisy, v["noisy"].at[seq], to, packet + offset)
            links.go(own_time, v["time"].at[seq], to, packet + 8 + offset)
        fetches["input"].wait()
        row = lax.broadcasted_iota(jnp.int32, (256, 256), 0)
        col = lax.broadcasted_iota(jnp.int32, (256, 256), 1)
        eye[...] = jnp.where(row == col, 1.0, 0.0).astype(bf16)

    act, act_t = v["act"], v["act_t"]

    def make_rows(member):
        at = pl.ds(pl.multiple_of(member * 128, 128), 128)
        wide = rows_dot(v["noisy"][member], v["input"][...])
        time = v["time"][member]
        parts = []
        for s in range(2):
            part = wide[s * PAD_STEPS : (s + 1) * PAD_STEPS] + time[s : s + 1]
            scale = lax.rsqrt(jnp.mean(part * part, axis=-1, keepdims=True) + EPS)
            parts.append((part * scale).astype(bf16))
        rows = jnp.concatenate(parts, axis=0)
        act[at, :] = rows
        for f in range(4):
            cols = slice(f * 256, (f + 1) * 256)
            act_t[cols, at] = lanes_dot(eye[...], rows[:, cols]).astype(bf16)

    def spread_rows():
        at = pl.ds(pl.multiple_of(seq * 128, 128), 128)
        feature = lax.broadcasted_iota(jnp.int32, (256, 128), 1)
        k = lax.broadcasted_iota(jnp.int32, (256, 128), 0)
        within = k % 16
        origin = (k // 16) * 8 + within
        first = jnp.where((within < 8) & (feature == origin), 1.0, 0.0).astype(bf16)
        second = jnp.where((within >= 8) & (feature == origin - 8), 1.0, 0.0).astype(bf16)
        for spread, name in ((first, "left"), (second, "right")):
            for i in range(8):
                cols, wide = slice(i * 128, (i + 1) * 128), slice(i * 256, (i + 1) * 256)
                v[name][:, wide] = lanes_dot(act[at, cols], spread).astype(bf16)
                v[name + "_t"][wide, :] = dot(spread, act_t[cols, at]).astype(bf16)

    def group_rows(low, high):
        def run():
            members = [place.group_member(offset, -1) for offset in range(low, high)]
            for offset, member in zip(range(low, high), members):
                if offset == 0:
                    continue
                to = (place.dp, member)
                links.arrived(v["noisy"].at[member], to, packet + offset)
                links.arrived(v["time"].at[member], to, packet + 8 + offset)
            for member in members:
                make_rows(member)

        return run

    def normalize(chunk):
        def run():
            loads[chunk].wait()
            s, start, count = chunks[chunk]

            def places(i):
                return [
                    pl.ds(pl.multiple_of(s * KEYS + start + i * 48 + j * 16, 16), 16)
                    for j in range(3)
                ]

            def scales(i):
                found = []
                for at in places(i):
                    wide = norm[at, :].astype(f32)
                    found.append(lax.rsqrt(jnp.mean(wide * wide, axis=-1, keepdims=True) + EPS))
                return tuple(found)

            def body(i, present):
                following = scales(jnp.minimum(i + 1, count // 48 - 1))
                for at, scale in zip(places(i), present):
                    norm[at, :] = (norm[at, :].astype(f32) * scale).astype(bf16)
                return following

            lax.fori_loop(0, count // 48, body, scales(0))

        return run

    def place_rows():
        fetches["cot_in"].wait()
        v["cot"][...] = jnp.zeros_like(v["cot"])
        for s in range(2):
            for h in range(8):
                v["cot"][h, s * PAD_STEPS : s * PAD_STEPS + STEPS, :] = v["cot_in"][
                    :, s, h * 256 : (h + 1) * 256
                ]
        for s in range(2):
            norm[s * KEYS + PREFIX : (s + 1) * KEYS, :] = jnp.zeros((KEYS - PREFIX, 2048), bf16)

    exchange = links.slots(16)

    def send_queries():
        wide = query_weight[...].reshape(1024, 256)
        for half in range(2):
            rows = slice(half * 512, (half + 1) * 512)
            value = dot(act[rows, :], wide).astype(bf16)
            v["query_out"][half * 4 : half * 4 + 4] = value.reshape(4, 128, 256)
        for offset in (2, 6, 1, 3, 5, 7, 4):
            member = place.group_member(offset)
            links.go(
                v["query_out"].at[member], v["query"].at[seq], (place.dp, member),
                exchange + offset,
            )
        v["query"][seq] = v["query_out"][seq]

    works = [gather_query(links, place, query_weight, send_queries)]
    works += [gather_part(links, place, v[f"weight_{part}"], ORDERS[part]) for part in range(3)]
    tasks = [lambda: (send_packets(), normalize(0)()), normalize(1), group_rows(0, 4), group_rows(4, 8)]
    tasks += [normalize(chunk) for chunk in range(2, 6)] + [spread_rows, place_rows]
    run_together(works, tasks)

    wp, kv = v["wp"], v["kv"]

    def block_rows(part, a, b):
        ref, order = v[f"weight_{part}"], ORDERS[part][::-1]
        pieces = []
        for c in range(2):
            for low in range(2):
                at = {"y": a, "z": b * 2 + low}
                if order[2] == "x":
                    pieces.append(ref[c, at[order[0]], at[order[1]]].reshape(64, 256))
                else:
                    for col in range(4):
                        at["x"] = col
                        pieces.append(ref[c, at[order[0]], at[order[1]], at[order[2]]])
        return pieces

    def unpack(k, carry):
        keys, values = carry
        a, b = k // 2, lax.rem(k, 2)
        for part in range(2):
            start = k * 256
            for piece in block_rows(part, a, b):
                at = pl.ds(pl.multiple_of(start, 16), piece.shape[0])
                wp[at, part * 256 : (part + 1) * 256] = piece
                start += piece.shape[0]
        block = jnp.concatenate(block_rows(2, a, b), axis=0)
        at = pl.ds(pl.multiple_of(k * 256, 256), 256)
        return keys + dot(v["left"][:, at], block), values + dot(v["right"][:, at], block)

    zero = jnp.zeros((2 * PAD_STEPS, 256), f32)
    keys, values = lax.fori_loop(0, 8, unpack, (zero, zero), unroll=4)
    keys, values = keys.astype(bf16), values.astype(bf16)

    def prefix(i, carry):
        at = pl.ds(pl.multiple_of(i * 448, 64), 448)
        kv[at, :] = dot(norm[at, :], wp[...]).astype(bf16)
        return carry

    lax.fori_loop(0, 4, prefix, 0)
    for s in range(2):
        rows = slice(s * PAD_STEPS, (s + 1) * PAD_STEPS)
        start = s * KEYS + PREFIX
        kv[start : start + PAD_STEPS, 0:256] = keys[rows]
        kv[start : start + PAD_STEPS, 256:512] = values[rows]

    low_ref, ds_ref, gkv = v["low"], v["ds"], v["gkv"]

    def sixteenth(rows):
        return (rows.astype(f32) * 0.0625).astype(bf16)

    def turn_pairs(rows, turned):
        first = lax.broadcasted_iota(jnp.int32, (256, 128), 1) < 64
        across = lanes_dot(eye[...], rows)
        for h in range(8):
            pair = across[:, (h // 2) * 128 : (h // 2 + 1) * 128]
            keep = first if h % 2 == 0 else jnp.logical_not(first)
            turned[h] = jnp.where(keep, pair, 0.0).astype(bf16)

    for s in range(2):
        cot = v["cot"][:, s * PAD_STEPS : (s + 1) * PAD_STEPS, :].reshape(512, 256)
        turn_pairs(cot, v["cot_t"].at[s])
    fetches["cameras"].wait()
    fetches["text"].wait()
    for offset in range(1, 8):
        member = place.group_member(offset, -1)
        links.arrived(v["query"].at[member], (place.dp, member), exchange + offset)

    def sample(s, carry):
        length = v["cameras"][s] * IMG + v["text"][s]
        mine = pl.ds(pl.multiple_of(s * PAD_STEPS, PAD_STEPS), PAD_STEPS)
        start = pl.multiple_of(s * KEYS, 128)
        tokens = pl.ds(start, KEYS)
        column = lax.broadcasted_iota(jnp.int32, (1, KEYS), 1)
        valid = (column < length) | ((column >= PREFIX) & (column < PREFIX + STEPS))
        bias = jnp.where(valid, 0.0, -1e30)
        query = v["query"][:, mine, :].reshape(512, 256)
        cot = v["cot"][:, mine, :].reshape(512, 256)
        logits = lanes_dot(sixteenth(query), kv[tokens, 0:256]) + bias
        expo = jnp.exp(logits - jnp.max(logits, axis=-1, keepdims=True))
        probs = expo * (1.0 / jnp.sum(expo, axis=-1, keepdims=True))
        low_ref[...] = probs.astype(bf16)
        dprob = lanes_dot(sixteenth(cot), kv[tokens, 256:512])
        inner = jnp.sum(probs * dprob, axis=-1, keepdims=True)
        ds_ref[...] = (probs * (dprob - inner)).astype(bf16)
        v["gq"][:, mine, :] = dot(ds_ref[...], kv[tokens, 0:256]).astype(bf16).reshape(8, 64, 256)
        attended = dot(low_ref[...], kv[tokens, 256:512]).astype(bf16)
        for h in range(8):
            attended_ref[s, :, h * 256 : (h + 1) * 256] = attended[h * 64 : h * 64 + STEPS]
        turn_pairs(query, v["query_t"])

        def tile(begin, width):
            at = pl.ds(begin, width)
            to = pl.ds(pl.multiple_of(start + begin, 128), width)
            for left, right, top in ((v["query_t"], ds_ref, 0), (v["cot_t"].at[s], low_ref, 256)):
                total = jnp.zeros((256, width), f32)
                for h in range(8):
                    term = dot(left[h], right[(h // 2) * 128 : (h // 2 + 1) * 128, at])
                    total = total + term.astype(bf16).astype(f32)
                gkv[top : top + 256, to] = total.astype(bf16)

        def wide_tile(t, carry):
            tile(pl.multiple_of(t * 256, 256), 256)
            return carry

        lax.fori_loop(0, 3, wide_tile, 0, unroll=3)
        tile(768, 128)
        return carry

    lax.fori_loop(0, 2, sample, 0)

    for offset in (2, 6, 1, 3, 5, 7, 4):
        member = place.group_member(offset)
        links.go(
            v["gq"].at[member], v["group_gq"].at[seq], (place.dp, member), exchange + 8 + offset
        )
    v["group_gq"][seq] = v["gq"][seq]

    for s in range(2):
        turned = gkv[:, s * KEYS + PREFIX - 48 : (s + 1) * KEYS].astype(f32).T[48 : 48 + PAD_STEPS]
        ds_ref[s * 64 : (s + 1) * 64, 0:512] = turned.astype(bf16)
    grad, pair = v["grad"], v["pair"]
    pairing = links.slots(8)

    def pair_op(k):
        a, b = k // 2, lax.rem(k, 2)
        return links.op(
            grad.at[a, b, 1 - core], pair.at[a, pl.ds(b * 2, 2)], place.sibling, pairing + k
        )

    def multiply(k):
        at = pl.ds(pl.multiple_of(k * 256, 256), 256)
        v["product"][lax.rem(k, 2)] = dot(gkv[...], norm[:, at])

    def deliver(k):
        at = pl.ds(pl.multiple_of(k * 256, 256), 256)
        a, b = lax.div(k, 2), lax.rem(k, 2)
        value = v["product"][b]
        high = value.astype(bf16)
        low = (value - high.astype(f32)).astype(bf16)
        value = lanes_dot(eye[...], high) + lanes_dot(eye[...], low)
        grad[a, b, :, :, :, 0:16, :] = value[:, 0:256].reshape(2, 2, 4, 16, 256)
        grad[a, b, :, :, :, 16:32, :] = value[:, 256:512].reshape(2, 2, 4, 16, 256)
        action = dot(v["left_t"][at, :], ds_ref[0:128, 0:256])
        action += dot(v["right_t"][at, :], ds_ref[0:128, 256:512])
        grad[a, b, :, :, :, 32:48, :] = action.reshape(2, 2, 4, 16, 256)
        pair_op(k).start()

    def grad_prefix(k, carry):
        deliver(k - 1)
        multiply(k)
        return carry

    multiply(0)
    lax.fori_loop(1, 8, grad_prefix, 0)
    deliver(7)

    def grad_query():
        for offset in range(1, 8):
            member = place.group_member(offset, -1)
            links.arrived(v["group_gq"].at[member], (place.dp, member), exchange + 8 + offset)
        rows = v["group_gq"][...].reshape(1024, 256)
        for a in range(4):
            value = dot(act_t[a * 256 : (a + 1) * 256, :], rows)
            v["grad_query"][a] = value.reshape(2, 2, 64, 256)

    def finish(part):
        def store(value):
            if part == 2:
                out_action_ref[:, 0:256] = value[0:8]
                out_action_ref[:, 256:512] = value[8:16]
            else:
                out_prefix_ref[:, part * 256 : (part + 1) * 256] = value

        return store

    def paired():
        for k in range(8):
            pair_op(k).wait_recv()
        yield

    query_work = reduce_query(links, place, grad_query, v, out_query_ref)
    works = [query_work, paired()]
    works += [reduce_part(links, place, grad, pair, v, part, finish(part)) for part in range(3)]
    early = list(links.sent)
    links.sent.clear()

    def drain(ops):
        def run():
            for op in ops:
                op.wait_send()

        return run

    run_together(works, [drain(early[i::4]) for i in range(4)])
    for op in links.sent:
        op.wait_send()
    for k in range(8):
        pair_op(k).wait_send()


def step(
    cameras, text_length, flow_time, hidden, noise, clean, input_weight, cot,
    own_prefix, own_action, own_query, sine, cosine,
):
    bf16, f32 = jnp.bfloat16, jnp.float32
    hbm, vmem = pl.BlockSpec(memory_space=pltpu.HBM), pl.BlockSpec(memory_space=pltpu.VMEM)
    scratch = dict(
        norm=pltpu.VMEM((2 * KEYS, 2048), bf16),
        own_noisy=pltpu.VMEM((32, 128), bf16),
        query_weight=pltpu.VMEM((4, 2, 2, 64, 256), bf16),
        noisy=pltpu.VMEM((8, 32, 128), bf16),
        time=pltpu.VMEM((8, 2, 1024), f32),
        own_time=pltpu.VMEM((2, 1024), f32),
        act=pltpu.VMEM((1024, 1024), bf16),
        act_t=pltpu.VMEM((1024, 1024), bf16),
        left=pltpu.VMEM((128, 2048), bf16),
        right=pltpu.VMEM((128, 2048), bf16),
        cot=pltpu.VMEM((8, 128, 256), bf16),
        eye=pltpu.VMEM((256, 256), bf16),
        left_t=pltpu.VMEM((2048, 128), bf16),
        right_t=pltpu.VMEM((2048, 128), bf16),
        query=pltpu.VMEM((8, 128, 256), bf16),
        query_out=pltpu.VMEM((8, 128, 256), bf16),
        gq=pltpu.VMEM((8, 128, 256), bf16),
        group_gq=pltpu.VMEM((8, 128, 256), bf16),
        wp=pltpu.VMEM((2048, 512), bf16),
        kv=pltpu.VMEM((2 * KEYS, 512), bf16),
        low=pltpu.VMEM((512, KEYS), bf16),
        ds=pltpu.VMEM((512, KEYS), bf16),
        query_t=pltpu.VMEM((8, 256, 128), bf16),
        cot_t=pltpu.VMEM((2, 8, 256, 128), bf16),
        gkv=pltpu.VMEM((512, 2 * KEYS), bf16),
        grad=pltpu.VMEM((4, 2, 2, 2, 4, ROWS, 256), f32),
        pair=pltpu.VMEM((4, 4, 4, ROWS, 256), f32),
        product=pltpu.VMEM((2, 512, 256), f32),
        grad_query=pltpu.VMEM((4, 2, 2, 64, 256), f32),
        query_pair=pltpu.VMEM((4, 2, 64, 256), f32),
        query_wire=pltpu.VMEM((4, 2, 64, 256), bf16),
        query_half=pltpu.VMEM((2, 64, 256), bf16),
        query_full=pltpu.VMEM((2, 2, 64, 256), bf16),
        query_sum=pltpu.VMEM((2, 64, 256), f32),
        query_far=pltpu.VMEM((64, 256), bf16),
        query_far_out=pltpu.VMEM((64, 256), bf16),
        send=pltpu.SemaphoreType.DMA((192,)),
        recv=pltpu.SemaphoreType.DMA((192,)),
        load=pltpu.SemaphoreType.DMA((16,)),
        flow=pltpu.SMEM((2,), f32),
        cameras=pltpu.SMEM((2,), jnp.int32),
        text=pltpu.SMEM((2,), jnp.int32),
        noise=pltpu.VMEM((2, 32, STEPS), bf16),
        clean=pltpu.VMEM((2, 32, STEPS), bf16),
        input=pltpu.VMEM((32, 1024), bf16),
        cot_in=pltpu.VMEM((STEPS, 2, 2048), bf16),
        own_prefix=pltpu.VMEM((16, 512), bf16),
        own_action=pltpu.VMEM((8, 512), bf16),
        own_query=pltpu.VMEM((64, 256), bf16),
    )
    for part in range(3):
        scratch[f"weight_{part}"] = pltpu.VMEM((2, 4, 4, 4, 16, 256), bf16)
        scratch[f"wire1_{part}"] = pltpu.VMEM((4, 4, 4, 16, 256), bf16)
        scratch[f"half1_{part}"] = pltpu.VMEM((2, 2, 4, 16, 256), bf16)
        scratch[f"full1_{part}"] = pltpu.VMEM((2, 4, 4, 16, 256), bf16)
        scratch[f"wire2_{part}"] = pltpu.VMEM((4, 4, 16, 256), bf16)
        scratch[f"full2_{part}"] = pltpu.VMEM((3, 4, 16, 256), bf16)
        scratch[f"sum3_{part}"] = pltpu.VMEM((4, 16, 256), f32)
        scratch[f"full3_{part}"] = pltpu.VMEM((3, 16, 256), f32)
    return pl.pallas_call(
        step_kernel,
        out_shape=(
            jax.ShapeDtypeStruct((2, STEPS, 2048), bf16),
            jax.ShapeDtypeStruct((64, 256), f32),
            jax.ShapeDtypeStruct((16, 512), f32),
            jax.ShapeDtypeStruct((8, 512), f32),
        ),
        in_specs=[hbm] * 11 + [vmem] * 2,
        out_specs=(vmem,) * 4,
        scratch_shapes=[scratch],
        compiler_params=pltpu.CompilerParams(
            collective_id=1, has_side_effects=True, vmem_limit_bytes=VMEM_LIMIT
        ),
        cost_estimate=pl.CostEstimate(
            flops=10**10, bytes_accessed=9 * 10**6, transcendentals=10**6
        ),
        name="step",
    )(
        *[
            pltpu.with_memory_space_constraint(operand, pltpu.HBM)
            for operand in (
                cameras, text_length, flow_time, hidden, noise, clean, input_weight, cot,
                own_prefix, own_action, own_query,
            )
        ],
        sine,
        cosine,
    )


def time_feature(flow_col, row_width):
    half_width = row_width // 2
    fraction = jnp.arange(half_width, dtype=jnp.float32) / (half_width - 1)
    period = 0.004 * 1000.0**fraction
    angle = flow_col[..., None] * (2.0 * math.pi / period)
    return jnp.sin(angle), jnp.cos(angle)


def on_device(
    prefix_hidden,
    cameras,
    text_length,
    action_noise,
    clean_actions,
    flow_time,
    input_weight,
    prefix_kv_weight,
    action_kv_weight,
    query_weight,
    cotangent,
):
    sine, cosine = time_feature(flow_time, 1024)
    return step(
        cameras,
        text_length,
        flow_time,
        prefix_hidden,
        action_noise.transpose(0, 2, 1),
        clean_actions.transpose(0, 2, 1),
        input_weight,
        cotangent.transpose(1, 0, 2),
        prefix_kv_weight,
        action_kv_weight,
        query_weight,
        sine,
        cosine,
    )


def solution(mesh):
    return jax.shard_map(
        on_device,
        mesh=mesh,
        in_specs=(
            P(("dp", "seq"), None, None),
            P(("dp", "seq")),
            P(("dp", "seq")),
            P(("dp", "seq"), None, None),
            P(("dp", "seq"), None, None),
            P(("dp", "seq")),
            P(),
            P(("dp", "seq"), None),
            P(("dp", "seq"), None),
            P("dp", "seq"),
            P(("dp", "seq"), None, None),
        ),
        out_specs=(
            P(("dp", "seq"), None, None),
            P("dp", "seq"),
            P(("dp", "seq"), None),
            P(("dp", "seq"), None),
        ),
        check_vma=False,
    )
```

```python
import math

import jax
import jax.numpy as jnp
from jax import lax
from jax.experimental import pallas as pl
from jax.experimental.pallas import tpu as pltpu
from jax.sharding import PartitionSpec as P

IMG = 256
EPS = 1e-06
MESH = pl.DeviceIdType.MESH
VMEM_LIMIT = 52 * 1024 * 1024
PREFIX, STEPS, PAD_STEPS, KEYS = 816, 50, 64, 896

ROWS = 48
ORDERS = ("xyz", "yzx", "zxy")
HALVES = (slice(0, 2), slice(2, 4))
FULL = slice(None)


class Place:
    def __init__(self):
        self.dp = lax.axis_index("dp")
        self.seq = lax.axis_index("seq")
        self.core = lax.rem(self.dp, 2)
        self.z_hi = lax.rem(self.dp // 2, 2)
        self.z_lo = self.seq // 4
        self.at = {
            "y": self.dp // 4,
            "z": self.z_hi * 2 + self.z_lo,
            "x": lax.rem(self.seq, 4),
        }
        self.sibling = self.device(core=1 - self.core)
        self.z_far = self.device(z=self.shifted("z", 2))

    def device(self, core=None, **moved):
        at = {**self.at, **moved}
        core = self.core if core is None else core
        return (
            at["y"] * 4 + (at["z"] // 2) * 2 + core,
            lax.rem(at["z"], 2) * 4 + at["x"],
        )

    def shifted(self, axis, by):
        return lax.rem(self.at[axis] + by, 4)

    def group_member(self, offset, sign=1):
        z_lo = lax.rem(self.z_lo + lax.div(offset, 4), 2)
        x = lax.rem(self.at["x"] + sign * lax.rem(offset, 4) + 4, 4)
        return z_lo * 4 + x

    def greet(self):
        barrier = pltpu.get_barrier_semaphore()
        others = [self.sibling, self.z_far]
        others += [(self.dp, self.group_member(offset)) for offset in range(1, 8)]
        others += [self.device(y=self.shifted("y", by)) for by in (1, 2, 3)]
        beyond = lax.rem(self.at["z"] + 3 + 2 * self.z_lo, 4)
        others.append(self.device(z=beyond))
        for other in others:
            pl.semaphore_signal(barrier, inc=1, device_id=other, device_id_type=MESH)
        self.greeted = len(others)

    def meet(self):
        pl.semaphore_wait(pltpu.get_barrier_semaphore(), self.greeted)


class Links:
    def __init__(self, send_sem, recv_sem):
        self.send_sem, self.recv_sem = send_sem, recv_sem
        self.used = 0
        self.sent = []

    def slots(self, count):
        self.used += count
        return self.used - count

    def op(self, src, dst, to, slot):
        return pltpu.make_async_remote_copy(
            src_ref=src,
            dst_ref=dst,
            send_sem=self.send_sem.at[slot],
            recv_sem=self.recv_sem.at[slot],
            device_id=to,
            device_id_type=MESH,
        )

    def go(self, src, dst, to, slot):
        op = self.op(src, dst, to, slot)
        op.start()
        self.sent.append(op)

    def arrived(self, dst, to, slot):
        self.op(dst, dst, to, slot).wait_recv()


def run_together(works, tasks=()):
    live, tasks = list(works), list(tasks)
    while live or tasks:
        live = [work for work in live if next(work, "end") != "end"]
        if tasks:
            tasks.pop(0)()


def direct(links, place, axis, view, slot):
    own = place.at[axis]
    for by in (2, 1, 3):
        to = place.device(**{axis: place.shifted(axis, by)})
        links.go(view(own), view(own), to, slot + by - 1)
    yield
    for by in (1, 3, 2):
        links.arrived(view(place.shifted(axis, 4 - by)), place.sibling, slot + by - 1)


def ring(links, place, axis, view, slot, landed):
    own, right, left, across = (place.shifted(axis, by) for by in (0, 1, 3, 2))
    to_right, to_left = (place.device(**{axis: at}) for at in (right, left))
    for half in (0, 1):
        links.go(view(own, half), view(own, half), to_right, slot + half)
        links.go(view(own, 1 - half), view(own, 1 - half), to_left, slot + 2 + half)
    landed(own)
    yield
    links.arrived(view(left, 0), to_right, slot)
    links.go(view(left, 0), view(left, 0), to_right, slot + 4)
    links.arrived(view(right, 1), to_left, slot + 2)
    links.go(view(right, 1), view(right, 1), to_left, slot + 5)
    yield
    links.arrived(view(left, 1), to_right, slot + 1)
    landed(left)
    links.arrived(view(right, 0), to_left, slot + 3)
    landed(right)
    yield
    links.arrived(view(across, 0), to_right, slot + 4)
    links.arrived(view(across, 1), to_left, slot + 5)
    landed(across)


class Share:
    def __init__(self, links, place, view):
        self.links, self.place, self.view = links, place, view
        self.slot, self.due = links.slots(4), []

    def __call__(self, block):
        links, core = self.links, self.place.core
        slot = self.slot + len(self.due)
        mine = self.view(core, block)
        links.go(mine, mine, self.place.sibling, slot)
        self.due.append((self.view(1 - core, block), slot))

    def wait(self):
        for view, slot in self.due:
            self.links.arrived(view, self.place.sibling, slot)


def gather_part(links, place, ref, order):
    core = place.core
    first, second, third = order
    slot = links.slots(12)
    at = place.at
    yield from direct(
        links, place, first, lambda block: ref.at[core, at[third], at[second], block], slot
    )
    yield from direct(links, place, second, lambda block: ref.at[core, at[third], block], slot + 3)
    share = Share(links, place, lambda core, block: ref.at[core, block])

    def view(block, half=None):
        return ref.at[core, block] if half is None else ref.at[core, block, HALVES[half]]

    yield from ring(links, place, third, view, slot + 6, share)
    yield
    share.wait()


def gather_query(links, place, query_ref, then):
    core, y, z_hi = place.core, place.at["y"], place.z_hi
    slot = links.slots(7)
    links.go(query_ref.at[y, z_hi, core], query_ref.at[y, z_hi, core], place.z_far, slot)
    yield
    links.arrived(query_ref.at[y, 1 - z_hi, core], place.z_far, slot)
    share = Share(links, place, lambda core, block: query_ref.at[block, :, core])

    def view(block, half=None):
        return query_ref.at[block, FULL if half is None else half, core]

    yield from ring(links, place, "y", view, slot + 1, share)
    yield
    share.wait()
    then()


def reduce_ring(links, place, axis, pack, wire, half, fulls, slot):
    own, right, left, across = (place.shifted(axis, by) for by in (0, 1, 3, 2))
    to_right, to_left = (place.device(**{axis: at}) for at in (right, left))
    pack(across, 0)
    links.go(wire(across, 0), half.at[0], to_right, slot)
    pack(across, 1)
    links.go(wire(across, 1), half.at[1], to_left, slot + 1)
    yield
    pack(right, 1)
    links.go(wire(right, 1), fulls(0, 1), to_right, slot + 2)
    pack(left, 0)
    links.go(wire(left, 0), fulls(1, 0), to_left, slot + 3)
    yield
    links.arrived(half.at[0], to_right, slot)
    pack(right, 0, half.at[0])
    links.go(wire(right, 0), fulls(0, 0), to_right, slot + 4)
    links.arrived(half.at[1], to_left, slot + 1)
    pack(left, 1, half.at[1])
    links.go(wire(left, 1), fulls(1, 1), to_left, slot + 5)
    yield
    links.arrived(fulls(0, 1), to_right, slot + 2)
    links.arrived(fulls(1, 0), to_left, slot + 3)
    links.arrived(fulls(0, 0), to_right, slot + 4)
    links.arrived(fulls(1, 1), to_left, slot + 5)


def reduce_direct(links, place, axis, block_of, landing, slot, ready=lambda block: None):
    for by in (2, 1, 3):
        block = place.shifted(axis, by)
        ready(block)
        links.go(
            block_of(block), landing.at[by - 1], place.device(**{axis: block}), slot + by - 1
        )
    yield
    for by in (1, 3, 2):
        links.arrived(landing.at[by - 1], place.sibling, slot + by - 1)


def reduce_part(links, place, grad_ref, pair_ref, v, part, finish):
    f32, bf16 = jnp.float32, jnp.bfloat16
    rows = slice(part * 16, part * 16 + 16)
    core = place.core
    first, second, third = ORDERS[part]
    wire, half, full = (v[f"{name}1_{part}"] for name in ("wire", "half", "full"))
    slot = links.slots(12)

    def mine(block, i, j):
        at = {first: block, second: i, third: j}
        y, z, x = at["y"], at["z"], at["x"]
        return grad_ref[y, z // 2, core, lax.rem(z, 2), x, rows, :] + pair_ref[y, z, x, rows, :]

    def pack(block, side, extra=None):
        for i in range(2):
            for j in range(4):
                value = mine(block, side * 2 + i, j)
                if extra is not None:
                    value = value + extra[i, j].astype(f32)
                wire[block, side * 2 + i, j] = value.astype(bf16)

    yield from reduce_ring(
        links, place, first, pack, lambda block, side: wire.at[block, HALVES[side]], half,
        lambda way, side: full.at[way, HALVES[side]], slot,
    )
    wire2, full2 = v[f"wire2_{part}"], v[f"full2_{part}"]

    def summed(i, j):
        value = mine(place.at[first], i, j)
        return value + full[0, i, j].astype(f32) + full[1, i, j].astype(f32)

    def ready(block):
        for j in range(4):
            wire2[block, j] = summed(block, j).astype(bf16)

    yield from reduce_direct(
        links, place, second, lambda block: wire2.at[block], full2, slot + 6, ready
    )
    total3, full3 = v[f"sum3_{part}"], v[f"full3_{part}"]
    for j in range(4):
        value = summed(place.at[second], j)
        for k in range(3):
            value = value + full2[k, j].astype(f32)
        total3[j] = value
    yield from reduce_direct(links, place, third, lambda block: total3.at[block], full3, slot + 9)
    finish(total3[place.at[third]] + full3[0] + full3[1] + full3[2])


def reduce_query(links, place, first, v, out_ref):
    f32, bf16 = jnp.float32, jnp.bfloat16
    core, z_hi = place.core, place.z_hi
    grad_ref, pair_ref, wire = v["grad_query"], v["query_pair"], v["query_wire"]
    half, full, total, far_ref = v["query_half"], v["query_full"], v["query_sum"], v["query_far"]
    slot = links.slots(8)
    first()
    links.go(grad_ref.at[:, :, 1 - core], pair_ref, place.sibling, slot)
    yield
    links.arrived(pair_ref, place.sibling, slot)

    def pack(block, side, extra=None):
        value = grad_ref[block, side, core] + pair_ref[block, side]
        if extra is not None:
            value = value + extra[...].astype(f32)
        wire[block, side] = value.astype(bf16)

    yield from reduce_ring(
        links, place, "y", pack, lambda block, side: wire.at[block, side], half,
        lambda way, side: full.at[way, side], slot + 1,
    )
    own = place.at["y"]
    value = grad_ref[own, :, core] + pair_ref[own]
    total[...] = value + full[0].astype(f32) + full[1].astype(f32)
    v["query_far_out"][...] = total[1 - z_hi].astype(bf16)
    links.go(v["query_far_out"], far_ref, place.z_far, slot + 7)
    yield
    links.arrived(far_ref, place.z_far, slot + 7)
    out_ref[...] = total[z_hi] + far_ref[...].astype(f32)


def lanes_dot(left, right):
    return lax.dot_general(
        left, right, (((1,), (1,)), ((), ())), preferred_element_type=jnp.float32
    )


def rows_dot(left, right):
    return lax.dot_general(
        left, right, (((0,), (0,)), ((), ())), preferred_element_type=jnp.float32
    )


def dot(left, right):
    return jnp.dot(left, right, preferred_element_type=jnp.float32)


def step_kernel(
    cameras_hbm, text_hbm, flow_hbm, hidden_hbm, noise_hbm, clean_hbm, input_hbm, cot_hbm,
    own_prefix_hbm, own_action_hbm, own_query_hbm, sin_ref, cos_ref,
    attended_ref, out_query_ref, out_prefix_ref, out_action_ref,
    v,
):
    f32, bf16 = jnp.float32, jnp.bfloat16
    place = Place()
    core, y, z_hi, z_lo, x = place.core, place.at["y"], place.z_hi, place.z_lo, place.at["x"]
    seq = place.seq
    links = Links(v["send"], v["recv"])
    place.greet()

    norm = v["norm"]
    operands = dict(
        flow=flow_hbm, noise=noise_hbm, clean=clean_hbm, own_prefix=own_prefix_hbm,
        own_action=own_action_hbm, own_query=own_query_hbm, input=input_hbm, cot_in=cot_hbm,
        cameras=cameras_hbm, text=text_hbm,
    )
    fetches = {}
    for i, (name, ref) in enumerate(operands.items()):
        fetches[name] = pltpu.make_async_copy(ref, v[name], v["load"].at[6 + i])
        fetches[name].start()
    loads = []
    chunks = [(s, start, count) for s in range(2) for start, count in ((0, 288), (288, 288), (576, 240))]
    for k, (s, start, count) in enumerate(chunks):
        load = pltpu.make_async_copy(
            hidden_hbm.at[s, pl.ds(start, count), :],
            norm.at[pl.ds(s * KEYS + start, count), :],
            v["load"].at[k],
        )
        load.start()
        loads.append(load)

    query_weight, eye = v["query_weight"], v["eye"]
    for name in ("own_prefix", "own_action", "own_query"):
        fetches[name].wait()
    own_prefix = v["own_prefix"]
    own_action = v["own_action"][...].astype(f32)
    own_action = jnp.concatenate([own_action[:, 0:256], own_action[:, 256:512]], axis=0)
    own_parts = (own_prefix[:, 0:256], own_prefix[:, 256:512], own_action.astype(bf16))
    for part, (first, second, third) in enumerate(ORDERS):
        at = place.at
        v[f"weight_{part}"][core, at[third], at[second], at[first]] = own_parts[part]
    query_weight[y, z_hi, core] = v["own_query"][...]
    place.meet()

    packet = links.slots(16)
    def send_packets():
        for name in ("flow", "noise", "clean"):
            fetches[name].wait()
        own_noisy = v["own_noisy"]
        noisy = []
        for s in range(2):
            t = v["flow"][s]
            noisy.append(t * v["noise"][s].astype(f32) + (1.0 - t) * v["clean"][s].astype(f32))
        blank = jnp.zeros((32, PAD_STEPS - STEPS), f32)
        own_noisy[...] = jnp.concatenate([noisy[0], blank, noisy[1], blank], axis=1).astype(bf16)
        v["noisy"][seq] = own_noisy[...]
        own_time = v["own_time"]
        own_time[:, 0:512] = sin_ref[...]
        own_time[:, 512:1024] = cos_ref[...]
        v["time"][seq] = own_time[...]
        for offset in range(1, 8):
            to = (place.dp, place.group_member(offset))
            links.go(own_noisy, v["noisy"].at[seq], to, packet + offset)
            links.go(own_time, v["time"].at[seq], to, packet + 8 + offset)
        fetches["input"].wait()
        row = lax.broadcasted_iota(jnp.int32, (256, 256), 0)
        col = lax.broadcasted_iota(jnp.int32, (256, 256), 1)
        eye[...] = jnp.where(row == col, 1.0, 0.0).astype(bf16)

    act, act_t = v["act"], v["act_t"]

    def make_rows(member):
        at = pl.ds(pl.multiple_of(member * 128, 128), 128)
        wide = rows_dot(v["noisy"][member], v["input"][...])
        time = v["time"][member]
        parts = []
        for s in range(2):
            part = wide[s * PAD_STEPS : (s + 1) * PAD_STEPS] + time[s : s + 1]
            scale = lax.rsqrt(jnp.mean(part * part, axis=-1, keepdims=True) + EPS)
            parts.append((part * scale).astype(bf16))
        rows = jnp.concatenate(parts, axis=0)
        act[at, :] = rows
        for f in range(4):
            cols = slice(f * 256, (f + 1) * 256)
            act_t[cols, at] = lanes_dot(eye[...], rows[:, cols]).astype(bf16)

    def spread_rows():
        at = pl.ds(pl.multiple_of(seq * 128, 128), 128)
        feature = lax.broadcasted_iota(jnp.int32, (256, 128), 1)
        k = lax.broadcasted_iota(jnp.int32, (256, 128), 0)
        within = k % 16
        origin = (k // 16) * 8 + within
        first = jnp.where((within < 8) & (feature == origin), 1.0, 0.0).astype(bf16)
        second = jnp.where((within >= 8) & (feature == origin - 8), 1.0, 0.0).astype(bf16)
        for spread, name in ((first, "left"), (second, "right")):
            for i in range(8):
                cols, wide = slice(i * 128, (i + 1) * 128), slice(i * 256, (i + 1) * 256)
                v[name][:, wide] = lanes_dot(act[at, cols], spread).astype(bf16)
                v[name + "_t"][wide, :] = dot(spread, act_t[cols, at]).astype(bf16)

    def group_rows(low, high):
        def run():
            members = [place.group_member(offset, -1) for offset in range(low, high)]
            for offset, member in zip(range(low, high), members):
                if offset == 0:
                    continue
                to = (place.dp, member)
                links.arrived(v["noisy"].at[member], to, packet + offset)
                links.arrived(v["time"].at[member], to, packet + 8 + offset)
            for member in members:
                make_rows(member)

        return run

    def normalize(chunk):
        def run():
            loads[chunk].wait()
            s, start, count = chunks[chunk]

            def places(i):
                return [
                    pl.ds(pl.multiple_of(s * KEYS + start + i * 48 + j * 16, 16), 16)
                    for j in range(3)
                ]

            def scales(i):
                found = []
                for at in places(i):
                    wide = norm[at, :].astype(f32)
                    found.append(lax.rsqrt(jnp.mean(wide * wide, axis=-1, keepdims=True) + EPS))
                return tuple(found)

            def body(i, present):
                following = scales(jnp.minimum(i + 1, count // 48 - 1))
                for at, scale in zip(places(i), present):
                    norm[at, :] = (norm[at, :].astype(f32) * scale).astype(bf16)
                return following

            lax.fori_loop(0, count // 48, body, scales(0))

        return run

    def place_rows():
        fetches["cot_in"].wait()
        v["cot"][...] = jnp.zeros_like(v["cot"])
        for s in range(2):
            for h in range(8):
                v["cot"][h, s * PAD_STEPS : s * PAD_STEPS + STEPS, :] = v["cot_in"][
                    :, s, h * 256 : (h + 1) * 256
                ]
        for s in range(2):
            norm[s * KEYS + PREFIX : (s + 1) * KEYS, :] = jnp.zeros((KEYS - PREFIX, 2048), bf16)

    exchange = links.slots(16)

    def send_queries():
        wide = query_weight[...].reshape(1024, 256)
        for half in range(2):
            rows = slice(half * 512, (half + 1) * 512)
            value = dot(act[rows, :], wide).astype(bf16)
            v["query_out"][half * 4 : half * 4 + 4] = value.reshape(4, 128, 256)
        for offset in (2, 6, 1, 3, 5, 7, 4):
            member = place.group_member(offset)
            links.go(
                v["query_out"].at[member], v["query"].at[seq], (place.dp, member),
                exchange + offset,
            )
        v["query"][seq] = v["query_out"][seq]

    works = [gather_query(links, place, query_weight, send_queries)]
    works += [gather_part(links, place, v[f"weight_{part}"], ORDERS[part]) for part in range(3)]
    tasks = [lambda: (send_packets(), normalize(0)()), normalize(1), group_rows(0, 4), group_rows(4, 8)]
    tasks += [normalize(chunk) for chunk in range(2, 6)] + [spread_rows, place_rows]
    run_together(works, tasks)

    wp, kv = v["wp"], v["kv"]

    def block_rows(part, a, b):
        ref, order = v[f"weight_{part}"], ORDERS[part][::-1]
        pieces = []
        for c in range(2):
            for low in range(2):
                at = {"y": a, "z": b * 2 + low}
                if order[2] == "x":
                    pieces.append(ref[c, at[order[0]], at[order[1]]].reshape(64, 256))
                else:
                    for col in range(4):
                        at["x"] = col
                        pieces.append(ref[c, at[order[0]], at[order[1]], at[order[2]]])
        return pieces

    def unpack(k, carry):
        keys, values = carry
        a, b = k // 2, lax.rem(k, 2)
        for part in range(2):
            start = k * 256
            for piece in block_rows(part, a, b):
                at = pl.ds(pl.multiple_of(start, 16), piece.shape[0])
                wp[at, part * 256 : (part + 1) * 256] = piece
                start += piece.shape[0]
        block = jnp.concatenate(block_rows(2, a, b), axis=0)
        at = pl.ds(pl.multiple_of(k * 256, 256), 256)
        return keys + dot(v["left"][:, at], block), values + dot(v["right"][:, at], block)

    zero = jnp.zeros((2 * PAD_STEPS, 256), f32)
    keys, values = lax.fori_loop(0, 8, unpack, (zero, zero), unroll=4)
    keys, values = keys.astype(bf16), values.astype(bf16)

    def prefix(i, carry):
        at = pl.ds(pl.multiple_of(i * 448, 64), 448)
        kv[at, :] = dot(norm[at, :], wp[...]).astype(bf16)
        return carry

    lax.fori_loop(0, 4, prefix, 0, unroll=2)
    for s in range(2):
        rows = slice(s * PAD_STEPS, (s + 1) * PAD_STEPS)
        start = s * KEYS + PREFIX
        kv[start : start + PAD_STEPS, 0:256] = keys[rows]
        kv[start : start + PAD_STEPS, 256:512] = values[rows]

    low_ref, ds_ref, gkv = v["low"], v["ds"], v["gkv"]

    def sixteenth(rows):
        return (rows.astype(f32) * 0.0625).astype(bf16)

    def turn_pairs(rows, turned):
        first = lax.broadcasted_iota(jnp.int32, (256, 128), 1) < 64
        across = lanes_dot(eye[...], rows)
        for h in range(8):
            pair = across[:, (h // 2) * 128 : (h // 2 + 1) * 128]
            keep = first if h % 2 == 0 else jnp.logical_not(first)
            turned[h] = jnp.where(keep, pair, 0.0).astype(bf16)

    for s in range(2):
        cot = v["cot"][:, s * PAD_STEPS : (s + 1) * PAD_STEPS, :].reshape(512, 256)
        turn_pairs(cot, v["cot_t"].at[s])
    fetches["cameras"].wait()
    fetches["text"].wait()
    for offset in range(1, 8):
        member = place.group_member(offset, -1)
        links.arrived(v["query"].at[member], (place.dp, member), exchange + offset)

    def sample(s, carry):
        length = v["cameras"][s] * IMG + v["text"][s]
        mine = pl.ds(pl.multiple_of(s * PAD_STEPS, PAD_STEPS), PAD_STEPS)
        start = pl.multiple_of(s * KEYS, 128)
        tokens = pl.ds(start, KEYS)
        column = lax.broadcasted_iota(jnp.int32, (1, KEYS), 1)
        valid = (column < length) | ((column >= PREFIX) & (column < PREFIX + STEPS))
        bias = jnp.where(valid, 0.0, -1e30)
        query = v["query"][:, mine, :].reshape(512, 256)
        cot = v["cot"][:, mine, :].reshape(512, 256)
        logits = lanes_dot(sixteenth(query), kv[tokens, 0:256]) + bias
        expo = jnp.exp(logits - jnp.max(logits, axis=-1, keepdims=True))
        probs = expo * (1.0 / jnp.sum(expo, axis=-1, keepdims=True))
        low_ref[...] = probs.astype(bf16)
        dprob = lanes_dot(sixteenth(cot), kv[tokens, 256:512])
        inner = jnp.sum(probs * dprob, axis=-1, keepdims=True)
        ds_ref[...] = (probs * (dprob - inner)).astype(bf16)
        v["gq"][:, mine, :] = dot(ds_ref[...], kv[tokens, 0:256]).astype(bf16).reshape(8, 64, 256)
        attended = dot(low_ref[...], kv[tokens, 256:512]).astype(bf16)
        for h in range(8):
            attended_ref[s, :, h * 256 : (h + 1) * 256] = attended[h * 64 : h * 64 + STEPS]
        turn_pairs(query, v["query_t"])

        def tile(begin, width):
            at = pl.ds(begin, width)
            to = pl.ds(pl.multiple_of(start + begin, 128), width)
            for left, right, top in ((v["query_t"], ds_ref, 0), (v["cot_t"].at[s], low_ref, 256)):
                total = jnp.zeros((256, width), f32)
                for h in range(8):
                    term = dot(left[h], right[(h // 2) * 128 : (h // 2 + 1) * 128, at])
                    total = total + term.astype(bf16).astype(f32)
                gkv[top : top + 256, to] = total.astype(bf16)

        def wide_tile(t, carry):
            tile(pl.multiple_of(t * 256, 256), 256)
            return carry

        lax.fori_loop(0, 3, wide_tile, 0, unroll=3)
        tile(768, 128)
        return carry

    lax.fori_loop(0, 2, sample, 0, unroll=2)

    for offset in (2, 6, 1, 3, 5, 7, 4):
        member = place.group_member(offset)
        links.go(
            v["gq"].at[member], v["group_gq"].at[seq], (place.dp, member), exchange + 8 + offset
        )
    v["group_gq"][seq] = v["gq"][seq]

    for s in range(2):
        turned = gkv[:, s * KEYS + PREFIX - 48 : (s + 1) * KEYS].astype(f32).T[48 : 48 + PAD_STEPS]
        ds_ref[s * 64 : (s + 1) * 64, 0:512] = turned.astype(bf16)
    grad, pair = v["grad"], v["pair"]
    pairing = links.slots(8)

    def pair_op(k):
        a, b = k // 2, lax.rem(k, 2)
        return links.op(
            grad.at[a, b, 1 - core], pair.at[a, pl.ds(b * 2, 2)], place.sibling, pairing + k
        )

    def multiply(k):
        at = pl.ds(pl.multiple_of(k * 256, 256), 256)
        v["product"][lax.rem(k, 2)] = dot(gkv[...], norm[:, at])

    def deliver(k):
        at = pl.ds(pl.multiple_of(k * 256, 256), 256)
        a, b = lax.div(k, 2), lax.rem(k, 2)
        value = v["product"][b]
        high = value.astype(bf16)
        low = (value - high.astype(f32)).astype(bf16)
        value = lanes_dot(eye[...], high) + lanes_dot(eye[...], low)
        grad[a, b, :, :, :, 0:16, :] = value[:, 0:256].reshape(2, 2, 4, 16, 256)
        grad[a, b, :, :, :, 16:32, :] = value[:, 256:512].reshape(2, 2, 4, 16, 256)
        action = dot(v["left_t"][at, :], ds_ref[0:128, 0:256])
        action += dot(v["right_t"][at, :], ds_ref[0:128, 256:512])
        grad[a, b, :, :, :, 32:48, :] = action.reshape(2, 2, 4, 16, 256)
        pair_op(k).start()

    def grad_prefix(k, carry):
        deliver(k - 1)
        multiply(k)
        return carry

    multiply(0)
    lax.fori_loop(1, 8, grad_prefix, 0)
    deliver(7)

    def grad_query():
        for offset in range(1, 8):
            member = place.group_member(offset, -1)
            links.arrived(v["group_gq"].at[member], (place.dp, member), exchange + 8 + offset)
        rows = v["group_gq"][...].reshape(1024, 256)
        for a in range(4):
            value = dot(act_t[a * 256 : (a + 1) * 256, :], rows)
            v["grad_query"][a] = value.reshape(2, 2, 64, 256)

    def finish(part):
        def store(value):
            if part == 2:
                out_action_ref[:, 0:256] = value[0:8]
                out_action_ref[:, 256:512] = value[8:16]
            else:
                out_prefix_ref[:, part * 256 : (part + 1) * 256] = value

        return store

    def paired():
        for k in range(8):
            pair_op(k).wait_recv()
        yield

    query_work = reduce_query(links, place, grad_query, v, out_query_ref)
    works = [query_work, paired()]
    works += [reduce_part(links, place, grad, pair, v, part, finish(part)) for part in range(3)]
    early = list(links.sent)
    links.sent.clear()

    def drain(ops):
        def run():
            for op in ops:
                op.wait_send()

        return run

    run_together(works, [drain(early[i::4]) for i in range(4)])
    for op in links.sent:
        op.wait_send()
    for k in range(8):
        pair_op(k).wait_send()


def step(
    cameras, text_length, flow_time, hidden, noise, clean, input_weight, cot,
    own_prefix, own_action, own_query, sine, cosine,
):
    bf16, f32 = jnp.bfloat16, jnp.float32
    hbm, vmem = pl.BlockSpec(memory_space=pltpu.HBM), pl.BlockSpec(memory_space=pltpu.VMEM)
    scratch = dict(
        norm=pltpu.VMEM((2 * KEYS, 2048), bf16),
        own_noisy=pltpu.VMEM((32, 128), bf16),
        query_weight=pltpu.VMEM((4, 2, 2, 64, 256), bf16),
        noisy=pltpu.VMEM((8, 32, 128), bf16),
        time=pltpu.VMEM((8, 2, 1024), f32),
        own_time=pltpu.VMEM((2, 1024), f32),
        act=pltpu.VMEM((1024, 1024), bf16),
        act_t=pltpu.VMEM((1024, 1024), bf16),
        left=pltpu.VMEM((128, 2048), bf16),
        right=pltpu.VMEM((128, 2048), bf16),
        cot=pltpu.VMEM((8, 128, 256), bf16),
        eye=pltpu.VMEM((256, 256), bf16),
        left_t=pltpu.VMEM((2048, 128), bf16),
        right_t=pltpu.VMEM((2048, 128), bf16),
        query=pltpu.VMEM((8, 128, 256), bf16),
        query_out=pltpu.VMEM((8, 128, 256), bf16),
        gq=pltpu.VMEM((8, 128, 256), bf16),
        group_gq=pltpu.VMEM((8, 128, 256), bf16),
        wp=pltpu.VMEM((2048, 512), bf16),
        kv=pltpu.VMEM((2 * KEYS, 512), bf16),
        low=pltpu.VMEM((512, KEYS), bf16),
        ds=pltpu.VMEM((512, KEYS), bf16),
        query_t=pltpu.VMEM((8, 256, 128), bf16),
        cot_t=pltpu.VMEM((2, 8, 256, 128), bf16),
        gkv=pltpu.VMEM((512, 2 * KEYS), bf16),
        grad=pltpu.VMEM((4, 2, 2, 2, 4, ROWS, 256), f32),
        pair=pltpu.VMEM((4, 4, 4, ROWS, 256), f32),
        product=pltpu.VMEM((2, 512, 256), f32),
        grad_query=pltpu.VMEM((4, 2, 2, 64, 256), f32),
        query_pair=pltpu.VMEM((4, 2, 64, 256), f32),
        query_wire=pltpu.VMEM((4, 2, 64, 256), bf16),
        query_half=pltpu.VMEM((2, 64, 256), bf16),
        query_full=pltpu.VMEM((2, 2, 64, 256), bf16),
        query_sum=pltpu.VMEM((2, 64, 256), f32),
        query_far=pltpu.VMEM((64, 256), bf16),
        query_far_out=pltpu.VMEM((64, 256), bf16),
        send=pltpu.SemaphoreType.DMA((192,)),
        recv=pltpu.SemaphoreType.DMA((192,)),
        load=pltpu.SemaphoreType.DMA((16,)),
        flow=pltpu.SMEM((2,), f32),
        cameras=pltpu.SMEM((2,), jnp.int32),
        text=pltpu.SMEM((2,), jnp.int32),
        noise=pltpu.VMEM((2, 32, STEPS), bf16),
        clean=pltpu.VMEM((2, 32, STEPS), bf16),
        input=pltpu.VMEM((32, 1024), bf16),
        cot_in=pltpu.VMEM((STEPS, 2, 2048), bf16),
        own_prefix=pltpu.VMEM((16, 512), bf16),
        own_action=pltpu.VMEM((8, 512), bf16),
        own_query=pltpu.VMEM((64, 256), bf16),
    )
    for part in range(3):
        scratch[f"weight_{part}"] = pltpu.VMEM((2, 4, 4, 4, 16, 256), bf16)
        scratch[f"wire1_{part}"] = pltpu.VMEM((4, 4, 4, 16, 256), bf16)
        scratch[f"half1_{part}"] = pltpu.VMEM((2, 2, 4, 16, 256), bf16)
        scratch[f"full1_{part}"] = pltpu.VMEM((2, 4, 4, 16, 256), bf16)
        scratch[f"wire2_{part}"] = pltpu.VMEM((4, 4, 16, 256), bf16)
        scratch[f"full2_{part}"] = pltpu.VMEM((3, 4, 16, 256), bf16)
        scratch[f"sum3_{part}"] = pltpu.VMEM((4, 16, 256), f32)
        scratch[f"full3_{part}"] = pltpu.VMEM((3, 16, 256), f32)
    return pl.pallas_call(
        step_kernel,
        out_shape=(
            jax.ShapeDtypeStruct((2, STEPS, 2048), bf16),
            jax.ShapeDtypeStruct((64, 256), f32),
            jax.ShapeDtypeStruct((16, 512), f32),
            jax.ShapeDtypeStruct((8, 512), f32),
        ),
        in_specs=[hbm] * 11 + [vmem] * 2,
        out_specs=(vmem,) * 4,
        scratch_shapes=[scratch],
        compiler_params=pltpu.CompilerParams(
            collective_id=1, has_side_effects=True, vmem_limit_bytes=VMEM_LIMIT
        ),
        cost_estimate=pl.CostEstimate(
            flops=10**10, bytes_accessed=9 * 10**6, transcendentals=10**6
        ),
        name="step",
    )(
        *[
            pltpu.with_memory_space_constraint(operand, pltpu.HBM)
            for operand in (
                cameras, text_length, flow_time, hidden, noise, clean, input_weight, cot,
                own_prefix, own_action, own_query,
            )
        ],
        sine,
        cosine,
    )


def time_feature(flow_col, row_width):
    half_width = row_width // 2
    fraction = jnp.arange(half_width, dtype=jnp.float32) / (half_width - 1)
    period = 0.004 * 1000.0**fraction
    angle = flow_col[..., None] * (2.0 * math.pi / period)
    return jnp.sin(angle), jnp.cos(angle)


def on_device(
    prefix_hidden,
    cameras,
    text_length,
    action_noise,
    clean_actions,
    flow_time,
    input_weight,
    prefix_kv_weight,
    action_kv_weight,
    query_weight,
    cotangent,
):
    sine, cosine = time_feature(flow_time, 1024)
    return step(
        cameras,
        text_length,
        flow_time,
        prefix_hidden,
        action_noise.transpose(0, 2, 1),
        clean_actions.transpose(0, 2, 1),
        input_weight,
        cotangent.transpose(1, 0, 2),
        prefix_kv_weight,
        action_kv_weight,
        query_weight,
        sine,
        cosine,
    )


def solution(mesh):
    return jax.shard_map(
        on_device,
        mesh=mesh,
        in_specs=(
            P(("dp", "seq"), None, None),
            P(("dp", "seq")),
            P(("dp", "seq")),
            P(("dp", "seq"), None, None),
            P(("dp", "seq"), None, None),
            P(("dp", "seq")),
            P(),
            P(("dp", "seq"), None),
            P(("dp", "seq"), None),
            P("dp", "seq"),
            P(("dp", "seq"), None, None),
        ),
        out_specs=(
            P(("dp", "seq"), None, None),
            P("dp", "seq"),
            P(("dp", "seq"), None),
            P(("dp", "seq"), None),
        ),
        check_vma=False,
    )
```
